128 devices in a mesh: gx: 16 (over y, x), yz: 8 (over z, core).
Axes of the slice: x: 4, y: 4, z: 4, core: 2. Of those that a mesh axis runs over, the one named last changes fastest.
Arguments:
- particle_phi: float32 [4, 16, 256, 128, 128], P(None, None, 'gx', 'yz'), may hold values from -6 to 6
- particle_offset: float32 [3, 16, 256, 128, 128], P(None, None, 'gx', 'yz'), may hold values from 0 to 1
- slot_count: int32 [256, 128, 128], P('gx', 'yz'), may hold values from 4 to 16
- velocity: float32 [3, 256, 128, 128], P(None, None, 'gx', 'yz'), may hold values from -6 to 6
- diffusivity: float32 [256, 128, 128], P(None, 'gx', 'yz'), may hold values from 0.1 to 2
- migrant_phi: float32 [4, 262144], P(None, ('gx', 'yz')), may hold values from -6 to 6
- migrant_offset: float32 [3, 262144], P(None, ('gx', 'yz')), may hold values from 0 to 1
- migrant_dest: int32 [262144, 1], P(('gx', 'yz')), may hold values from 0 to 127; in each aligned block of 2048 rows (0 to 2047, 2048 to 4095, ...) at most 64 rows name the same one
- migrant_cell: int32 [262144], P(('gx', 'yz')), may hold values from 0 to 32767
Outputs:
- particle_new: float32 [4, 16, 256, 128, 128], P(None, None, 'gx', 'yz')
- migrant_new: float32 [4, 262144], P(None, ('gx', 'yz'))
The draws below stay inside these ranges and needn't reach their ends.
Inputs may be any that keep to these rules, and one draw needn't show every extreme that they name: The first slot_count slots of a cell hold particles; the others are padding. `migrant_dest`: brick index gx_index * 8 + yz_index; the rows of one device name one brick at most 64 times, and in every draw some device names some brick exactly 64 times. `migrant_cell`: x * 16 * 128 + y * 128 + z within the new brick.
All inputs are finite; a program needn't handle non-finite values.
Results may differ from the reference program's by a relative error of at most 0.0003.
Values sent between devices are 32-bit elements; how exact they have to be, the bound alone decides.
No kernel may reach another device: no remote copies, remote signals or barrier semaphores. Data moves between devices by JAX's collectives and lax.ppermute only.
A program may use at most 192 MiB of HBM per device.

```python
import math
import jax
import jax.numpy as jnp
import numpy as np
from jax import lax

BX = 16
BY = 16
NZ = 128
SLOTS = 16
MIG_DEV = 2048
CAP = 64
NX = 256
NY = 128
CELLS = 32768
MIG_TOTAL = 262144
N_YZ = 8
DEVICES = 128


def set_ends(values, own_key, least, top_value):
    dims = values.shape
    spot = [jax.random.randint(jax.random.fold_in(own_key, axis), (), 0, dims[axis]) for axis in range(len(dims))]
    values = values.at[tuple(spot)].set(least)
    longest = dims.index(max(dims))
    spot[longest] = (spot[longest] + 1) % dims[longest]
    return values.at[tuple(spot)].set(top_value)


def level_of(own_key, extent, split, smallest, largest):
    factor_of = 1.0
    for dim, blocks in split:
        steps = jax.random.uniform(jax.random.fold_in(jax.random.fold_in(own_key, 6), dim), (blocks,), jnp.float32, smallest / len(split), largest / len(split))
        factor_of = factor_of * jnp.repeat(jnp.exp(steps), extent[dim] // blocks).reshape((-1,) + (1,) * (len(extent) - 1 - dim))
    return factor_of


def deal_out(rng, own, number, rows, number_of, top, bound, skew):
    ranking = jax.random.permutation(rng, number_of)
    heavy_load, common = portions_of(number_of, rows * top, bound, skew, True), portions_of(number_of, rows * top, bound, skew, False)
    places = jnp.arange(number_of)

    def named(lengths, turn):
        used = int((lengths > 0).sum())
        fixed = max(1, used // 4)
        shifted = fixed + (places - fixed + turn * (used - fixed)) % max(1, number_of - fixed)
        return jnp.zeros((number_of,), jnp.int32).at[ranking[jnp.where(places < fixed, places, shifted)]].set(jnp.asarray(lengths, jnp.int32))

    lengths = jnp.where(number % 4 == 0, named(heavy_load, number // 4), named(common, number - number // 4 - 1))
    mixed = jax.random.permutation(jax.random.fold_in(own, 3), number_of)
    source_of, sink = mixed[0:number_of // 2 * 2:2], mixed[1:number_of // 2 * 2:2]
    room = jnp.minimum(lengths[source_of] - 1, bound - lengths[sink]) // 2
    room = jnp.where((source_of == ranking[0]) | (sink == ranking[0]) | (lengths[sink] == 0), 0, jnp.maximum(room, 0))
    shifted = jax.random.randint(jax.random.fold_in(own, 4), (number_of // 2,), 0, 1 << 20) % (room + 1)
    lengths = lengths.at[source_of].add(-shifted).at[sink].add(shifted)
    labels = jnp.searchsorted(jnp.cumsum(lengths), jnp.arange(rows * top), side="right").astype(jnp.int32)
    table = labels.reshape(top, rows).T
    table = table[jax.random.permutation(jax.random.fold_in(own, 1), rows)]
    turn = jax.random.randint(jax.random.fold_in(own, 2), (rows, 1), 0, top)
    return jnp.take_along_axis(table, (jnp.arange(top)[None, :] + turn) % top, axis=1)


def portions_of(number_of, total, limit, skew, full):
    loads = [(1 << 20) // math.isqrt(rank ** skew) + 1 for rank in range(1, number_of + 1)]
    largest = limit if full else min(limit, max(-(-total // number_of), total * loads[0] // sum(loads)))
    least = 1 if total - largest >= number_of - 1 else 0
    counts, rest = [largest] + [least] * (number_of - 1), total - largest - least * (number_of - 1)
    while rest > 0:
        candidates = [i for i in range(1, number_of) if counts[i] < largest] or [i for i in range(1, number_of) if counts[i] < limit]
        whole, remaining = sum([loads[i] for i in candidates]), rest
        for i in candidates:
            extra = min(limit - counts[i], max(1, remaining * loads[i] // whole), rest)
            counts[i] = counts[i] + extra
            rest = rest - extra
    return np.array(counts)


def noise(stream_key, shape, width, bound, cuts=(), held_as=jnp.bfloat16):
    level = level_of(stream_key, shape, cuts, -0.22, 0.18) if cuts else 1.0
    drawn = jax.random.normal(stream_key, shape, jnp.float32) * width * level
    return jnp.minimum(jnp.maximum(drawn, -bound), bound).astype(held_as)


def setup_inputs(seed: int = 0) -> dict:
    keys = jax.random.split(jax.random.key(seed), 10)
    particle_phi = noise(keys[0], (4, SLOTS, NX, NY, NZ), 1.0, 6.0, ((2, 16), (3, 8)), jnp.float32)
    particle_offset = jnp.clip(1.0 * jax.random.uniform(keys[1], (3, SLOTS, NX, NY, NZ), jnp.float32) ** level_of(keys[1], (3, SLOTS, NX, NY, NZ), ((2, 16), (3, 8)), -0.2, 0.2), 0.0, 1.0)
    slot_count = set_ends(jax.random.randint(keys[2], (NX, NY, NZ), max(1, SLOTS // 4), SLOTS + 1), jax.random.fold_in(keys[2], 1), max(1, SLOTS // 4), SLOTS).astype(jnp.int32)
    velocity = noise(keys[3], (3, NX, NY, NZ), 1.0, 6.0, ((2, 16), (3, 8)), jnp.float32)
    diffusivity = jnp.clip(jnp.exp(math.log(2.0) - 2.9957323 * jax.random.uniform(keys[4], (NX, NY, NZ), jnp.float32) ** level_of(keys[4], (NX, NY, NZ), ((1, 16), (2, 8)), -0.2, 0.2)), 0.1, 2.0)
    migrant_phi = noise(keys[5], (4, MIG_TOTAL), 1.0, 6.0, ((1, 128),), jnp.float32)
    migrant_offset = jnp.clip(1.0 * jax.random.uniform(keys[6], (3, MIG_TOTAL), jnp.float32) ** level_of(keys[6], (3, MIG_TOTAL), ((1, 128),), -0.2, 0.2), 0.0, 1.0)
    migrant_dest_keys = jax.random.split(jax.random.fold_in(keys[7], 1), MIG_TOTAL // MIG_DEV)
    migrant_dest_turns = jax.random.permutation(jax.random.fold_in(keys[7], 3), MIG_TOTAL // MIG_DEV)
    migrant_dest = jax.vmap(lambda own, number: deal_out(jax.random.fold_in(keys[7], 2), own, number, MIG_DEV, DEVICES, 1, CAP, 2))(migrant_dest_keys, migrant_dest_turns).reshape((MIG_TOTAL, 1))
    migrant_cell = set_ends(jax.random.randint(keys[8], (MIG_TOTAL,), 0, CELLS), jax.random.fold_in(keys[8], 1), 0, CELLS - 1).astype(jnp.int32)
    return dict(particle_phi=particle_phi, particle_offset=particle_offset, slot_count=slot_count, velocity=velocity, diffusivity=diffusivity, migrant_phi=migrant_phi, migrant_offset=migrant_offset, migrant_dest=migrant_dest, migrant_cell=migrant_cell)


time_step = 0.08
mix_coeff = 0.5


def neighbour_terms(padded_mean, padded_gamma, velocity):
    centre = padded_mean[:, 1:-1, 1:-1, 1:-1]
    gamma_centre = padded_gamma[1:-1, 1:-1, 1:-1]
    diffusion = jnp.zeros_like(centre)
    advection = jnp.zeros_like(centre)
    for axis_index in range(3):
        upper_cut = [slice(1, -1), slice(1, -1), slice(1, -1)]
        lower_cut = [slice(1, -1), slice(1, -1), slice(1, -1)]
        upper_cut[axis_index] = slice(2, None)
        lower_cut[axis_index] = slice(None, -2)
        mean_upper = padded_mean[(slice(None),) + tuple(upper_cut)]
        mean_lower = padded_mean[(slice(None),) + tuple(lower_cut)]
        gamma_upper = padded_gamma[tuple(upper_cut)]
        gamma_lower = padded_gamma[tuple(lower_cut)]
        diffusion = diffusion + 0.5 * (gamma_centre + gamma_upper) * (mean_upper - centre)
        diffusion = diffusion + 0.5 * (gamma_centre + gamma_lower) * (mean_lower - centre)
        advection = advection + velocity[axis_index] * (mean_upper - mean_lower) * 0.5
    return time_step * (diffusion - advection)


def corner_weight(frac_value, shift_value):
    if shift_value == 1:
        return frac_value
    return 1.0 - frac_value


def mix_update(phi_now, blended):
    mixed_mean = blended[0:4]
    carried = blended[4:8]
    rate_gamma = blended[8]
    return phi_now + carried - mix_coeff * rate_gamma * (phi_now - mixed_mean)


def reference(particle_phi, particle_offset, slot_count, velocity, diffusivity, migrant_phi, migrant_offset, migrant_dest, migrant_cell):
    slot_ids = jnp.arange(SLOTS, dtype=jnp.int32)
    occupied = slot_ids[:, None, None, None] < slot_count[None]
    local_sum = jnp.sum(jnp.where(occupied[None], particle_phi, 0.0), axis=1)
    destination = migrant_dest[:, 0]
    cell_x = (destination // N_YZ) * BX + migrant_cell // (BY * NZ)
    cell_y = (destination % N_YZ) * BY + (migrant_cell // NZ) % BY
    cell_z = migrant_cell % NZ
    flat_cell = ((cell_x * NY + cell_y) * NZ + cell_z).astype(jnp.int32)
    total_cells = NX * NY * NZ
    moved_sum = jnp.zeros((4, total_cells), jnp.float32).at[:, flat_cell].add(migrant_phi).reshape(4, NX, NY, NZ)
    moved_count = jnp.zeros((total_cells,), jnp.float32).at[flat_cell].add(1.0).reshape(NX, NY, NZ)
    cell_mean = (local_sum + moved_sum) / (slot_count.astype(jnp.float32) + moved_count)
    padded_mean = jnp.pad(cell_mean, ((0, 0), (1, 1), (1, 1), (1, 1)))
    padded_gamma = jnp.pad(diffusivity, 1)
    transport = neighbour_terms(padded_mean, padded_gamma, velocity)
    fields = jnp.concatenate([cell_mean, transport, diffusivity[None]], axis=0)
    corner_table = jnp.pad(fields, ((0, 0), (0, 1), (0, 1), (0, 1)))

    def update_slot(slot_index):
        phi_now = lax.dynamic_index_in_dim(particle_phi, slot_index, 1, keepdims=False)
        frac_now = lax.dynamic_index_in_dim(particle_offset, slot_index, 1, keepdims=False)
        blended = jnp.zeros((9, NX, NY, NZ), jnp.float32)
        for shift_x in (0, 1):
            for shift_y in (0, 1):
                for shift_z in (0, 1):
                    weight = corner_weight(frac_now[0], shift_x) * corner_weight(frac_now[1], shift_y) * corner_weight(frac_now[2], shift_z)
                    corner = corner_table[:, shift_x:shift_x + NX, shift_y:shift_y + NY, shift_z:shift_z + NZ]
                    blended = blended + weight[None] * corner
        fresh_phi = mix_update(phi_now, blended)
        return jnp.where(slot_index < slot_count, fresh_phi, 0.0)

    updated = lax.map(update_slot, slot_ids)
    particle_new = jnp.moveaxis(updated, 0, 1)
    flat_table = corner_table.reshape(9, -1)
    moved_blend = jnp.zeros((9, migrant_phi.shape[1]), jnp.float32)
    for shift_x in (0, 1):
        for shift_y in (0, 1):
            for shift_z in (0, 1):
                flat_index = (((cell_x + shift_x) * (NY + 1) + cell_y + shift_y) * (NZ + 1) + cell_z + shift_z).astype(jnp.int32)
                weight = corner_weight(migrant_offset[0], shift_x) * corner_weight(migrant_offset[1], shift_y) * corner_weight(migrant_offset[2], shift_z)
                moved_blend = moved_blend + weight[None] * jnp.take(flat_table, flat_index, axis=1)
    migrant_new = mix_update(migrant_phi, moved_blend)
    return particle_new, migrant_new
```

```python
import functools

import jax
import jax.numpy as jnp
from jax import lax
from jax.experimental import pallas as pl
from jax.experimental.pallas import tpu as pltpu
from jax.sharding import PartitionSpec as P

time_step = 0.08
mix_coeff = 0.5
f32 = jnp.float32
bf16 = jnp.bfloat16
MB = 2**20
WHOLE = pl.BlockSpec(memory_space=pltpu.VMEM)
SCALARS = pl.BlockSpec(memory_space=pltpu.SMEM)


def iota(shape, dim):
    return lax.broadcasted_iota(jnp.int32, shape, dim)


def split(value):
    top = value.astype(bf16).astype(f32)
    return top, value - top


def dot_nt(left, right):
    return lax.dot_general(left, right, (((1,), (1,)), ((), ())), preferred_element_type=f32)


def dot_nn(left, right):
    return lax.dot_general(left, right, (((1,), (0,)), ((), ())), preferred_element_type=f32)


def call(body, outs, specs, scratch=(), vmem=48, cost=None, name=None):
    return pl.pallas_call(
        body,
        out_shape=tuple(jax.ShapeDtypeStruct(s, d) for s, d in outs),
        in_specs=list(specs),
        out_specs=tuple(WHOLE for _ in outs),
        scratch_shapes=list(scratch),
        compiler_params=pltpu.CompilerParams(vmem_limit_bytes=vmem * MB),
        cost_estimate=cost,
        name=name,
    )


def dispatch_body(dest_ref, cell_ref, phi_ref, off_ref, out_ref, rank_ref, *, bricks, cap):
    rows = dest_ref.shape[1]
    hot = jnp.where(iota((bricks, rows), 0) == dest_ref[...], 1.0, 0.0).astype(bf16)
    step = 256
    before = jnp.where(iota((step, step), 0) < iota((step, step), 1), 1.0, 0.0).astype(bf16)
    carry = jnp.zeros((bricks, 1), f32)
    ranks = []
    for b in range(rows // step):
        part = hot[:, b * step : (b + 1) * step]
        wide = part.astype(f32)
        count = dot_nn(part, before) + carry
        ranks.append(jnp.sum(wide * count, axis=0, keepdims=True))
        carry = carry + jnp.sum(wide, axis=1, keepdims=True)
    rank = jnp.concatenate(ranks, axis=1).astype(jnp.int32)
    rank_ref[...] = rank
    here = iota((cap, rows), 0) == rank
    channels = [phi_ref[c : c + 1, :] for c in range(4)]
    channels += [off_ref[c : c + 1, :] for c in range(3)]
    channels.append((cell_ref[...] + 1).astype(f32))
    tops, rests = [], []
    for row in channels:
        top, rest = split(row)
        tops.append(jnp.where(here, top, 0.0).astype(bf16))
        rests.append(jnp.where(here, rest, 0.0).astype(bf16))
    sent = dot_nt(jnp.concatenate(tops, axis=0), hot) + dot_nt(
        jnp.concatenate(rests, axis=0), hot
    )
    sent = sent.T
    for r in range(4):
        out_ref[:, r, :] = sent[:, 128 * r : 128 * (r + 1)]


def collect_body(dest_ref, rank_ref, back_ref, out_ref, *, bricks, cap):
    rows = dest_ref.shape[1]
    hot = jnp.where(iota((bricks, rows), 0) == dest_ref[...], 1.0, 0.0).astype(bf16)
    table = jnp.concatenate([back_ref[:, 0, :], back_ref[:, 1, :]], axis=1).T
    top, rest = split(table)
    both = jnp.concatenate([top, rest], axis=1).astype(bf16)
    got = dot_nn(both, jnp.concatenate([hot, hot], axis=0))
    here = iota((cap, rows), 0) == rank_ref[...]
    for c in range(4):
        picked = jnp.where(here, got[c * cap : (c + 1) * cap], 0.0)
        out_ref[c : c + 1, :] = jnp.sum(picked, axis=0, keepdims=True)


def local_body(phi_ref, count_ref, out_ref):
    count = count_ref[0]
    for c in range(4):
        total = None
        for s in range(phi_ref.shape[1]):
            value = jnp.where(count > s, phi_ref[c, s, 0], 0.0)
            total = value if total is None else total + value
        out_ref[c, 0] = total


def scatter_body(
    arr_ref, local_ref, count_ref, mean_ref, xs_ref, ehi_ref, elo_ref, e15_ref, e01_ref, acc_ref
):
    half = arr_ref.shape[0] // 2
    lane = iota((half, 128), 1)
    for r in range(4):
        low = arr_ref[0:half, r, :]
        high = arr_ref[half : 2 * half, r, :]
        xs_ref[2 * r] = jnp.where(lane < 64, low, pltpu.roll(high, 64, 1))
        xs_ref[2 * r + 1] = jnp.where(lane < 64, pltpu.roll(low, 64, 1), high)
    acc_ref[...] = jnp.zeros_like(acc_ref)

    def step(i, carry):
        at = pl.multiple_of(i * 8, 8)
        cell = xs_ref[7, pl.ds(at, 8), :].astype(jnp.int32) - 1
        plane = cell >> 7
        depth = cell & 127
        parts = [split(xs_ref[c, pl.ds(at, 8), :]) for c in range(4)]
        lefts, rights = [], []
        for u in range(8):
            at_z = iota((128, 128), 0) == depth[u : u + 1]
            at_p = iota((256, 128), 0) == plane[u : u + 1]
            rights.append(jnp.where(at_p, 1.0, 0.0).astype(bf16))
            blocks = [jnp.where(at_z, 1.0, 0.0).astype(bf16)]
            for top, rest in parts:
                blocks.append(jnp.where(at_z, top[u : u + 1], 0.0).astype(bf16))
                blocks.append(jnp.where(at_z, rest[u : u + 1], 0.0).astype(bf16))
            lefts.append(jnp.concatenate(blocks, axis=0))
        acc_ref[...] += dot_nt(
            jnp.concatenate(lefts, axis=1), jnp.concatenate(rights, axis=1)
        )
        return carry

    lax.fori_loop(0, half // 8, step, 0)
    wx, wy = count_ref.shape[0], count_ref.shape[1]
    number = acc_ref[0:128, :].T.reshape(wx, wy, 128)
    share = 1.0 / (count_ref[...].astype(f32) + number)
    for c in range(4):
        at = 128 + 256 * c
        moved = (acc_ref[at : at + 128, :] + acc_ref[at + 128 : at + 256, :]).T
        mean = (local_ref[c] + moved.reshape(wx, wy, 128)) * share
        mean_ref[c] = mean
        ehi_ref[c] = mean[wx - 1 : wx]
        elo_ref[c] = mean[0:2]
        e15_ref[c] = mean[:, wy - 1, :]
        e01_ref[0, c] = mean[:, 0, :]
        e01_ref[1, c] = mean[:, 1, :]


def edge_body(lo_ref, hi_ref, e15_ref, e01_ref, up_ref, down_ref):
    wy = lo_ref.shape[2]
    for ref, source, y in (
        (up_ref, lambda c: e15_ref[c], wy - 1),
        (down_ref.at[0], lambda c: e01_ref[0, c], 0),
        (down_ref.at[1], lambda c: e01_ref[1, c], 1),
    ):
        for c in range(4):
            ref[c, 0:16, :] = source(c)
            ref[c, 16:24, :] = jnp.concatenate(
                [
                    hi_ref[c, 0, y : y + 1, :],
                    hi_ref[c, 1, y : y + 1, :],
                    lo_ref[c, 0, y : y + 1, :],
                    jnp.zeros((5, 128), f32),
                ],
                axis=0,
            )


def pencil_x_body(vel_ref, gam_ref, out_ref):
    groups = out_ref.shape[0]
    pieces = [vel_ref[c].reshape(128, vel_ref.shape[3]).T for c in range(3)]
    pieces.append(gam_ref[...].reshape(128, gam_ref.shape[2]).T)
    rows = jnp.concatenate(pieces, axis=1)
    row = iota((8, 512), 0)
    zero = jnp.zeros((8, 512), f32)
    for p in range(groups):
        out_ref[p, 0:16, :] = rows[16 * p : 16 * p + 16]
        above = rows[16 * p + 16 : 16 * p + 24] if p < groups - 1 else zero
        below = pltpu.roll(rows[16 * p - 8 : 16 * p], 3, 0) if p > 0 else zero
        out_ref[p, 16:24, :] = jnp.where(
            row < 2, above, jnp.where(row == 2, below, 0.0)
        )


def pencil_y_body(in_ref, out_ref):
    groups = out_ref.shape[0]
    lane = iota((24, 128), 1)
    zero = jnp.zeros((24, 128), f32)
    for q in range(groups):
        out_ref[q, :, 0:512] = in_ref[2 * q]
        out_ref[q, :, 512:1024] = in_ref[2 * q + 1]
        pieces = []
        for c in range(4):
            lanes = slice(128 * c, 128 * c + 128)
            above = in_ref[2 * q + 2, :, lanes] if q < groups - 1 else zero
            below = pltpu.roll(in_ref[2 * q - 1, :, lanes], 48, 1) if q > 0 else zero
            pieces.append(jnp.where(lane < 32, above, jnp.where(lane < 48, below, 0.0)))
        for e in (0, 1):
            out_ref[q, :, 1024 + 128 * e : 1152 + 128 * e] = jnp.where(
                lane < 64, pieces[2 * e], pltpu.roll(pieces[2 * e + 1], 64, 1)
            )


def brick_body(in_ref, brick_ref, col_ref, tall_ref):
    lane = iota((8, 128), 1)
    for tile in range(10):
        for xt in range(3):
            group = [in_ref[j, 8 * xt : 8 * xt + 8, 128 * tile : 128 * tile + 128] for j in range(8)]
            for bit in (4, 2, 1):
                shift = 16 * bit
                high = (lane // shift) % 2 == 1
                fresh = list(group)
                for j in range(8):
                    if j & bit:
                        continue
                    first, second = group[j], group[j | bit]
                    fresh[j] = jnp.where(high, pltpu.roll(second, shift, 1), first)
                    fresh[j | bit] = jnp.where(high, second, pltpu.roll(first, 128 - shift, 1))
                group = fresh
            for g in range(8):
                if tile < 8:
                    c, y = tile % 4, 8 * (tile // 4) + g
                    at = (c * 16 + y) * 24 + 8 * xt
                    tall_ref[at : at + 8, :] = group[g]
                elif g % 4 < 3:
                    c, y = 2 * (tile - 8) + g // 4, g % 4
                    col_ref[c, y, 8 * xt : 8 * xt + 8, :] = group[g]
    for c in range(4):
        for x in range(19):
            for yt in (0, 8):
                brick_ref[c, x, yt : yt + 8, :] = tall_ref[
                    pl.ds((c * 16 + yt) * 24 + x, 8, stride=24), :
                ]


def z_shift(value, up):
    lane = iota(value.shape, value.ndim - 1)
    if up:
        return jnp.where(lane == 127, 0.0, pltpu.roll(value, 127, value.ndim - 1))
    return jnp.where(lane == 0, 0.0, pltpu.roll(value, 1, value.ndim - 1))


def flux(centre, gamma, sides, velocity):
    total = None
    drift = None
    for (up, gamma_up, down, gamma_down), speed in zip(sides, velocity):
        term = (gamma + gamma_up) * (up - centre) + (gamma + gamma_down) * (down - centre)
        total = term if total is None else total + term
        move = speed * (up - down)
        drift = move if drift is None else drift + move
    return (0.5 * time_step) * (total - drift)


def slot_terms(xs_ref, at):
    def row(c):
        return jnp.concatenate([xs_ref[c, pl.ds(at + e, 1), :] for e in (0, 1)], axis=1)

    cell = row(7).astype(jnp.int32) - 1
    filled = cell >= 0
    depth = cell & 127
    x = jnp.where(filled, cell >> 11, -2)
    y = (cell >> 7) & 15
    return row, x, y, depth


def hat(number, at, frac):
    spot = iota((number, at.shape[1]), 0)
    return jnp.where(spot == at, 1.0 - frac, 0.0) + jnp.where(spot == at + 1, frac, 0.0)


def depth_weights(depth, frac):
    top, rest = split(hat(128, depth, frac))
    top = top.astype(bf16)
    return jnp.concatenate([top, top, rest.astype(bf16)], axis=0)


def widen(tab_ref, lhs_ref):
    top, rest = split(tab_ref[...])
    top = top.astype(bf16)
    lhs_ref[:, 0:128] = top
    lhs_ref[:, 128:256] = rest.astype(bf16)
    lhs_ref[:, 256:384] = top


def total_y(value):
    return jnp.sum(value, axis=0, keepdims=True)


def blend_inner_body(mean_ref, brick_ref, col_ref, xs_ref, out_ref, tab_ref, lhs_ref):
    for c in range(4):
        tab_ref[256 * c : 256 * c + 256, :] = mean_ref[c].reshape(256, 128)
    tab_ref[1024:1280, :] = brick_ref[3, 0:16].reshape(256, 128)
    tab_ref[1280:1296, :] = brick_ref[3, 16]
    tab_ref[1296:1320, :] = col_ref[3, 0]
    tab_ref[1320:1328, :] = jnp.zeros((8, 128), f32)
    widen(tab_ref, lhs_ref)

    def step(i, carry):
        row, x, y, depth = slot_terms(xs_ref, 2 * i)
        along = dot_nn(lhs_ref[...], depth_weights(depth, row(6)))
        wx = hat(24, x, row(4))
        wy = hat(24, y, row(5))
        sums = [None] * 5
        for k in range(16):
            weight = wx[k : k + 1] * wy[0:16]
            for c in range(5):
                at = 256 * c + 16 * k
                term = along[at : at + 16] * weight
                sums[c] = term if sums[c] is None else sums[c] + term
        sums[4] = sums[4] + along[1280:1296] * (wx[16:17] * wy[0:16])
        got = [total_y(value) for value in sums]
        got[4] = got[4] + total_y(along[1296:1320] * (wx * wy[16:17]))
        for c in range(5):
            for e in (0, 1):
                out_ref[c, pl.ds(2 * i + e, 1), :] = got[c][:, 128 * e : 128 * e + 128]
        return carry

    lax.fori_loop(0, xs_ref.shape[1] // 2, step, 0)


def transport_body(
    last_ref, mean_ref, lo_ref, hi_ref, ylo_ref, yhi_ref, brick_ref, col_ref, f_ref, tcol_ref, mp_ref, gp_ref
):
    x_in = jnp.where(last_ref[0] == 1, 0.0, 1.0).astype(f32)
    y_in = jnp.where(last_ref[1] == 1, 0.0, 1.0).astype(f32)
    for c in range(4):
        mp_ref[c, 0:16, 8:24, :] = mean_ref[c]
        mp_ref[c, 16:18, 8:24, :] = hi_ref[c]
        mp_ref[c, 18, 8:24, :] = lo_ref[c, 0]
        mp_ref[c, :, 7, :] = ylo_ref[c, 0:19, :]
        mp_ref[c, :, 24, :] = yhi_ref[0, c, 0:19, :]
    gp_ref[:, 8:24, :] = brick_ref[3]
    gp_ref[:, 7, :] = col_ref[3, 2, 0:19, :]
    gp_ref[:, 24, :] = col_ref[3, 0, 0:19, :]

    def plane(x, carry):
        below = jnp.where(x == 0, 18, x - 1)
        keep = jnp.where(x == 16, x_in, 1.0)
        gamma = gp_ref[x, 8:24, :]
        gammas = [
            (gp_ref[x + 1, 8:24, :], gp_ref[below, 8:24, :]),
            (gp_ref[x, 9:25, :], gp_ref[x, 7:23, :]),
            (z_shift(gamma, True), z_shift(gamma, False)),
        ]
        velocity = [brick_ref[d, x] for d in range(3)]
        for c in range(4):
            centre = mp_ref[c, x, 8:24, :]
            means = [
                (mp_ref[c, x + 1, 8:24, :], mp_ref[c, below, 8:24, :]),
                (mp_ref[c, x, 9:25, :], mp_ref[c, x, 7:23, :]),
                (z_shift(centre, True), z_shift(centre, False)),
            ]
            sides = [(m[0], g[0], m[1], g[1]) for m, g in zip(means, gammas)]
            f_ref[c, x, 0:16, :] = centre
            f_ref[4 + c, x, 0:16, :] = flux(centre, gamma, sides, velocity) * keep
        f_ref[8, x, 0:16, :] = gamma
        return carry

    lax.fori_loop(0, 17, plane, 0)
    row = iota((24, 128), 0)

    def x_up(value):
        return pltpu.roll(value, 23, 0)

    def x_down(value):
        return jnp.where(row == 0, value[18:19], pltpu.roll(value, 1, 0))

    keep = jnp.where(row == 16, x_in, 1.0) * y_in
    gamma = col_ref[3, 0]
    gamma_low = jnp.concatenate([gp_ref[:, 23, :], jnp.zeros((5, 128), f32)], axis=0)
    gammas = [
        (x_up(gamma), x_down(gamma)),
        (col_ref[3, 1], gamma_low),
        (z_shift(gamma, True), z_shift(gamma, False)),
    ]
    velocity = [col_ref[d, 0] for d in range(3)]
    for c in range(4):
        centre = yhi_ref[0, c]
        low = jnp.concatenate([mp_ref[c, :, 23, :], jnp.zeros((5, 128), f32)], axis=0)
        means = [
            (x_up(centre), x_down(centre)),
            (yhi_ref[1, c], low),
            (z_shift(centre, True), z_shift(centre, False)),
        ]
        sides = [(m[0], g[0], m[1], g[1]) for m, g in zip(means, gammas)]
        moved = flux(centre, gamma, sides, velocity) * keep
        tcol_ref[c] = centre
        tcol_ref[4 + c] = moved
        f_ref[c, :, 16, :] = centre[0:17]
        f_ref[4 + c, :, 16, :] = moved[0:17]
    f_ref[8, :, 16, :] = gamma[0:17]


def blend_outer_body(f_ref, tcol_ref, inner_ref, xs_ref, out_ref, tab_ref, lhs_ref, new_ref):
    for c in range(4):
        tab_ref[256 * c : 256 * c + 256, :] = f_ref[4 + c, 0:16, 0:16, :].reshape(256, 128)
    for c in range(8):
        tab_ref[1024 + 16 * c : 1040 + 16 * c, :] = f_ref[c, 16, 0:16, :]
        tab_ref[1152 + 24 * c : 1176 + 24 * c, :] = tcol_ref[c]
    widen(tab_ref, lhs_ref)

    def step(i, carry):
        row, x, y, depth = slot_terms(xs_ref, 2 * i)
        along = dot_nn(lhs_ref[...], depth_weights(depth, row(6)))
        wx = hat(24, x, row(4))
        wy = hat(24, y, row(5))
        sums = [None] * 4
        for k in range(16):
            weight = wx[k : k + 1] * wy[0:16]
            for c in range(4):
                at = 256 * c + 16 * k
                term = along[at : at + 16] * weight
                sums[c] = term if sums[c] is None else sums[c] + term
        top = wx[16:17] * wy[0:16]
        side = wx * wy[16:17]
        got = []
        for c in range(8):
            value = total_y(along[1024 + 16 * c : 1040 + 16 * c] * top)
            value = value + total_y(along[1152 + 24 * c : 1176 + 24 * c] * side)
            if c >= 4:
                value = value + total_y(sums[c - 4])
            got.append(value)

        def inner(c):
            return jnp.concatenate([inner_ref[c, pl.ds(2 * i + e, 1), :] for e in (0, 1)], axis=1)

        rate = mix_coeff * inner(4)
        for c in range(4):
            phi = row(c)
            fresh = phi + got[4 + c] - rate * (phi - (got[c] + inner(c)))
            for e in (0, 1):
                new_ref[c, pl.ds(2 * i + e, 1), :] = fresh[:, 128 * e : 128 * e + 128]
        return carry

    half = xs_ref.shape[1]
    lax.fori_loop(0, half // 2, step, 0)
    lane = iota((half, 128), 1)
    for r in range(2):
        low, high = new_ref[2 * r], new_ref[2 * r + 1]
        out_ref[0:half, r, :] = jnp.where(lane < 64, low, pltpu.roll(high, 64, 1))
        out_ref[half : 2 * half, r, :] = jnp.where(lane < 64, pltpu.roll(low, 64, 1), high)


def update_body(phi_ref, off_ref, count_ref, f_ref, out_ref, coef_ref):
    x = pl.program_id(0)
    slots = phi_ref.shape[1]
    for yt in (0, 8):
        for ch in range(9):
            corner = {}
            for sx in (0, 1):
                for sy in (0, 1):
                    value = f_ref[ch, x + sx, yt + sy : yt + sy + 8, :]
                    corner[sx, sy, 0] = value
                    corner[sx, sy, 1] = z_shift(value, True) - value
            for sz in (0, 1):
                c00, c01 = corner[0, 0, sz], corner[0, 1, sz]
                c10, c11 = corner[1, 0, sz], corner[1, 1, sz]
                dx = c10 - c00
                coef_ref[ch, sz] = c00
                coef_ref[ch, 2 + sz] = c01 - c00
                coef_ref[ch, 4 + sz] = dx
                coef_ref[ch, 6 + sz] = (c11 - c01) - dx
        count = count_ref[0, yt : yt + 8, :]
        rows = slice(yt, yt + 8)
        width = 4

        def group(i, carry):
            at = [i * width + s for s in range(width)]
            a = [off_ref[0, s, 0, rows, :] for s in at]
            b = [off_ref[1, s, 0, rows, :] for s in at]
            d = [off_ref[2, s, 0, rows, :] for s in at]

            def blend(ch):
                k = [coef_ref[ch, n] for n in range(8)]
                return [
                    ((k[7] * d[n] + k[6]) * b[n] + (k[5] * d[n] + k[4])) * a[n]
                    + ((k[3] * d[n] + k[2]) * b[n] + (k[1] * d[n] + k[0]))
                    for n in range(width)
                ]

            rate = [mix_coeff * value for value in blend(8)]
            for c in range(4):
                mean = blend(c)
                moved = blend(4 + c)
                for n in range(width):
                    phi = phi_ref[c, at[n], 0, rows, :]
                    fresh = phi + moved[n] - rate[n] * (phi - mean[n])
                    out_ref[c, at[n], 0, rows, :] = jnp.where(count > at[n], fresh, 0.0)
            return carry

        lax.fori_loop(0, slots // width, group, 0)


def shifted(value, axis, by):
    count = lax.axis_size(axis)
    pairs = [(i, i + by) for i in range(count) if 0 <= i + by < count]
    return lax.ppermute(value, axis, pairs)


def exchange(value, axis):
    return lax.all_to_all(value, axis, split_axis=0, concat_axis=0, tiled=True)


def shards(phi, offset, count, velocity, diffusivity, m_phi, m_offset, m_dest, m_cell):
    slots, wx, wy, depth = phi.shape[1:]
    groups_x, groups_y = lax.axis_size("gx"), lax.axis_size("yz")
    bricks = groups_x * groups_y
    rows = m_phi.shape[1]
    cap = 4 * rows // bricks
    half = bricks // 2

    dest = m_dest.reshape(1, rows)
    cell = m_cell.reshape(1, rows)
    sent, rank = call(
        functools.partial(dispatch_body, bricks=bricks, cap=cap),
        [((bricks, 4, 128), f32), ((1, rows), jnp.int32)],
        [WHOLE] * 4,
        name="dispatch",
    )(dest, cell, m_phi, m_offset)

    pencil, = call(
        pencil_x_body, [((groups_x, 24, 512), f32)], [WHOLE] * 2, name="pencil_x"
    )(jnp.transpose(velocity, (0, 2, 3, 1)), jnp.transpose(diffusivity, (1, 2, 0)))
    pencil = exchange(pencil, "gx")
    arrived = exchange(sent, ("gx", "yz"))

    block_phi = pl.BlockSpec((4, slots, 1, wy, depth), lambda i: (0, 0, i, 0, 0))
    block_off = pl.BlockSpec((3, slots, 1, wy, depth), lambda i: (0, 0, i, 0, 0))
    block_count = pl.BlockSpec((1, wy, depth), lambda i: (i, 0, 0))
    local_sum = pl.pallas_call(
        local_body,
        out_shape=jax.ShapeDtypeStruct((4, wx, wy, depth), f32),
        grid=(wx,),
        in_specs=[block_phi, block_count],
        out_specs=pl.BlockSpec((4, 1, wy, depth), lambda i: (0, i, 0, 0)),
        compiler_params=pltpu.CompilerParams(vmem_limit_bytes=16 * MB),
        cost_estimate=pl.CostEstimate(flops=4 * 10**6, bytes_accessed=9 * 10**6, transcendentals=0),
        name="local_sum",
    )(phi, count)

    wide, = call(pencil_y_body, [((groups_y, 24, 1280), f32)], [WHOLE], name="pencil_y")(pencil)
    wide = exchange(wide, "yz")
    brick, col = call(
        brick_body,
        [((4, 19, wy, depth), f32), ((4, 3, 24, depth), f32)],
        [WHOLE],
        [pltpu.VMEM((4 * 16 * 24, 128), f32)],
        name="brick",
    )(wide)

    mean, xs, ehi, elo, e15, e01 = call(
        scatter_body,
        [
            ((4, wx, wy, depth), f32),
            ((8, half, 128), f32),
            ((4, 1, wy, depth), f32),
            ((4, 2, wy, depth), f32),
            ((4, wx, depth), f32),
            ((2, 4, wx, depth), f32),
        ],
        [WHOLE] * 3,
        [pltpu.VMEM((9 * 128, 256), f32)],
        name="scatter",
    )(arrived, local_sum, count)

    lo = shifted(ehi, "gx", 1)
    hi = shifted(elo, "gx", -1)
    inner, = call(
        blend_inner_body,
        [((5, half, 128), f32)],
        [WHOLE] * 4,
        [pltpu.VMEM((1328, 128), f32), pltpu.VMEM((1328, 384), bf16)],
        cost=pl.CostEstimate(flops=8 * 10**9, bytes_accessed=3 * 10**6, transcendentals=0),
        name="blend_inner",
    )(mean, brick, col, xs)
    up, down = call(
        edge_body,
        [((4, 24, depth), f32), ((2, 4, 24, depth), f32)],
        [WHOLE] * 4,
        name="edge",
    )(lo, hi, e15, e01)
    ylo = shifted(up, "yz", 1)
    yhi = shifted(down, "yz", -1)

    last = jnp.stack(
        [
            (lax.axis_index("gx") == groups_x - 1).astype(jnp.int32),
            (lax.axis_index("yz") == groups_y - 1).astype(jnp.int32),
        ]
    )
    fields, edge = call(
        transport_body,
        [((9, 17, 24, depth), f32), ((8, 24, depth), f32)],
        [SCALARS] + [WHOLE] * 7,
        [pltpu.VMEM((4, 19, 32, 128), f32), pltpu.VMEM((19, 32, 128), f32)],
        name="transport",
    )(last, mean, lo, hi, ylo, yhi, brick, col)
    moved_new, = call(
        blend_outer_body,
        [((bricks, 2, 128), f32)],
        [WHOLE] * 4,
        [
            pltpu.VMEM((1344, 128), f32),
            pltpu.VMEM((1344, 384), bf16),
            pltpu.VMEM((4, half, 128), f32),
        ],
        name="blend_outer",
    )(fields, edge, inner, xs)
    back = exchange(moved_new, ("gx", "yz"))

    particle_new = pl.pallas_call(
        update_body,
        out_shape=jax.ShapeDtypeStruct(phi.shape, f32),
        grid=(wx,),
        in_specs=[
            block_phi,
            block_off,
            block_count,
            pl.BlockSpec((9, 17, 24, depth), lambda i: (0, 0, 0, 0)),
        ],
        out_specs=block_phi,
        scratch_shapes=[pltpu.VMEM((9, 8, 8, 128), f32)],
        compiler_params=pltpu.CompilerParams(vmem_limit_bytes=24 * MB),
        cost_estimate=pl.CostEstimate(flops=8 * 10**7, bytes_accessed=25 * 10**6, transcendentals=0),
        name="update",
    )(phi, offset, count, fields)

    migrant_new, = call(
        functools.partial(collect_body, bricks=bricks, cap=cap),
        [((4, rows), f32)],
        [WHOLE] * 3,
        name="collect",
    )(dest, rank, back)
    return particle_new, migrant_new


def solution(mesh):
    placed = (
        P(None, None, "gx", "yz", None),
        P(None, None, "gx", "yz", None),
        P("gx", "yz", None),
        P(None, None, "gx", "yz"),
        P(None, "gx", "yz"),
        P(None, ("gx", "yz")),
        P(None, ("gx", "yz")),
        P(("gx", "yz"), None),
        P(("gx", "yz")),
    )
    return jax.shard_map(
        shards,
        mesh=mesh,
        in_specs=placed,
        out_specs=(P(None, None, "gx", "yz", None), P(None, ("gx", "yz"))),
        check_vma=False,
    )
```

```python
import functools

import jax
import jax.numpy as jnp
from jax import lax
from jax.experimental import pallas as pl
from jax.experimental.pallas import tpu as pltpu
from jax.sharding import PartitionSpec as P

time_step = 0.08
mix_coeff = 0.5
span = 8
f32 = jnp.float32
bf16 = jnp.bfloat16
MB = 2**20
WHOLE = pl.BlockSpec(memory_space=pltpu.VMEM)
SCALARS = pl.BlockSpec(memory_space=pltpu.SMEM)


def iota(shape, dim):
    return lax.broadcasted_iota(jnp.int32, shape, dim)


def split(value):
    top = value.astype(bf16).astype(f32)
    return top, value - top


def dot_nt(left, right):
    return lax.dot_general(left, right, (((1,), (1,)), ((), ())), preferred_element_type=f32)


def dot_nn(left, right):
    return lax.dot_general(left, right, (((1,), (0,)), ((), ())), preferred_element_type=f32)


def places(number, width):
    return iota((number, width), 0).astype(f32).astype(bf16)


def tall(row, number):
    part = jnp.broadcast_to(row, (16, row.shape[1])).astype(bf16)
    return jnp.concatenate([part] * (number // 16), axis=0)


def marked(spots, row):
    one, none = jnp.ones((), bf16), jnp.zeros((), bf16)
    return jnp.where(spots == tall(row, spots.shape[0]), one, none)


def call(body, outs, specs, scratch=(), vmem=48, cost=None, name=None):
    return pl.pallas_call(
        body,
        out_shape=tuple(jax.ShapeDtypeStruct(s, d) for s, d in outs),
        in_specs=list(specs),
        out_specs=tuple(WHOLE for _ in outs),
        scratch_shapes=list(scratch),
        compiler_params=pltpu.CompilerParams(vmem_limit_bytes=vmem * MB),
        cost_estimate=cost,
        name=name,
    )


def dispatch_body(dest_ref, cell_ref, phi_ref, off_ref, out_ref, rank_ref, *, bricks, cap):
    rows = dest_ref.shape[1]
    hot = jnp.where(iota((bricks, rows), 0) == dest_ref[...], 1.0, 0.0).astype(bf16)
    key = cell_ref[...] * rows + iota((1, rows), 1)
    key_down = jnp.broadcast_to(key, (8, rows)).T[:, 0:1]
    step = 256
    ranks = []
    for b in range(rows // step):
        cut = slice(b * step, (b + 1) * step)
        before = jnp.where(key_down < key[:, cut], 1.0, 0.0).astype(bf16)
        count = dot_nn(hot, before)
        ranks.append(jnp.sum(hot[:, cut].astype(f32) * count, axis=0, keepdims=True))
    rank = jnp.concatenate(ranks, axis=1).astype(jnp.int32)
    rank_ref[...] = rank
    here = iota((cap, rows), 0) == rank
    channels = [phi_ref[c : c + 1, :] for c in range(4)]
    channels += [off_ref[c : c + 1, :] for c in range(3)]
    channels.append((cell_ref[...] + 1).astype(f32))
    tops, rests = [], []
    for row in channels:
        top, rest = split(row)
        tops.append(jnp.where(here, top, 0.0).astype(bf16))
        rests.append(jnp.where(here, rest, 0.0).astype(bf16))
    sent = dot_nt(jnp.concatenate(tops, axis=0), hot) + dot_nt(
        jnp.concatenate(rests, axis=0), hot
    )
    sent = sent.T
    for r in range(4):
        out_ref[:, r, :] = sent[:, 128 * r : 128 * (r + 1)]


def collect_body(dest_ref, rank_ref, back_ref, out_ref, *, bricks, cap):
    rows = dest_ref.shape[1]
    hot = jnp.where(iota((bricks, rows), 0) == dest_ref[...], 1.0, 0.0).astype(bf16)
    table = jnp.concatenate([back_ref[:, 0, :], back_ref[:, 1, :]], axis=1).T
    top, rest = split(table)
    both = jnp.concatenate([top, rest], axis=1).astype(bf16)
    got = dot_nn(both, jnp.concatenate([hot, hot], axis=0))
    here = iota((cap, rows), 0) == rank_ref[...]
    for c in range(4):
        picked = jnp.where(here, got[c * cap : (c + 1) * cap], 0.0)
        out_ref[c : c + 1, :] = jnp.sum(picked, axis=0, keepdims=True)


def local_body(phi_ref, count_ref, out_ref):
    for x in range(count_ref.shape[0]):
        count = count_ref[x]
        for c in range(4):
            total = None
            for s in range(phi_ref.shape[1]):
                value = jnp.where(count > s, phi_ref[c, s, x], 0.0)
                total = value if total is None else total + value
            out_ref[c, x] = total


def scatter_body(
    arr_ref, local_ref, count_ref, mean_ref, xs_ref, bound_ref, ehi_ref, elo_ref, e15_ref, e01_ref, acc_ref
):
    half = xs_ref.shape[1]
    for r in range(4):
        turned = arr_ref[:, r, :].T
        xs_ref[2 * r] = turned[0:half]
        xs_ref[2 * r + 1] = turned[half : 2 * half]
    code = arr_ref[:, 3, :].astype(jnp.int32) - 1
    line = code >> 11
    bound_ref[0:1, :] = jnp.min(jnp.where(code >= 0, line, 16), axis=0, keepdims=True)
    bound_ref[1:2, :] = jnp.max(jnp.where(code >= 0, line, -1), axis=0, keepdims=True)
    acc_ref[...] = jnp.zeros_like(acc_ref)
    spots = places(256, 128)

    def step(i, carry):
        at = pl.multiple_of(i * 16, 16)
        cell = xs_ref[7, pl.ds(at, 16), :].astype(jnp.int32) - 1
        plane = (cell >> 7).astype(f32)
        depth = (cell & 127).astype(f32)
        parts = [split(xs_ref[c, pl.ds(at, 16), :]) for c in range(4)]
        lefts, rights = [], []
        for u in range(16):
            rights.append(marked(spots, plane[u : u + 1]))
            at_z = marked(spots[0:128], depth[u : u + 1])
            pieces = [at_z]
            for top, rest in parts:
                pieces.append(at_z * tall(top[u : u + 1], 128))
                pieces.append(at_z * tall(rest[u : u + 1], 128))
            lefts.append(jnp.concatenate(pieces, axis=0))
        acc_ref[...] += dot_nt(
            jnp.concatenate(lefts, axis=1), jnp.concatenate(rights, axis=1)
        )
        return carry

    lax.fori_loop(0, half // 16, step, 0)
    wx, wy = count_ref.shape[0], count_ref.shape[1]
    number = acc_ref[0:128, :].T.reshape(wx, wy, 128)
    share = 1.0 / (count_ref[...].astype(f32) + number)
    for c in range(4):
        at = 128 + 256 * c
        moved = (acc_ref[at : at + 128, :] + acc_ref[at + 128 : at + 256, :]).T
        mean = (local_ref[c] + moved.reshape(wx, wy, 128)) * share
        mean_ref[c] = mean
        ehi_ref[c] = mean[wx - 1 : wx]
        elo_ref[c] = mean[0:2]
        e15_ref[c] = mean[:, wy - 1, :]
        e01_ref[0, c] = mean[:, 0, :]
        e01_ref[1, c] = mean[:, 1, :]


def edge_body(lo_ref, hi_ref, e15_ref, e01_ref, up_ref, down_ref):
    wy = lo_ref.shape[2]
    for ref, source, y in (
        (up_ref, lambda c: e15_ref[c], wy - 1),
        (down_ref.at[0], lambda c: e01_ref[0, c], 0),
        (down_ref.at[1], lambda c: e01_ref[1, c], 1),
    ):
        for c in range(4):
            ref[c, 0:16, :] = source(c)
            ref[c, 16:24, :] = jnp.concatenate(
                [
                    hi_ref[c, 0, y : y + 1, :],
                    hi_ref[c, 1, y : y + 1, :],
                    lo_ref[c, 0, y : y + 1, :],
                    jnp.zeros((5, 128), f32),
                ],
                axis=0,
            )


def pencil_x_body(vel_ref, gam_ref, out_ref):
    groups = out_ref.shape[0]
    pieces = [vel_ref[c].reshape(128, vel_ref.shape[3]).T for c in range(3)]
    pieces.append(gam_ref[...].reshape(128, gam_ref.shape[2]).T)
    rows = jnp.concatenate(pieces, axis=1)
    row = iota((8, 512), 0)
    zero = jnp.zeros((8, 512), f32)
    for p in range(groups):
        out_ref[p, 0:16, :] = rows[16 * p : 16 * p + 16]
        above = rows[16 * p + 16 : 16 * p + 24] if p < groups - 1 else zero
        below = pltpu.roll(rows[16 * p - 8 : 16 * p], 3, 0) if p > 0 else zero
        out_ref[p, 16:24, :] = jnp.where(
            row < 2, above, jnp.where(row == 2, below, 0.0)
        )


def pencil_y_body(in_ref, out_ref):
    groups = out_ref.shape[0]
    lane = iota((24, 128), 1)
    zero = jnp.zeros((24, 128), f32)
    for q in range(groups):
        out_ref[q, :, 0:512] = in_ref[2 * q]
        out_ref[q, :, 512:1024] = in_ref[2 * q + 1]
        pieces = []
        for c in range(4):
            lanes = slice(128 * c, 128 * c + 128)
            above = in_ref[2 * q + 2, :, lanes] if q < groups - 1 else zero
            below = pltpu.roll(in_ref[2 * q - 1, :, lanes], 48, 1) if q > 0 else zero
            pieces.append(jnp.where(lane < 32, above, jnp.where(lane < 48, below, 0.0)))
        for e in (0, 1):
            out_ref[q, :, 1024 + 128 * e : 1152 + 128 * e] = jnp.where(
                lane < 64, pieces[2 * e], pltpu.roll(pieces[2 * e + 1], 64, 1)
            )


def brick_body(in_ref, brick_ref, col_ref, tall_ref):
    lane = iota((8, 128), 1)
    for tile in range(10):
        for xt in range(3):
            group = [in_ref[j, 8 * xt : 8 * xt + 8, 128 * tile : 128 * tile + 128] for j in range(8)]
            for bit in (4, 2, 1):
                shift = 16 * bit
                high = (lane // shift) % 2 == 1
                fresh = list(group)
                for j in range(8):
                    if j & bit:
                        continue
                    first, second = group[j], group[j | bit]
                    fresh[j] = jnp.where(high, pltpu.roll(second, shift, 1), first)
                    fresh[j | bit] = jnp.where(high, second, pltpu.roll(first, 128 - shift, 1))
                group = fresh
            for g in range(8):
                if tile < 8:
                    c, y = tile % 4, 8 * (tile // 4) + g
                    at = (c * 16 + y) * 24 + 8 * xt
                    tall_ref[at : at + 8, :] = group[g]
                elif g % 4 < 3:
                    c, y = 2 * (tile - 8) + g // 4, g % 4
                    col_ref[c, y, 8 * xt : 8 * xt + 8, :] = group[g]
    for c in range(4):
        for x in range(19):
            for yt in (0, 8):
                brick_ref[c, x, yt : yt + 8, :] = tall_ref[
                    pl.ds((c * 16 + yt) * 24 + x, 8, stride=24), :
                ]


def z_shift(value, up):
    lane = iota(value.shape, value.ndim - 1)
    if up:
        return jnp.where(lane == 127, 0.0, pltpu.roll(value, 127, value.ndim - 1))
    return jnp.where(lane == 0, 0.0, pltpu.roll(value, 1, value.ndim - 1))


def flux(centre, gamma, sides, velocity):
    total = None
    drift = None
    for (up, gamma_up, down, gamma_down), speed in zip(sides, velocity):
        term = (gamma + gamma_up) * (up - centre) + (gamma + gamma_down) * (down - centre)
        total = term if total is None else total + term
        move = speed * (up - down)
        drift = move if drift is None else drift + move
    return (0.5 * time_step) * (total - drift)


def slot_terms(xs_ref, at):
    def row(c):
        return jnp.concatenate([xs_ref[c, pl.ds(at + e, 1), :] for e in (0, 1)], axis=1)

    cell = row(7).astype(jnp.int32) - 1
    filled = cell >= 0
    depth = cell & 127
    x = jnp.where(filled, cell >> 11, -2)
    y = (cell >> 7) & 15
    return row, x, y, depth


def hat(number, at, frac):
    spot = iota((number, at.shape[1]), 0)
    return jnp.where(spot == at, 1.0 - frac, 0.0) + jnp.where(spot == at + 1, frac, 0.0)


def depth_weights(spots, depth, frac):
    at = depth.astype(f32)
    here = spots == tall(at, 128)
    above = spots == tall(at + 1.0, 128)
    none = jnp.zeros((), bf16)
    parts = []
    for low, high in zip(split(1.0 - frac), split(frac)):
        parts.append(
            jnp.where(here, tall(low, 128), jnp.where(above, tall(high, 128), none))
        )
    return jnp.concatenate([parts[0], parts[0], parts[1]], axis=0)


def widen(tab_ref, lhs_ref):
    top, rest = split(tab_ref[...])
    top = top.astype(bf16)
    lhs_ref[:, 0:128] = top
    lhs_ref[:, 128:256] = rest.astype(bf16)
    lhs_ref[:, 256:384] = top


def total_y(value):
    return jnp.sum(value, axis=0, keepdims=True)


def tile_terms(spots, xs_ref, bound_ref, i):
    row, x, y, depth = slot_terms(xs_ref, 2 * i)
    half = xs_ref.shape[1]
    low = jnp.minimum(bound_ref[0, half + 2 * i], bound_ref[0, half + 2 * i + 1])
    high = jnp.maximum(bound_ref[1, half + 2 * i], bound_ref[1, half + 2 * i + 1])
    windows = (high + 1 - low + span) >> 3
    rows_z = depth_weights(spots, depth, row(6))
    wy = hat(24, y, row(5))
    return row, x, low, windows, rows_z, wy


def window_sums(lhs_ref, per, blocks, low, x, frac, rows_z, wy, sums):
    at = pl.multiple_of(low * per, 16)
    along = dot_nn(lhs_ref[pl.ds(at, span * per), :], rows_z)
    wx = hat(span, x - low, frac)
    sums = list(sums)
    for k in range(span):
        inside = wx[k : k + 1] * wy[0:16]
        for n in range(blocks):
            sums[n] = sums[n] + along[per * k + 16 * n : per * k + 16 * n + 16] * inside
        if len(sums) > blocks:
            rim = wx[k : k + 1] * wy[16:17]
            sums[blocks] = sums[blocks] + along[per * k + 16 * blocks : per * (k + 1)] * rim
    return tuple(sums)


def blend_tiles(lhs_ref, per, blocks, xs_ref, bound_ref, tiles, finish):
    spots = places(128, 256)

    def group(g, carry):
        held = []
        for e in range(tiles):
            i = g * tiles + e
            row, x, low, windows, rows_z, wy = tile_terms(spots, xs_ref, bound_ref, i)
            zero = tuple(jnp.zeros((16, 256), f32) for _ in range(per // 16))
            sums = window_sums(lhs_ref, per, blocks, low, x, row(4), rows_z, wy, zero)
            held.append((i, row, x, low, windows, rows_z, wy, sums))
        for i, row, x, low, windows, rows_z, wy, sums in held:

            def more(w, now):
                return window_sums(
                    lhs_ref, per, blocks, low + span * w, x, row(4), rows_z, wy, now
                )

            finish(i, row, lax.fori_loop(1, windows, more, sums))
        return carry

    lax.fori_loop(0, xs_ref.shape[1] // (2 * tiles), group, 0)


def keep_row(ref, c, i, value):
    for e in (0, 1):
        ref[c, pl.ds(2 * i + e, 1), :] = value[:, 128 * e : 128 * e + 128]


def blend_inner_body(bound_ref, mean_ref, hi_ref, xs_ref, out_ref, tab_ref, lhs_ref):
    for c in range(4):
        for x in range(16):
            tab_ref[64 * x + 16 * c : 64 * x + 16 * c + 16, :] = mean_ref[c, x]
        tab_ref[1024 + 16 * c : 1040 + 16 * c, :] = hi_ref[c, 0]
    tab_ref[1088:, :] = jnp.zeros((64 * (span - 1), 128), f32)
    widen(tab_ref, lhs_ref)

    def finish(i, row, sums):
        for c in range(4):
            keep_row(out_ref, c, i, total_y(sums[c]))

    blend_tiles(lhs_ref, 64, 4, xs_ref, bound_ref, 8, finish)


def transport_body(
    last_ref, mean_ref, lo_ref, hi_ref, ylo_ref, yhi_ref, brick_ref, col_ref, f_ref, rise_ref, mp_ref, gp_ref
):
    x_in = jnp.where(last_ref[0] == 1, 0.0, 1.0).astype(f32)
    y_in = jnp.where(last_ref[1] == 1, 0.0, 1.0).astype(f32)
    for c in range(4):
        mp_ref[c, 0:16, 8:24, :] = mean_ref[c]
        mp_ref[c, 16:18, 8:24, :] = hi_ref[c]
        mp_ref[c, 18, 8:24, :] = lo_ref[c, 0]
        mp_ref[c, :, 7, :] = ylo_ref[c, 0:19, :]
        mp_ref[c, :, 24, :] = yhi_ref[0, c, 0:19, :]
    gp_ref[:, 8:24, :] = brick_ref[3]
    gp_ref[:, 7, :] = col_ref[3, 2, 0:19, :]
    gp_ref[:, 24, :] = col_ref[3, 0, 0:19, :]

    def plane(x, carry):
        below = jnp.where(x == 0, 18, x - 1)
        keep = jnp.where(x == 16, x_in, 1.0)
        gamma = gp_ref[x, 8:24, :]
        gammas = [
            (gp_ref[x + 1, 8:24, :], gp_ref[below, 8:24, :]),
            (gp_ref[x, 9:25, :], gp_ref[x, 7:23, :]),
            (z_shift(gamma, True), z_shift(gamma, False)),
        ]
        velocity = [brick_ref[d, x] for d in range(3)]
        for c in range(4):
            centre = mp_ref[c, x, 8:24, :]
            means = [
                (mp_ref[c, x + 1, 8:24, :], mp_ref[c, below, 8:24, :]),
                (mp_ref[c, x, 9:25, :], mp_ref[c, x, 7:23, :]),
                (z_shift(centre, True), z_shift(centre, False)),
            ]
            sides = [(m[0], g[0], m[1], g[1]) for m, g in zip(means, gammas)]
            moved = flux(centre, gamma, sides, velocity) * keep
            f_ref[c, x, 0:16, :] = centre
            f_ref[4 + c, x, 0:16, :] = moved
            rise_ref[c, x, 0:16, :] = means[2][0] - centre
            rise_ref[4 + c, x, 0:16, :] = z_shift(moved, True) - moved
        f_ref[8, x, 0:16, :] = gamma
        rise_ref[8, x, 0:16, :] = gammas[2][0] - gamma
        return carry

    lax.fori_loop(0, 17, plane, 0)
    row = iota((24, 128), 0)

    def x_up(value):
        return pltpu.roll(value, 23, 0)

    def x_down(value):
        return jnp.where(row == 0, value[18:19], pltpu.roll(value, 1, 0))

    keep = jnp.where(row == 16, x_in, 1.0) * y_in
    gamma = col_ref[3, 0]
    gamma_low = jnp.concatenate([gp_ref[:, 23, :], jnp.zeros((5, 128), f32)], axis=0)
    gammas = [
        (x_up(gamma), x_down(gamma)),
        (col_ref[3, 1], gamma_low),
        (z_shift(gamma, True), z_shift(gamma, False)),
    ]
    velocity = [col_ref[d, 0] for d in range(3)]
    for c in range(4):
        centre = yhi_ref[0, c]
        low = jnp.concatenate([mp_ref[c, :, 23, :], jnp.zeros((5, 128), f32)], axis=0)
        means = [
            (x_up(centre), x_down(centre)),
            (yhi_ref[1, c], low),
            (z_shift(centre, True), z_shift(centre, False)),
        ]
        sides = [(m[0], g[0], m[1], g[1]) for m, g in zip(means, gammas)]
        moved = flux(centre, gamma, sides, velocity) * keep
        f_ref[c, :, 16, :] = centre[0:17]
        f_ref[4 + c, :, 16, :] = moved[0:17]
        rise_ref[c, :, 16, :] = (means[2][0] - centre)[0:17]
        rise_ref[4 + c, :, 16, :] = (z_shift(moved, True) - moved)[0:17]
    f_ref[8, :, 16, :] = gamma[0:17]
    rise_ref[8, :, 16, :] = (gammas[2][0] - gamma)[0:17]


def blend_outer_body(bound_ref, f_ref, inner_ref, xs_ref, out_ref, tab_ref, lhs_ref, new_ref):
    for x in range(17):
        for c in range(5):
            tab_ref[96 * x + 16 * c : 96 * x + 16 * c + 16, :] = f_ref[4 + c, x, 0:16, :]
        tab_ref[96 * x + 80 : 96 * x + 96, :] = jnp.concatenate(
            [f_ref[c, x, 16:17, :] for c in range(9)] + [jnp.zeros((7, 128), f32)], axis=0
        )
    tab_ref[96 * 17 :, :] = jnp.zeros((96 * (span - 1), 128), f32)
    widen(tab_ref, lhs_ref)

    def finish(i, row, sums):
        def inner(c):
            return jnp.concatenate([inner_ref[c, pl.ds(2 * i + e, 1), :] for e in (0, 1)], axis=1)

        rim = sums[5]
        rate = mix_coeff * (total_y(sums[4]) + rim[8:9])
        for c in range(4):
            phi = row(c)
            mean = inner(c) + rim[c : c + 1]
            moved = total_y(sums[c]) + rim[4 + c : 5 + c]
            keep_row(new_ref, c, i, phi + moved - rate * (phi - mean))

    blend_tiles(lhs_ref, 96, 5, xs_ref, bound_ref, 8, finish)
    half = xs_ref.shape[1]
    for r in range(2):
        both = jnp.concatenate([new_ref[2 * r], new_ref[2 * r + 1]], axis=0)
        out_ref[:, r, :] = both.T


def update_body(phi_ref, off_ref, count_ref, f_ref, rise_ref, out_ref, coef_ref):
    deep, wy = count_ref.shape[0], count_ref.shape[1]
    first = pl.program_id(0) * deep
    slots = phi_ref.shape[1]
    width = 4
    for x in range(deep):
        for ch in range(9):
            for sz, ref in enumerate((f_ref, rise_ref)):
                c00 = ref[ch, first + x, 0:wy, :]
                c01 = ref[ch, first + x, 1 : wy + 1, :]
                c10 = ref[ch, first + x + 1, 0:wy, :]
                c11 = ref[ch, first + x + 1, 1 : wy + 1, :]
                dx = c10 - c00
                coef_ref[ch, sz] = c00
                coef_ref[ch, 2 + sz] = c01 - c00
                coef_ref[ch, 4 + sz] = dx
                coef_ref[ch, 6 + sz] = (c11 - c01) - dx
        count = count_ref[x]

        def group(i, carry):
            at = [i * width + s for s in range(width)]
            a = [off_ref[0, s, x] for s in at]
            b = [off_ref[1, s, x] for s in at]
            d = [off_ref[2, s, x] for s in at]

            def blend(ch):
                k = [coef_ref[ch, n] for n in range(8)]
                return [
                    ((k[7] * d[n] + k[6]) * b[n] + (k[5] * d[n] + k[4])) * a[n]
                    + ((k[3] * d[n] + k[2]) * b[n] + (k[1] * d[n] + k[0]))
                    for n in range(width)
                ]

            rate = [mix_coeff * value for value in blend(8)]
            for c in range(4):
                mean = blend(c)
                moved = blend(4 + c)
                for n in range(width):
                    phi = phi_ref[c, at[n], x]
                    fresh = phi + moved[n] - rate[n] * (phi - mean[n])
                    out_ref[c, at[n], x] = jnp.where(count > at[n], fresh, 0.0)
            return carry

        lax.fori_loop(0, slots // width, group, 0)


def shifted(value, axis, by):
    count = lax.axis_size(axis)
    pairs = [(i, i + by) for i in range(count) if 0 <= i + by < count]
    return lax.ppermute(value, axis, pairs)


def exchange(value, axis):
    return lax.all_to_all(value, axis, split_axis=0, concat_axis=0, tiled=True)


def shards(phi, offset, count, velocity, diffusivity, m_phi, m_offset, m_dest, m_cell):
    slots, wx, wy, depth = phi.shape[1:]
    groups_x, groups_y = lax.axis_size("gx"), lax.axis_size("yz")
    bricks = groups_x * groups_y
    rows = m_phi.shape[1]
    cap = 4 * rows // bricks

    dest = m_dest.reshape(1, rows)
    cell = m_cell.reshape(1, rows)
    sent, rank = call(
        functools.partial(dispatch_body, bricks=bricks, cap=cap),
        [((bricks, 4, 128), f32), ((1, rows), jnp.int32)],
        [WHOLE] * 4,
        vmem=60,
        name="dispatch",
    )(dest, cell, m_phi, m_offset)
    arrived = exchange(sent, ("gx", "yz"))

    pencil, = call(
        pencil_x_body, [((groups_x, 24, 512), f32)], [WHOLE] * 2, vmem=8, name="pencil_x"
    )(jnp.transpose(velocity, (0, 2, 3, 1)), jnp.transpose(diffusivity, (1, 2, 0)))
    def blocks(first, deep):
        return pl.BlockSpec((first, slots, deep, wy, depth), lambda i: (0, 0, i, 0, 0))

    def cells(deep):
        return pl.BlockSpec((deep, wy, depth), lambda i: (i, 0, 0))

    local_sum = pl.pallas_call(
        local_body,
        out_shape=jax.ShapeDtypeStruct((4, wx, wy, depth), f32),
        grid=(wx // 8,),
        in_specs=[blocks(4, 8), cells(8)],
        out_specs=pl.BlockSpec((4, 8, wy, depth), lambda i: (0, i, 0, 0)),
        compiler_params=pltpu.CompilerParams(vmem_limit_bytes=60 * MB),
        cost_estimate=pl.CostEstimate(flops=4 * 10**6, bytes_accessed=9 * 10**6, transcendentals=0),
        name="local_sum",
    )(phi, count)

    arrived, local_sum, pencil = lax.optimization_barrier((arrived, local_sum, pencil))
    pencil = exchange(pencil, "gx")
    mean, xs, bound, ehi, elo, e15, e01 = call(
        scatter_body,
        [
            ((4, wx, wy, depth), f32),
            ((8, cap, 128), f32),
            ((2, 128), jnp.int32),
            ((4, 1, wy, depth), f32),
            ((4, 2, wy, depth), f32),
            ((4, wx, depth), f32),
            ((2, 4, wx, depth), f32),
        ],
        [WHOLE] * 3,
        [pltpu.VMEM((9 * 128, 256), f32)],
        vmem=16,
        cost=pl.CostEstimate(flops=4 * 10**9, bytes_accessed=2 * 10**6, transcendentals=0),
        name="scatter",
    )(arrived, local_sum, count)

    pencil, xs = lax.optimization_barrier((pencil, xs))
    lo = shifted(ehi, "gx", 1)
    hi = shifted(elo, "gx", -1)
    wide, = call(
        pencil_y_body, [((groups_y, 24, 1280), f32)], [WHOLE], vmem=8, name="pencil_y"
    )(pencil)
    up, down = call(
        edge_body,
        [((4, 24, depth), f32), ((2, 4, 24, depth), f32)],
        [WHOLE] * 4,
        vmem=4,
        name="edge",
    )(lo, hi, e15, e01)
    ylo = shifted(up, "yz", 1)
    yhi = shifted(down, "yz", -1)
    wide = exchange(wide, "yz")
    inner, = call(
        blend_inner_body,
        [((4, cap, 128), f32)],
        [SCALARS] + [WHOLE] * 3,
        [pltpu.VMEM((1536, 128), f32), pltpu.VMEM((1536, 384), bf16)],
        vmem=16,
        cost=pl.CostEstimate(flops=8 * 10**9, bytes_accessed=3 * 10**6, transcendentals=0),
        name="blend_inner",
    )(bound, mean, hi, xs)
    wide, inner = lax.optimization_barrier((wide, inner))
    brick, col = call(
        brick_body,
        [((4, 19, wy, depth), f32), ((4, 3, 24, depth), f32)],
        [WHOLE],
        [pltpu.VMEM((4 * 16 * 24, 128), f32)],
        vmem=8,
        name="brick",
    )(wide)

    last = jnp.stack(
        [
            (lax.axis_index("gx") == groups_x - 1).astype(jnp.int32),
            (lax.axis_index("yz") == groups_y - 1).astype(jnp.int32),
        ]
    )
    fields, rises = call(
        transport_body,
        [((9, 17, 24, depth), f32), ((9, 17, 24, depth), f32)],
        [SCALARS] + [WHOLE] * 7,
        [pltpu.VMEM((4, 19, 32, 128), f32), pltpu.VMEM((19, 32, 128), f32)],
        vmem=12,
        name="transport",
    )(last, mean, lo, hi, ylo, yhi, brick, col)
    moved_new, = call(
        blend_outer_body,
        [((bricks, 2, 128), f32)],
        [SCALARS] + [WHOLE] * 3,
        [
            pltpu.VMEM((2304, 128), f32),
            pltpu.VMEM((2304, 384), bf16),
            pltpu.VMEM((4, cap, 128), f32),
        ],
        vmem=16,
        name="blend_outer",
    )(bound, fields, inner, xs)
    back = exchange(moved_new, ("gx", "yz"))

    whole = pl.BlockSpec((9, 17, 24, depth), lambda i: (0, 0, 0, 0))
    particle_new = pl.pallas_call(
        update_body,
        out_shape=jax.ShapeDtypeStruct(phi.shape, f32),
        grid=(wx // 2,),
        in_specs=[blocks(4, 2), blocks(3, 2), cells(2), whole, whole],
        out_specs=blocks(4, 2),
        scratch_shapes=[pltpu.VMEM((9, 8, wy, depth), f32)],
        compiler_params=pltpu.CompilerParams(vmem_limit_bytes=60 * MB),
        cost_estimate=pl.CostEstimate(flops=8 * 10**7, bytes_accessed=25 * 10**6, transcendentals=0),
        name="update",
    )(phi, offset, count, fields, rises)

    migrant_new, = call(
        functools.partial(collect_body, bricks=bricks, cap=cap),
        [((4, rows), f32)],
        [WHOLE] * 3,
        vmem=12,
        name="collect",
    )(dest, rank, back)
    return particle_new, migrant_new


def solution(mesh):
    placed = (
        P(None, None, "gx", "yz", None),
        P(None, None, "gx", "yz", None),
        P("gx", "yz", None),
        P(None, None, "gx", "yz"),
        P(None, "gx", "yz"),
        P(None, ("gx", "yz")),
        P(None, ("gx", "yz")),
        P(("gx", "yz"), None),
        P(("gx", "yz")),
    )
    return jax.shard_map(
        shards,
        mesh=mesh,
        in_specs=placed,
        out_specs=(P(None, None, "gx", "yz", None), P(None, ("gx", "yz"))),
        check_vma=False,
    )
```

```python
import functools

import jax
import jax.numpy as jnp
from jax import lax
from jax.experimental import pallas as pl
from jax.experimental.pallas import tpu as pltpu
from jax.sharding import PartitionSpec as P

time_step = 0.08
mix_coeff = 0.5
span = 8
further = 4
tiles_held = 8
f32 = jnp.float32
bf16 = jnp.bfloat16
MB = 2**20
WHOLE = pl.BlockSpec(memory_space=pltpu.VMEM)
SCALARS = pl.BlockSpec(memory_space=pltpu.SMEM)


def iota(shape, dim):
    return lax.broadcasted_iota(jnp.int32, shape, dim)


def split(value):
    top = value.astype(bf16).astype(f32)
    return top, value - top


def dot_nt(left, right):
    return lax.dot_general(left, right, (((1,), (1,)), ((), ())), preferred_element_type=f32)


def dot_nn(left, right):
    return lax.dot_general(left, right, (((1,), (0,)), ((), ())), preferred_element_type=f32)


def places(number, width):
    return iota((number, width), 0).astype(f32).astype(bf16)


def tall(row, number):
    part = jnp.broadcast_to(row, (16, row.shape[1])).astype(bf16)
    return jnp.concatenate([part] * (number // 16), axis=0)


def marked(spots, row):
    one, none = jnp.ones((), bf16), jnp.zeros((), bf16)
    return jnp.where(spots == tall(row, spots.shape[0]), one, none)


def call(body, outs, specs, scratch=(), vmem=48, cost=None, name=None):
    return pl.pallas_call(
        body,
        out_shape=tuple(jax.ShapeDtypeStruct(s, d) for s, d in outs),
        in_specs=list(specs),
        out_specs=tuple(WHOLE for _ in outs),
        scratch_shapes=list(scratch),
        compiler_params=pltpu.CompilerParams(vmem_limit_bytes=vmem * MB),
        cost_estimate=cost,
        name=name,
    )


def dispatch_body(dest_ref, cell_ref, phi_ref, off_ref, out_ref, rank_ref, *, bricks, cap):
    rows = dest_ref.shape[1]
    hot = jnp.where(iota((bricks, rows), 0) == dest_ref[...], 1.0, 0.0).astype(bf16)
    lines = 16
    line = cell_ref[...] >> 11
    on_line = jnp.where(iota((lines, rows), 0) == line, 1.0, 0.0)
    lined = on_line.astype(bf16)
    bucket = (dest_ref[...] * lines + line).astype(f32)
    bucket_down = jnp.broadcast_to(bucket, (8, rows)).T[:, 0:1]
    total = dot_nt(lined, hot)
    lasts = [None] * lines
    left = jnp.full((1, bricks), float(cap), f32)
    for k in range(lines - 1, -1, -1):
        left = left - total[k : k + 1]
        lasts[k] = left
    free = jnp.zeros((1, bricks), f32)
    starts = []
    for k in range(lines):
        free = jnp.maximum(free, float(k * cap // lines))
        starts.append(jnp.minimum(free, lasts[k]))
        free = free + total[k : k + 1]
    base = jnp.concatenate(starts, axis=0)
    step = 256
    earlier = iota((step, step), 0) < iota((step, step), 1)
    ranks = []
    for b in range(rows // step):
        cut = slice(b * step, (b + 1) * step)
        start = dot_nn(base.astype(bf16), hot[:, cut])
        start = jnp.sum(start * on_line[:, cut], axis=0, keepdims=True)
        same = (bucket_down[cut] == bucket[:, cut]) & earlier
        ranks.append(start + jnp.sum(jnp.where(same, 1.0, 0.0), axis=0, keepdims=True))
        base = base + dot_nt(lined[:, cut], hot[:, cut])
    rank = jnp.concatenate(ranks, axis=1).astype(jnp.int32)
    rank_ref[...] = rank
    here = iota((cap, rows), 0) == rank
    channels = [phi_ref[c : c + 1, :] for c in range(4)]
    channels += [off_ref[c : c + 1, :] for c in range(3)]
    channels.append((cell_ref[...] + 1).astype(f32))
    tops, rests = [], []
    for row in channels:
        top, rest = split(row)
        tops.append(jnp.where(here, top, 0.0).astype(bf16))
        rests.append(jnp.where(here, rest, 0.0).astype(bf16))
    sent = dot_nt(jnp.concatenate(tops, axis=0), hot) + dot_nt(
        jnp.concatenate(rests, axis=0), hot
    )
    sent = sent.T
    for r in range(4):
        out_ref[:, r, :] = sent[:, 128 * r : 128 * (r + 1)]


def collect_body(dest_ref, rank_ref, back_ref, out_ref, *, bricks, cap):
    rows = dest_ref.shape[1]
    hot = jnp.where(iota((bricks, rows), 0) == dest_ref[...], 1.0, 0.0).astype(bf16)
    table = jnp.concatenate([back_ref[:, 0, :], back_ref[:, 1, :]], axis=1).T
    top, rest = split(table)
    both = jnp.concatenate([top, rest], axis=1).astype(bf16)
    got = dot_nn(both, jnp.concatenate([hot, hot], axis=0))
    here = iota((cap, rows), 0) == rank_ref[...]
    for c in range(4):
        picked = jnp.where(here, got[c * cap : (c + 1) * cap], 0.0)
        out_ref[c : c + 1, :] = jnp.sum(picked, axis=0, keepdims=True)


def local_body(phi_ref, count_ref, out_ref):
    for x in range(count_ref.shape[0]):
        count = count_ref[x]
        for c in range(4):
            total = None
            for s in range(phi_ref.shape[1]):
                value = jnp.where(count > s, phi_ref[c, s, x], 0.0)
                total = value if total is None else total + value
            out_ref[c, x] = total


def scatter_body(
    arr_ref, local_ref, count_ref, mean_ref, xs_ref, bound_ref, ehi_ref, elo_ref, e15_ref, e01_ref, acc_ref
):
    half = xs_ref.shape[1]
    for r in range(4):
        turned = arr_ref[:, r, :].T
        xs_ref[2 * r] = turned[0:half]
        xs_ref[2 * r + 1] = turned[half : 2 * half]
    code = arr_ref[:, 3, :].astype(jnp.int32) - 1
    line = code >> 11
    bound_ref[0:1, :] = jnp.min(jnp.where(code >= 0, line, 16), axis=0, keepdims=True)
    most = jnp.max(jnp.where(code >= 0, line, -1), axis=0, keepdims=True)
    bound_ref[1:2, :] = most
    place = iota((1, 128), 1) - half
    in_use = jnp.where((place >= 0) & (most >= 0), place + 1, 0)
    used = jnp.max(in_use, axis=1, keepdims=True)
    used = (used + 2 * tiles_held - 1) // (2 * tiles_held)
    bound_ref[2:3, :] = jnp.broadcast_to(used, (1, 128))
    acc_ref[...] = jnp.zeros_like(acc_ref)
    spots = places(256, 128)

    def step(i, carry):
        at = pl.multiple_of(i * 16, 16)
        cell = xs_ref[7, pl.ds(at, 16), :].astype(jnp.int32) - 1
        plane = (cell >> 7).astype(f32)
        depth = (cell & 127).astype(f32)
        parts = [split(xs_ref[c, pl.ds(at, 16), :]) for c in range(4)]
        lefts, rights = [], []
        for u in range(16):
            rights.append(marked(spots, plane[u : u + 1]))
            at_z = marked(spots[0:128], depth[u : u + 1])
            pieces = [at_z]
            for top, rest in parts:
                pieces.append(at_z * tall(top[u : u + 1], 128))
                pieces.append(at_z * tall(rest[u : u + 1], 128))
            lefts.append(jnp.concatenate(pieces, axis=0))
        acc_ref[...] += dot_nt(
            jnp.concatenate(lefts, axis=1), jnp.concatenate(rights, axis=1)
        )
        return carry

    lax.fori_loop(0, half // 16, step, 0)
    wx, wy = count_ref.shape[0], count_ref.shape[1]
    number = acc_ref[0:128, :].T.reshape(wx, wy, 128)
    share = 1.0 / (count_ref[...].astype(f32) + number)
    for c in range(4):
        at = 128 + 256 * c
        moved = (acc_ref[at : at + 128, :] + acc_ref[at + 128 : at + 256, :]).T
        mean = (local_ref[c] + moved.reshape(wx, wy, 128)) * share
        mean_ref[c] = mean
        ehi_ref[c] = mean[wx - 1 : wx]
        elo_ref[c] = mean[0:2]
        e15_ref[c] = mean[:, wy - 1, :]
        e01_ref[0, c] = mean[:, 0, :]
        e01_ref[1, c] = mean[:, 1, :]


def edge_body(lo_ref, hi_ref, e15_ref, e01_ref, up_ref, down_ref):
    wy = lo_ref.shape[2]
    for ref, source, y in (
        (up_ref, lambda c: e15_ref[c], wy - 1),
        (down_ref.at[0], lambda c: e01_ref[0, c], 0),
        (down_ref.at[1], lambda c: e01_ref[1, c], 1),
    ):
        for c in range(4):
            ref[c, 0:16, :] = source(c)
            ref[c, 16:24, :] = jnp.concatenate(
                [
                    hi_ref[c, 0, y : y + 1, :],
                    hi_ref[c, 1, y : y + 1, :],
                    lo_ref[c, 0, y : y + 1, :],
                    jnp.zeros((5, 128), f32),
                ],
                axis=0,
            )


def pencil_x_body(vel_ref, gam_ref, out_ref):
    groups = out_ref.shape[0]
    pieces = [vel_ref[c].reshape(128, vel_ref.shape[3]).T for c in range(3)]
    pieces.append(gam_ref[...].reshape(128, gam_ref.shape[2]).T)
    rows = jnp.concatenate(pieces, axis=1)
    row = iota((8, 512), 0)
    zero = jnp.zeros((8, 512), f32)
    for p in range(groups):
        out_ref[p, 0:16, :] = rows[16 * p : 16 * p + 16]
        above = rows[16 * p + 16 : 16 * p + 24] if p < groups - 1 else zero
        below = pltpu.roll(rows[16 * p - 8 : 16 * p], 3, 0) if p > 0 else zero
        out_ref[p, 16:24, :] = jnp.where(
            row < 2, above, jnp.where(row == 2, below, 0.0)
        )


def pencil_y_body(in_ref, out_ref):
    groups = out_ref.shape[0]
    lane = iota((24, 128), 1)
    line = lane[0:16]
    zero = jnp.zeros((24, 128), f32)
    for q in range(groups):
        out_ref[q, :, 0:512] = in_ref[2 * q, 0:16, :]
        out_ref[q, :, 512:1024] = in_ref[2 * q + 1, 0:16, :]
        pieces = []
        for c in range(4):
            lanes = slice(128 * c, 128 * c + 128)
            above = in_ref[2 * q + 2, :, lanes] if q < groups - 1 else zero
            below = zero
            if c == 3 and q > 0:
                below = pltpu.roll(in_ref[2 * q - 1, :, lanes], 48, 1)
            pieces.append(jnp.where(lane < 32, above, jnp.where(lane < 48, below, 0.0)))
        first, second, third, fourth = pieces
        second = pltpu.roll(second, 16, 1)
        third = pltpu.roll(third, 32, 1)
        speeds = jnp.where(lane < 16, first, jnp.where(lane < 32, second, third))
        rows = [
            in_ref[2 * q + h, 16:17, 128 * c : 128 * c + 128] for c in range(3) for h in (0, 1)
        ]
        rows += [
            in_ref[2 * q + h, 16 + e : 17 + e, 384:512] for e in range(3) for h in (0, 1)
        ]
        rows.append(speeds[16:17])
        rows.append(fourth[16:19])
        out_ref[q, :, 1024:1152] = jnp.concatenate(rows, axis=0)
        out_ref[q, :, 1152:1280] = jnp.where(
            line < 48, speeds[0:16], pltpu.roll(fourth[0:16], 48, 1)
        )


def turned_lanes(group, lane):
    for bit in (4, 2, 1):
        shift = 16 * bit
        high = (lane // shift) % 2 == 1
        fresh = list(group)
        for j in range(8):
            if j & bit:
                continue
            first, second = group[j], group[j | bit]
            if bit == 4:
                moved = pltpu.roll(jnp.where(high, first, second), shift, 1)
                fresh[j] = jnp.where(high, moved, first)
                fresh[j | bit] = jnp.where(high, second, moved)
            else:
                fresh[j] = jnp.where(high, pltpu.roll(second, shift, 1), first)
                fresh[j | bit] = jnp.where(high, second, pltpu.roll(first, 128 - shift, 1))
        group = fresh
    return group


def brick_part(in_ref, brick_ref, col_ref, tall_ref):
    lane = iota((8, 128), 1)
    col_ref[...] = jnp.zeros_like(col_ref)
    for tile in range(10):
        for xt in range(2):
            group = turned_lanes(
                [in_ref[j, 8 * xt : 8 * xt + 8, 128 * tile : 128 * tile + 128] for j in range(8)],
                lane,
            )
            for g in range(8):
                if tile < 8:
                    at = (16 * (tile % 4) + 8 * (tile // 4) + g) * 24 + 8 * xt
                    tall_ref[at : at + 8, :] = group[g]
                elif tile == 9:
                    if g < 6:
                        c, y = (g, 0) if g < 3 else (3, g - 3)
                        col_ref[c, y, 8 * xt : 8 * xt + 8, :] = group[g]
                else:
                    for k in range(8):
                        n = 8 * xt + k
                        if n < 12:
                            c, e = (n // 2, 0) if n < 6 else (3, (n - 6) // 2)
                            at = (16 * c + 8 * (n % 2) + g) * 24 + 16 + e
                            tall_ref[at : at + 1, :] = group[g][k : k + 1]
                        elif n == 12 and g < 3:
                            col_ref[g, 0, 16:17, :] = group[g][k : k + 1]
                        elif n > 12 and g < 3:
                            col_ref[3, g, n + 3 : n + 4, :] = group[g][k : k + 1]
    for c in range(4):
        for x in range(19 if c == 3 else 17):
            for yt in (0, 8):
                brick_ref[c, x, yt : yt + 8, :] = tall_ref[
                    pl.ds((c * 16 + yt) * 24 + x, 8, stride=24), :
                ]


def z_shift(value, up):
    lane = iota(value.shape, value.ndim - 1)
    if up:
        return jnp.where(lane == 127, 0.0, pltpu.roll(value, 127, value.ndim - 1))
    return jnp.where(lane == 0, 0.0, pltpu.roll(value, 1, value.ndim - 1))


def flux(centre, gamma, sides, velocity):
    total = None
    drift = None
    for (up, gamma_up, down, gamma_down), speed in zip(sides, velocity):
        term = (gamma + gamma_up) * (up - centre) + (gamma + gamma_down) * (down - centre)
        total = term if total is None else total + term
        move = speed * (up - down)
        drift = move if drift is None else drift + move
    return (0.5 * time_step) * (total - drift)


def slot_terms(xs_ref, at):
    def row(c):
        return jnp.concatenate([xs_ref[c, pl.ds(at + e, 1), :] for e in (0, 1)], axis=1)

    cell = row(7).astype(jnp.int32) - 1
    filled = cell >= 0
    depth = cell & 127
    x = jnp.where(filled, cell >> 11, -2)
    y = (cell >> 7) & 15
    return row, x, y, depth


def hat(number, at, frac):
    spot = iota((number, at.shape[1]), 0)
    return jnp.where(spot == at, 1.0 - frac, 0.0) + jnp.where(spot == at + 1, frac, 0.0)


def depth_weights(spots, depth, frac):
    at = depth.astype(f32)
    here = spots == tall(at, 128)
    above = spots == tall(at + 1.0, 128)
    none = jnp.zeros((), bf16)
    parts = []
    for low, high in zip(split(1.0 - frac), split(frac)):
        parts.append(
            jnp.where(here, tall(low, 128), jnp.where(above, tall(high, 128), none))
        )
    return jnp.concatenate([parts[0], parts[0], parts[1]], axis=0)


def widen(tab_ref, lhs_ref):
    top, rest = split(tab_ref[...])
    top = top.astype(bf16)
    lhs_ref[:, 0:128] = top
    lhs_ref[:, 128:256] = rest.astype(bf16)
    lhs_ref[:, 256:384] = top


def total_y(value):
    return jnp.sum(value, axis=0, keepdims=True)


def tile_terms(spots, xs_ref, bound_ref, i):
    row, x, y, depth = slot_terms(xs_ref, 2 * i)
    half = xs_ref.shape[1]
    low = jnp.minimum(bound_ref[0, half + 2 * i], bound_ref[0, half + 2 * i + 1])
    high = jnp.maximum(bound_ref[1, half + 2 * i], bound_ref[1, half + 2 * i + 1])
    windows = (high + 1 - low - span + further) >> 2
    rows_z = depth_weights(spots, depth, row(6))
    wy = hat(24, y, row(5))
    return row, x, low, windows, rows_z, wy


def window_sums(lhs_ref, planes, per, blocks, low, x, frac, rows_z, wy, sums):
    at = pl.multiple_of(low * per, 16)
    along = dot_nn(lhs_ref[pl.ds(at, planes * per), :], rows_z)
    wx = hat(8, x - low, frac)
    sums = list(sums)
    for k in range(planes):
        inside = wx[k : k + 1] * wy[0:16]
        for n in range(blocks):
            sums[n] = sums[n] + along[per * k + 16 * n : per * k + 16 * n + 16] * inside
        if len(sums) > blocks:
            rim = wx[k : k + 1] * wy[16:17]
            sums[blocks] = sums[blocks] + along[per * k + 16 * blocks : per * (k + 1)] * rim
    return tuple(sums)


def blend_tiles(lhs_ref, per, blocks, xs_ref, bound_ref, tiles, finish):
    spots = places(128, 256)
    zero = tuple(jnp.zeros((16, 256), f32) for _ in range(per // 16))

    def group(g, carry):
        held = []
        for e in range(tiles):
            i = g * tiles + e
            row, x, low, windows, rows_z, wy = tile_terms(spots, xs_ref, bound_ref, i)
            args = (x, row(4), rows_z, wy)
            sums = window_sums(lhs_ref, span, per, blocks, low, *args, zero)
            held.append((i, row, low + span, windows, args, sums))
        for i, row, start, windows, args, sums in held:

            def more(w, now):
                return window_sums(
                    lhs_ref, further, per, blocks, start + further * w, *args, now
                )

            finish(i, row, lax.fori_loop(0, windows, more, sums))
        return carry

    lax.fori_loop(0, bound_ref[2, 0], group, 0)


def keep_row(ref, c, i, value):
    for e in (0, 1):
        ref[c, pl.ds(2 * i + e, 1), :] = value[:, 128 * e : 128 * e + 128]


def blend_inner_body(bound_ref, mean_ref, hi_ref, xs_ref, out_ref, tab_ref, lhs_ref):
    for c in range(4):
        for x in range(16):
            tab_ref[64 * x + 16 * c : 64 * x + 16 * c + 16, :] = mean_ref[c, x]
        tab_ref[1024 + 16 * c : 1040 + 16 * c, :] = hi_ref[c, 0]
    tab_ref[1088:, :] = jnp.zeros((64 * (span - 1), 128), f32)
    widen(tab_ref, lhs_ref)
    out_ref[...] = jnp.zeros_like(out_ref)

    def finish(i, row, sums):
        for c in range(4):
            keep_row(out_ref, c, i, total_y(sums[c]))

    blend_tiles(lhs_ref, 64, 4, xs_ref, bound_ref, tiles_held, finish)


def transport_part(
    last_ref, mean_ref, lo_ref, hi_ref, ylo_ref, yhi_ref, brick_ref, col_ref, f_ref, rise_ref, mp_ref, gp_ref
):
    x_in = jnp.where(last_ref[0] == 1, 0.0, 1.0).astype(f32)
    y_in = jnp.where(last_ref[1] == 1, 0.0, 1.0).astype(f32)
    for c in range(4):
        mp_ref[c, 0:16, 8:24, :] = mean_ref[c]
        mp_ref[c, 16:18, 8:24, :] = hi_ref[c]
        mp_ref[c, 18, 8:24, :] = lo_ref[c, 0]
        mp_ref[c, :, 7, :] = ylo_ref[c, 0:19, :]
        mp_ref[c, :, 24, :] = yhi_ref[0, c, 0:19, :]
    gp_ref[:, 8:24, :] = brick_ref[3]
    gp_ref[:, 7, :] = col_ref[3, 2, 0:19, :]
    gp_ref[:, 24, :] = col_ref[3, 0, 0:19, :]

    def plane(x, carry):
        below = jnp.where(x == 0, 18, x - 1)
        keep = jnp.where(x == 16, x_in, 1.0)
        gamma = gp_ref[x, 8:24, :]
        gammas = [
            (gp_ref[x + 1, 8:24, :], gp_ref[below, 8:24, :]),
            (gp_ref[x, 9:25, :], gp_ref[x, 7:23, :]),
            (z_shift(gamma, True), z_shift(gamma, False)),
        ]
        velocity = [brick_ref[d, x] for d in range(3)]
        for c in range(4):
            centre = mp_ref[c, x, 8:24, :]
            means = [
                (mp_ref[c, x + 1, 8:24, :], mp_ref[c, below, 8:24, :]),
                (mp_ref[c, x, 9:25, :], mp_ref[c, x, 7:23, :]),
                (z_shift(centre, True), z_shift(centre, False)),
            ]
            sides = [(m[0], g[0], m[1], g[1]) for m, g in zip(means, gammas)]
            moved = flux(centre, gamma, sides, velocity) * keep
            f_ref[c, x, 0:16, :] = centre
            f_ref[4 + c, x, 0:16, :] = moved
            rise_ref[c, x, 0:16, :] = means[2][0] - centre
            rise_ref[4 + c, x, 0:16, :] = z_shift(moved, True) - moved
        f_ref[8, x, 0:16, :] = gamma
        rise_ref[8, x, 0:16, :] = gammas[2][0] - gamma
        return carry

    lax.fori_loop(0, 17, plane, 0)
    row = iota((24, 128), 0)

    def x_up(value):
        return pltpu.roll(value, 23, 0)

    def x_down(value):
        return jnp.where(row == 0, value[18:19], pltpu.roll(value, 1, 0))

    keep = jnp.where(row == 16, x_in, 1.0) * y_in
    gamma = col_ref[3, 0]
    gamma_low = jnp.concatenate([gp_ref[:, 23, :], jnp.zeros((5, 128), f32)], axis=0)
    gammas = [
        (x_up(gamma), x_down(gamma)),
        (col_ref[3, 1], gamma_low),
        (z_shift(gamma, True), z_shift(gamma, False)),
    ]
    velocity = [col_ref[d, 0] for d in range(3)]
    for c in range(4):
        centre = yhi_ref[0, c]
        low = jnp.concatenate([mp_ref[c, :, 23, :], jnp.zeros((5, 128), f32)], axis=0)
        means = [
            (x_up(centre), x_down(centre)),
            (yhi_ref[1, c], low),
            (z_shift(centre, True), z_shift(centre, False)),
        ]
        sides = [(m[0], g[0], m[1], g[1]) for m, g in zip(means, gammas)]
        moved = flux(centre, gamma, sides, velocity) * keep
        f_ref[c, :, 16, :] = centre[0:17]
        f_ref[4 + c, :, 16, :] = moved[0:17]
        rise_ref[c, :, 16, :] = (means[2][0] - centre)[0:17]
        rise_ref[4 + c, :, 16, :] = (z_shift(moved, True) - moved)[0:17]
    f_ref[8, :, 16, :] = gamma[0:17]
    rise_ref[8, :, 16, :] = (gammas[2][0] - gamma)[0:17]


def outer_part(bound_ref, f_ref, inner_ref, xs_ref, out_ref, tab_ref, lhs_ref, new_ref):
    for x in range(17):
        for c in range(5):
            tab_ref[96 * x + 16 * c : 96 * x + 16 * c + 16, :] = f_ref[4 + c, x, 0:16, :]
        tab_ref[96 * x + 80 : 96 * x + 96, :] = jnp.concatenate(
            [f_ref[c, x, 16:17, :] for c in range(9)] + [jnp.zeros((7, 128), f32)], axis=0
        )
    tab_ref[96 * 17 :, :] = jnp.zeros((96 * (span - 1), 128), f32)
    widen(tab_ref, lhs_ref)
    new_ref[...] = jnp.zeros_like(new_ref)

    def finish(i, row, sums):
        def inner(c):
            return jnp.concatenate([inner_ref[c, pl.ds(2 * i + e, 1), :] for e in (0, 1)], axis=1)

        rim = sums[5]
        rate = mix_coeff * (total_y(sums[4]) + rim[8:9])
        for c in range(4):
            phi = row(c)
            mean = inner(c) + rim[c : c + 1]
            moved = total_y(sums[c]) + rim[4 + c : 5 + c]
            keep_row(new_ref, c, i, phi + moved - rate * (phi - mean))

    blend_tiles(lhs_ref, 96, 5, xs_ref, bound_ref, tiles_held, finish)
    half = xs_ref.shape[1]
    for r in range(2):
        both = jnp.concatenate([new_ref[2 * r], new_ref[2 * r + 1]], axis=0)
        out_ref[:, r, :] = both.T


def fields_body(
    last_ref, bound_ref, wide_ref, mean_ref, lo_ref, hi_ref, ylo_ref, yhi_ref, inner_ref, xs_ref,
    f_ref, rise_ref, out_ref,
    brick_ref, col_ref, tall_ref, mp_ref, gp_ref, tab_ref, lhs_ref, new_ref,
):
    brick_part(wide_ref, brick_ref, col_ref, tall_ref)
    transport_part(
        last_ref, mean_ref, lo_ref, hi_ref, ylo_ref, yhi_ref, brick_ref, col_ref, f_ref, rise_ref, mp_ref, gp_ref
    )
    outer_part(bound_ref, f_ref, inner_ref, xs_ref, out_ref, tab_ref, lhs_ref, new_ref)


def update_body(phi_ref, off_ref, count_ref, f_ref, rise_ref, out_ref, coef_ref):
    deep, wy = count_ref.shape[0], count_ref.shape[1]
    first = pl.program_id(0) * deep
    slots = phi_ref.shape[1]
    width = 4
    for x in range(deep):
        for ch in range(9):
            for sz, ref in enumerate((f_ref, rise_ref)):
                c00 = ref[ch, first + x, 0:wy, :]
                c01 = ref[ch, first + x, 1 : wy + 1, :]
                c10 = ref[ch, first + x + 1, 0:wy, :]
                c11 = ref[ch, first + x + 1, 1 : wy + 1, :]
                dx = c10 - c00
                coef_ref[ch, sz] = c00
                coef_ref[ch, 2 + sz] = c01 - c00
                coef_ref[ch, 4 + sz] = dx
                coef_ref[ch, 6 + sz] = (c11 - c01) - dx
        count = count_ref[x]

        def group(i, carry):
            at = [i * width + s for s in range(width)]
            a = [off_ref[0, s, x] for s in at]
            b = [off_ref[1, s, x] for s in at]
            d = [off_ref[2, s, x] for s in at]

            def blend(ch):
                k = [coef_ref[ch, n] for n in range(8)]
                return [
                    ((k[7] * d[n] + k[6]) * b[n] + (k[5] * d[n] + k[4])) * a[n]
                    + ((k[3] * d[n] + k[2]) * b[n] + (k[1] * d[n] + k[0]))
                    for n in range(width)
                ]

            rate = [mix_coeff * value for value in blend(8)]
            for c in range(4):
                mean = blend(c)
                moved = blend(4 + c)
                for n in range(width):
                    phi = phi_ref[c, at[n], x]
                    fresh = phi + moved[n] - rate[n] * (phi - mean[n])
                    out_ref[c, at[n], x] = jnp.where(count > at[n], fresh, 0.0)
            return carry

        lax.fori_loop(0, slots // width, group, 0)


def shifted(value, axis, by):
    count = lax.axis_size(axis)
    pairs = [(i, i + by) for i in range(count) if 0 <= i + by < count]
    return lax.ppermute(value, axis, pairs)


def exchange(value, axis):
    return lax.all_to_all(value, axis, split_axis=0, concat_axis=0, tiled=True)


def shards(phi, offset, count, velocity, diffusivity, m_phi, m_offset, m_dest, m_cell):
    slots, wx, wy, depth = phi.shape[1:]
    groups_x, groups_y = lax.axis_size("gx"), lax.axis_size("yz")
    bricks = groups_x * groups_y
    rows = m_phi.shape[1]
    cap = 4 * rows // bricks

    dest = m_dest.reshape(1, rows)
    cell = m_cell.reshape(1, rows)
    sent, rank = call(
        functools.partial(dispatch_body, bricks=bricks, cap=cap),
        [((bricks, 4, 128), f32), ((1, rows), jnp.int32)],
        [WHOLE] * 4,
        vmem=60,
        name="dispatch",
    )(dest, cell, m_phi, m_offset)
    arrived = exchange(sent, ("gx", "yz"))

    pencil, = call(
        pencil_x_body, [((groups_x, 24, 512), f32)], [WHOLE] * 2, vmem=8, name="pencil_x"
    )(jnp.transpose(velocity, (0, 2, 3, 1)), jnp.transpose(diffusivity, (1, 2, 0)))
    def blocks(first, deep):
        return pl.BlockSpec((first, slots, deep, wy, depth), lambda i: (0, 0, i, 0, 0))

    def cells(deep):
        return pl.BlockSpec((deep, wy, depth), lambda i: (i, 0, 0))

    local_sum = pl.pallas_call(
        local_body,
        out_shape=jax.ShapeDtypeStruct((4, wx, wy, depth), f32),
        grid=(wx // 8,),
        in_specs=[blocks(4, 8), cells(8)],
        out_specs=pl.BlockSpec((4, 8, wy, depth), lambda i: (0, i, 0, 0)),
        compiler_params=pltpu.CompilerParams(vmem_limit_bytes=54 * MB),
        cost_estimate=pl.CostEstimate(flops=4 * 10**6, bytes_accessed=9 * 10**6, transcendentals=0),
        name="local_sum",
    )(phi, count)

    arrived, local_sum, pencil = lax.optimization_barrier((arrived, local_sum, pencil))
    pencil = exchange(pencil, "gx")
    mean, xs, bound, ehi, elo, e15, e01 = call(
        scatter_body,
        [
            ((4, wx, wy, depth), f32),
            ((8, cap, 128), f32),
            ((3, 128), jnp.int32),
            ((4, 1, wy, depth), f32),
            ((4, 2, wy, depth), f32),
            ((4, wx, depth), f32),
            ((2, 4, wx, depth), f32),
        ],
        [WHOLE] * 3,
        [pltpu.VMEM((9 * 128, 256), f32)],
        vmem=16,
        cost=pl.CostEstimate(flops=4 * 10**9, bytes_accessed=2 * 10**6, transcendentals=0),
        name="scatter",
    )(arrived, local_sum, count)

    pencil, xs = lax.optimization_barrier((pencil, xs))
    lo = shifted(ehi, "gx", 1)
    hi = shifted(elo, "gx", -1)
    wide, = call(
        pencil_y_body, [((groups_y, 16, 1280), f32)], [WHOLE], vmem=8, name="pencil_y"
    )(pencil)
    e15, _ = lax.optimization_barrier((e15, wide))
    up, down = call(
        edge_body,
        [((4, 24, depth), f32), ((2, 4, 24, depth), f32)],
        [WHOLE] * 4,
        vmem=4,
        name="edge",
    )(lo, hi, e15, e01)
    ylo = shifted(up, "yz", 1)
    yhi = shifted(down, "yz", -1)
    wide = exchange(wide, "yz")
    inner, = call(
        blend_inner_body,
        [((4, cap, 128), f32)],
        [SCALARS] + [WHOLE] * 3,
        [pltpu.VMEM((1536, 128), f32), pltpu.VMEM((1536, 384), bf16)],
        vmem=16,
        cost=pl.CostEstimate(flops=8 * 10**9, bytes_accessed=3 * 10**6, transcendentals=0),
        name="blend_inner",
    )(bound, mean, hi, xs)
    wide, inner = lax.optimization_barrier((wide, inner))
    last = jnp.stack(
        [
            (lax.axis_index("gx") == groups_x - 1).astype(jnp.int32),
            (lax.axis_index("yz") == groups_y - 1).astype(jnp.int32),
        ]
    )
    fields, rises, moved_new = pl.pallas_call(
        fields_body,
        out_shape=(
            jax.ShapeDtypeStruct((9, 17, 24, depth), f32),
            jax.ShapeDtypeStruct((9, 17, 24, depth), f32),
            jax.ShapeDtypeStruct((bricks, 2, 128), f32),
        ),
        in_specs=[SCALARS] * 2 + [WHOLE] * 8,
        out_specs=(WHOLE, WHOLE, WHOLE),
        scratch_shapes=[
            pltpu.VMEM((4, 19, wy, depth), f32),
            pltpu.VMEM((4, 3, 24, depth), f32),
            pltpu.VMEM((4 * 16 * 24, 128), f32),
            pltpu.VMEM((4, 19, 32, 128), f32),
            pltpu.VMEM((19, 32, 128), f32),
            pltpu.VMEM((2304, 128), f32),
            pltpu.VMEM((2304, 384), bf16),
            pltpu.VMEM((4, cap, 128), f32),
        ],
        compiler_params=pltpu.CompilerParams(vmem_limit_bytes=28 * MB),
        name="fields",
    )(last, bound, wide, mean, lo, hi, ylo, yhi, inner, xs)
    back = exchange(moved_new, ("gx", "yz"))

    particle_new = pl.pallas_call(
        update_body,
        out_shape=jax.ShapeDtypeStruct(phi.shape, f32),
        grid=(wx // 2,),
        in_specs=[blocks(4, 2), blocks(3, 2), cells(2), WHOLE, WHOLE],
        out_specs=blocks(4, 2),
        scratch_shapes=[pltpu.VMEM((9, 8, wy, depth), f32)],
        compiler_params=pltpu.CompilerParams(vmem_limit_bytes=54 * MB),
        cost_estimate=pl.CostEstimate(flops=8 * 10**7, bytes_accessed=25 * 10**6, transcendentals=0),
        name="update",
    )(phi, offset, count, fields, rises)

    migrant_new, = call(
        functools.partial(collect_body, bricks=bricks, cap=cap),
        [((4, rows), f32)],
        [WHOLE] * 3,
        vmem=12,
        name="collect",
    )(dest, rank, back)
    return particle_new, migrant_new


def solution(mesh):
    placed = (
        P(None, None, "gx", "yz", None),
        P(None, None, "gx", "yz", None),
        P("gx", "yz", None),
        P(None, None, "gx", "yz"),
        P(None, "gx", "yz"),
        P(None, ("gx", "yz")),
        P(None, ("gx", "yz")),
        P(("gx", "yz"), None),
        P(("gx", "yz")),
    )
    return jax.shard_map(
        shards,
        mesh=mesh,
        in_specs=placed,
        out_specs=(P(None, None, "gx", "yz", None), P(None, ("gx", "yz"))),
        check_vma=False,
    )
```

```python
import functools

import jax
import jax.numpy as jnp
from jax import lax
from jax.experimental import pallas as pl
from jax.experimental.pallas import tpu as pltpu
from jax.sharding import PartitionSpec as P

time_step = 0.08
mix_coeff = 0.5
span = 8
further = 4
tiles_held = 8
f32 = jnp.float32
bf16 = jnp.bfloat16
MB = 2**20
WHOLE = pl.BlockSpec(memory_space=pltpu.VMEM)
SCALARS = pl.BlockSpec(memory_space=pltpu.SMEM)


def iota(shape, dim):
    return lax.broadcasted_iota(jnp.int32, shape, dim)


def split(value):
    top = value.astype(bf16).astype(f32)
    return top, value - top


def dot_nt(left, right):
    return lax.dot_general(left, right, (((1,), (1,)), ((), ())), preferred_element_type=f32)


def dot_nn(left, right):
    return lax.dot_general(left, right, (((1,), (0,)), ((), ())), preferred_element_type=f32)


def places(number, width):
    return iota((number, width), 0).astype(f32).astype(bf16)


def tall(row, number):
    part = jnp.broadcast_to(row, (16, row.shape[1])).astype(bf16)
    return jnp.concatenate([part] * (number // 16), axis=0)


def marked(spots, row):
    one, none = jnp.ones((), bf16), jnp.zeros((), bf16)
    return jnp.where(spots == tall(row, spots.shape[0]), one, none)


def call(body, outs, specs, scratch=(), vmem=48, cost=None, name=None):
    return pl.pallas_call(
        body,
        out_shape=tuple(jax.ShapeDtypeStruct(s, d) for s, d in outs),
        in_specs=list(specs),
        out_specs=tuple(WHOLE for _ in outs),
        scratch_shapes=list(scratch),
        compiler_params=pltpu.CompilerParams(vmem_limit_bytes=vmem * MB),
        cost_estimate=cost,
        name=name,
    )


def dispatch_body(dest_ref, cell_ref, phi_ref, off_ref, out_ref, rank_ref, *, bricks, cap):
    rows = dest_ref.shape[1]
    hot = jnp.where(iota((bricks, rows), 0) == dest_ref[...], 1.0, 0.0).astype(bf16)
    lines = 16
    line = cell_ref[...] >> 11
    on_line = jnp.where(iota((lines, rows), 0) == line, 1.0, 0.0)
    lined = on_line.astype(bf16)
    bucket = (dest_ref[...] * lines + line).astype(f32)
    bucket_down = jnp.broadcast_to(bucket, (8, rows)).T[:, 0:1]
    total = dot_nt(lined, hot)
    lasts = [None] * lines
    left = jnp.full((1, bricks), float(cap), f32)
    for k in range(lines - 1, -1, -1):
        left = left - total[k : k + 1]
        lasts[k] = left
    free = jnp.zeros((1, bricks), f32)
    starts = []
    for k in range(lines):
        free = jnp.maximum(free, float(k * cap // lines))
        starts.append(jnp.minimum(free, lasts[k]))
        free = free + total[k : k + 1]
    base = jnp.concatenate(starts, axis=0)
    step = 256
    earlier = iota((step, step), 0) < iota((step, step), 1)
    ranks = []
    for b in range(rows // step):
        cut = slice(b * step, (b + 1) * step)
        start = dot_nn(base.astype(bf16), hot[:, cut])
        start = jnp.sum(start * on_line[:, cut], axis=0, keepdims=True)
        same = (bucket_down[cut] == bucket[:, cut]) & earlier
        ranks.append(start + jnp.sum(jnp.where(same, 1.0, 0.0), axis=0, keepdims=True))
        base = base + dot_nt(lined[:, cut], hot[:, cut])
    rank = jnp.concatenate(ranks, axis=1).astype(jnp.int32)
    rank_ref[...] = rank
    here = iota((cap, rows), 0) == rank
    channels = [phi_ref[c : c + 1, :] for c in range(4)]
    channels += [off_ref[c : c + 1, :] for c in range(3)]
    channels.append((cell_ref[...] + 1).astype(f32))
    tops, rests = [], []
    for row in channels:
        top, rest = split(row)
        tops.append(jnp.where(here, top, 0.0).astype(bf16))
        rests.append(jnp.where(here, rest, 0.0).astype(bf16))
    sent = dot_nt(jnp.concatenate(tops, axis=0), hot) + dot_nt(
        jnp.concatenate(rests, axis=0), hot
    )
    sent = sent.T
    for r in range(4):
        out_ref[:, r, :] = sent[:, 128 * r : 128 * (r + 1)]


def collect_body(dest_ref, rank_ref, back_ref, out_ref, *, bricks, cap):
    rows = dest_ref.shape[1]
    hot = jnp.where(iota((bricks, rows), 0) == dest_ref[...], 1.0, 0.0).astype(bf16)
    table = jnp.concatenate([back_ref[:, 0, :], back_ref[:, 1, :]], axis=1).T
    top, rest = split(table)
    both = jnp.concatenate([top, rest], axis=1).astype(bf16)
    got = dot_nn(both, jnp.concatenate([hot, hot], axis=0))
    here = iota((cap, rows), 0) == rank_ref[...]
    for c in range(4):
        picked = jnp.where(here, got[c * cap : (c + 1) * cap], 0.0)
        out_ref[c : c + 1, :] = jnp.sum(picked, axis=0, keepdims=True)


def local_body(phi_ref, count_ref, out_ref):
    for x in range(count_ref.shape[0]):
        count = count_ref[x]
        for c in range(4):
            total = None
            for s in range(phi_ref.shape[1]):
                value = jnp.where(count > s, phi_ref[c, s, x], 0.0)
                total = value if total is None else total + value
            out_ref[c, x] = total


def scatter_body(
    arr_ref, local_ref, count_ref, mean_ref, xs_ref, bound_ref, ehi_ref, elo_ref, e15_ref, e01_ref, acc_ref
):
    half = xs_ref.shape[1]
    for r in range(4):
        turned = arr_ref[:, r, :].T
        xs_ref[2 * r] = turned[0:half]
        xs_ref[2 * r + 1] = turned[half : 2 * half]
    code = arr_ref[:, 3, :].astype(jnp.int32) - 1
    line = code >> 11
    bound_ref[0:1, :] = jnp.min(jnp.where(code >= 0, line, 16), axis=0, keepdims=True)
    most = jnp.max(jnp.where(code >= 0, line, -1), axis=0, keepdims=True)
    bound_ref[1:2, :] = most
    place = iota((1, 128), 1) - half
    in_use = jnp.where((place >= 0) & (most >= 0), place + 1, 0)
    used = jnp.max(in_use, axis=1, keepdims=True)
    used = (used + 2 * tiles_held - 1) // (2 * tiles_held)
    bound_ref[2:3, :] = jnp.broadcast_to(used, (1, 128))
    acc_ref[...] = jnp.zeros_like(acc_ref)
    spots = places(256, 128)

    def step(i, carry):
        at = pl.multiple_of(i * 16, 16)
        cell = xs_ref[7, pl.ds(at, 16), :].astype(jnp.int32) - 1
        plane = (cell >> 7).astype(f32)
        depth = (cell & 127).astype(f32)
        parts = [split(xs_ref[c, pl.ds(at, 16), :]) for c in range(4)]
        lefts, rights = [], []
        for u in range(16):
            rights.append(marked(spots, plane[u : u + 1]))
            at_z = marked(spots[0:128], depth[u : u + 1])
            pieces = [at_z]
            for top, rest in parts:
                pieces.append(at_z * tall(top[u : u + 1], 128))
                pieces.append(at_z * tall(rest[u : u + 1], 128))
            lefts.append(jnp.concatenate(pieces, axis=0))
        acc_ref[...] += dot_nt(
            jnp.concatenate(lefts, axis=1), jnp.concatenate(rights, axis=1)
        )
        return carry

    lax.fori_loop(0, half // 16, step, 0)
    wx, wy = count_ref.shape[0], count_ref.shape[1]
    number = acc_ref[0:128, :].T.reshape(wx, wy, 128)
    share = 1.0 / (count_ref[...].astype(f32) + number)
    for c in range(4):
        at = 128 + 256 * c
        moved = (acc_ref[at : at + 128, :] + acc_ref[at + 128 : at + 256, :]).T
        mean = (local_ref[c] + moved.reshape(wx, wy, 128)) * share
        mean_ref[c] = mean
        ehi_ref[c] = mean[wx - 1 : wx]
        elo_ref[c] = mean[0:2]
        e15_ref[c] = mean[:, wy - 1, :]
        e01_ref[0, c] = mean[:, 0, :]
        e01_ref[1, c] = mean[:, 1, :]


def edge_body(lo_ref, hi_ref, e15_ref, e01_ref, up_ref, down_ref):
    wy = lo_ref.shape[2]
    for ref, source, y in (
        (up_ref, lambda c: e15_ref[c], wy - 1),
        (down_ref.at[0], lambda c: e01_ref[0, c], 0),
        (down_ref.at[1], lambda c: e01_ref[1, c], 1),
    ):
        for c in range(4):
            ref[c, 0:16, :] = source(c)
            ref[c, 16:24, :] = jnp.concatenate(
                [
                    hi_ref[c, 0, y : y + 1, :],
                    hi_ref[c, 1, y : y + 1, :],
                    lo_ref[c, 0, y : y + 1, :],
                    jnp.zeros((5, 128), f32),
                ],
                axis=0,
            )


def pencil_x_body(vel_ref, gam_ref, out_ref):
    groups = out_ref.shape[0]
    pieces = [vel_ref[c].reshape(128, vel_ref.shape[3]).T for c in range(3)]
    pieces.append(gam_ref[...].reshape(128, gam_ref.shape[2]).T)
    rows = jnp.concatenate(pieces, axis=1)
    row = iota((8, 512), 0)
    zero = jnp.zeros((8, 512), f32)
    for p in range(groups):
        out_ref[p, 0:16, :] = rows[16 * p : 16 * p + 16]
        above = rows[16 * p + 16 : 16 * p + 24] if p < groups - 1 else zero
        below = pltpu.roll(rows[16 * p - 8 : 16 * p], 3, 0) if p > 0 else zero
        out_ref[p, 16:24, :] = jnp.where(
            row < 2, above, jnp.where(row == 2, below, 0.0)
        )


def pencil_y_body(in_ref, out_ref):
    groups = out_ref.shape[0]
    lane = iota((24, 128), 1)
    line = lane[0:16]
    zero = jnp.zeros((24, 128), f32)
    for q in range(groups):
        out_ref[q, :, 0:512] = in_ref[2 * q, 0:16, :]
        out_ref[q, :, 512:1024] = in_ref[2 * q + 1, 0:16, :]
        pieces = []
        for c in range(4):
            lanes = slice(128 * c, 128 * c + 128)
            above = in_ref[2 * q + 2, :, lanes] if q < groups - 1 else zero
            below = zero
            if c == 3 and q > 0:
                below = pltpu.roll(in_ref[2 * q - 1, :, lanes], 48, 1)
            pieces.append(jnp.where(lane < 32, above, jnp.where(lane < 48, below, 0.0)))
        first, second, third, fourth = pieces
        second = pltpu.roll(second, 16, 1)
        third = pltpu.roll(third, 32, 1)
        speeds = jnp.where(lane < 16, first, jnp.where(lane < 32, second, third))
        rows = [
            in_ref[2 * q + h, 16:17, 128 * c : 128 * c + 128] for c in range(3) for h in (0, 1)
        ]
        rows += [
            in_ref[2 * q + h, 16 + e : 17 + e, 384:512] for e in range(3) for h in (0, 1)
        ]
        rows.append(speeds[16:17])
        rows.append(fourth[16:19])
        out_ref[q, :, 1024:1152] = jnp.concatenate(rows, axis=0)
        out_ref[q, :, 1152:1280] = jnp.where(
            line < 48, speeds[0:16], pltpu.roll(fourth[0:16], 48, 1)
        )


def turned_lanes(group, lane):
    for bit in (4, 2, 1):
        shift = 16 * bit
        high = (lane // shift) % 2 == 1
        fresh = list(group)
        for j in range(8):
            if j & bit:
                continue
            first, second = group[j], group[j | bit]
            if bit == 4:
                moved = pltpu.roll(jnp.where(high, first, second), shift, 1)
                fresh[j] = jnp.where(high, moved, first)
                fresh[j | bit] = jnp.where(high, second, moved)
            else:
                fresh[j] = jnp.where(high, pltpu.roll(second, shift, 1), first)
                fresh[j | bit] = jnp.where(high, second, pltpu.roll(first, 128 - shift, 1))
        group = fresh
    return group


def brick_part(in_ref, brick_ref, col_ref, tall_ref):
    lane = iota((8, 128), 1)
    col_ref[...] = jnp.zeros_like(col_ref)
    for tile in range(10):
        for xt in range(2):
            group = turned_lanes(
                [in_ref[j, 8 * xt : 8 * xt + 8, 128 * tile : 128 * tile + 128] for j in range(8)],
                lane,
            )
            for g in range(8):
                if tile < 8:
                    at = (16 * (tile % 4) + 8 * (tile // 4) + g) * 24 + 8 * xt
                    tall_ref[at : at + 8, :] = group[g]
                elif tile == 9:
                    if g < 6:
                        c, y = (g, 0) if g < 3 else (3, g - 3)
                        col_ref[c, y, 8 * xt : 8 * xt + 8, :] = group[g]
                else:
                    for k in range(8):
                        n = 8 * xt + k
                        if n < 12:
                            c, e = (n // 2, 0) if n < 6 else (3, (n - 6) // 2)
                            at = (16 * c + 8 * (n % 2) + g) * 24 + 16 + e
                            tall_ref[at : at + 1, :] = group[g][k : k + 1]
                        elif n == 12 and g < 3:
                            col_ref[g, 0, 16:17, :] = group[g][k : k + 1]
                        elif n > 12 and g < 3:
                            col_ref[3, g, n + 3 : n + 4, :] = group[g][k : k + 1]
    for c in range(4):
        for x in range(19 if c == 3 else 17):
            for yt in (0, 8):
                brick_ref[c, x, yt : yt + 8, :] = tall_ref[
                    pl.ds((c * 16 + yt) * 24 + x, 8, stride=24), :
                ]


def z_shift(value, up):
    lane = iota(value.shape, value.ndim - 1)
    if up:
        return jnp.where(lane == 127, 0.0, pltpu.roll(value, 127, value.ndim - 1))
    return jnp.where(lane == 0, 0.0, pltpu.roll(value, 1, value.ndim - 1))


def flux(centre, gamma, sides, velocity):
    total = None
    drift = None
    for (up, gamma_up, down, gamma_down), speed in zip(sides, velocity):
        term = (gamma + gamma_up) * (up - centre) + (gamma + gamma_down) * (down - centre)
        total = term if total is None else total + term
        move = speed * (up - down)
        drift = move if drift is None else drift + move
    return (0.5 * time_step) * (total - drift)


def slot_terms(xs_ref, at):
    def row(c):
        return jnp.concatenate([xs_ref[c, pl.ds(at + e, 1), :] for e in (0, 1)], axis=1)

    cell = row(7).astype(jnp.int32) - 1
    filled = cell >= 0
    depth = cell & 127
    x = jnp.where(filled, cell >> 11, -2)
    y = (cell >> 7) & 15
    return row, x, y, depth


def hat(number, at, frac):
    spot = iota((number, at.shape[1]), 0)
    return jnp.where(spot == at, 1.0 - frac, 0.0) + jnp.where(spot == at + 1, frac, 0.0)


def depth_weights(spots, depth, frac):
    at = depth.astype(f32)
    here = spots == tall(at, 128)
    above = spots == tall(at + 1.0, 128)
    none = jnp.zeros((), bf16)
    parts = []
    for low, high in zip(split(1.0 - frac), split(frac)):
        parts.append(
            jnp.where(here, tall(low, 128), jnp.where(above, tall(high, 128), none))
        )
    return jnp.concatenate([parts[0], parts[0], parts[1]], axis=0)


def widen(tab_ref, lhs_ref):
    top, rest = split(tab_ref[...])
    top = top.astype(bf16)
    lhs_ref[:, 0:128] = top
    lhs_ref[:, 128:256] = rest.astype(bf16)
    lhs_ref[:, 256:384] = top


def total_y(value):
    return jnp.sum(value, axis=0, keepdims=True)


def tile_terms(spots, xs_ref, bound_ref, i):
    row, x, y, depth = slot_terms(xs_ref, 2 * i)
    half = xs_ref.shape[1]
    low = jnp.minimum(bound_ref[0, half + 2 * i], bound_ref[0, half + 2 * i + 1])
    high = jnp.maximum(bound_ref[1, half + 2 * i], bound_ref[1, half + 2 * i + 1])
    windows = (high + 1 - low - span + further) >> 2
    rows_z = depth_weights(spots, depth, row(6))
    wy = hat(24, y, row(5))
    return row, x, low, windows, rows_z, wy


def window_sums(lhs_ref, planes, per, blocks, low, x, frac, rows_z, wy, sums):
    at = pl.multiple_of(low * per, 16)
    along = dot_nn(lhs_ref[pl.ds(at, planes * per), :], rows_z)
    wx = hat(8, x - low, frac)
    sums = list(sums)
    for k in range(planes):
        inside = wx[k : k + 1] * wy[0:16]
        for n in range(blocks):
            sums[n] = sums[n] + along[per * k + 16 * n : per * k + 16 * n + 16] * inside
        if len(sums) > blocks:
            rim = wx[k : k + 1] * wy[16:17]
            sums[blocks] = sums[blocks] + along[per * k + 16 * blocks : per * (k + 1)] * rim
    return tuple(sums)


def blend_tiles(lhs_ref, per, blocks, xs_ref, bound_ref, tiles, finish):
    spots = places(128, 256)
    zero = tuple(jnp.zeros((16, 256), f32) for _ in range(per // 16))

    def group(g, carry):
        held = []
        for e in range(tiles):
            i = g * tiles + e
            row, x, low, windows, rows_z, wy = tile_terms(spots, xs_ref, bound_ref, i)
            args = (x, row(4), rows_z, wy)
            sums = window_sums(lhs_ref, span, per, blocks, low, *args, zero)
            held.append((i, row, low + span, windows, args, sums))
        for i, row, start, windows, args, sums in held:

            def more(w, now):
                return window_sums(
                    lhs_ref, further, per, blocks, start + further * w, *args, now
                )

            finish(i, row, lax.fori_loop(0, windows, more, sums))
        return carry

    lax.fori_loop(0, bound_ref[2, 0], group, 0)


def keep_row(ref, c, i, value):
    for e in (0, 1):
        ref[c, pl.ds(2 * i + e, 1), :] = value[:, 128 * e : 128 * e + 128]


def blend_inner_body(bound_ref, mean_ref, hi_ref, xs_ref, out_ref, tab_ref, lhs_ref):
    for c in range(4):
        for x in range(16):
            tab_ref[64 * x + 16 * c : 64 * x + 16 * c + 16, :] = mean_ref[c, x]
        tab_ref[1024 + 16 * c : 1040 + 16 * c, :] = hi_ref[c, 0]
    tab_ref[1088:, :] = jnp.zeros((64 * (span - 1), 128), f32)
    widen(tab_ref, lhs_ref)
    out_ref[...] = jnp.zeros_like(out_ref)

    def finish(i, row, sums):
        for c in range(4):
            keep_row(out_ref, c, i, total_y(sums[c]))

    blend_tiles(lhs_ref, 64, 4, xs_ref, bound_ref, tiles_held, finish)


def transport_part(
    last_ref, mean_ref, lo_ref, hi_ref, ylo_ref, yhi_ref, brick_ref, col_ref, f_ref, rise_ref, mp_ref, gp_ref
):
    x_in = jnp.where(last_ref[0] == 1, 0.0, 1.0).astype(f32)
    y_in = jnp.where(last_ref[1] == 1, 0.0, 1.0).astype(f32)
    for c in range(4):
        mp_ref[c, 0:16, 8:24, :] = mean_ref[c]
        mp_ref[c, 16:18, 8:24, :] = hi_ref[c]
        mp_ref[c, 18, 8:24, :] = lo_ref[c, 0]
        mp_ref[c, :, 7, :] = ylo_ref[c, 0:19, :]
        mp_ref[c, :, 24, :] = yhi_ref[0, c, 0:19, :]
    gp_ref[:, 8:24, :] = brick_ref[3]
    gp_ref[:, 7, :] = col_ref[3, 2, 0:19, :]
    gp_ref[:, 24, :] = col_ref[3, 0, 0:19, :]

    def plane(x, carry):
        below = jnp.where(x == 0, 18, x - 1)
        keep = jnp.where(x == 16, x_in, 1.0)
        gamma = gp_ref[x, 8:24, :]
        gammas = [
            (gp_ref[x + 1, 8:24, :], gp_ref[below, 8:24, :]),
            (gp_ref[x, 9:25, :], gp_ref[x, 7:23, :]),
            (z_shift(gamma, True), z_shift(gamma, False)),
        ]
        velocity = [brick_ref[d, x] for d in range(3)]
        for c in range(4):
            centre = mp_ref[c, x, 8:24, :]
            means = [
                (mp_ref[c, x + 1, 8:24, :], mp_ref[c, below, 8:24, :]),
                (mp_ref[c, x, 9:25, :], mp_ref[c, x, 7:23, :]),
                (z_shift(centre, True), z_shift(centre, False)),
            ]
            sides = [(m[0], g[0], m[1], g[1]) for m, g in zip(means, gammas)]
            moved = flux(centre, gamma, sides, velocity) * keep
            f_ref[c, x, 0:16, :] = centre
            f_ref[4 + c, x, 0:16, :] = moved
            rise_ref[c, x, 0:16, :] = means[2][0] - centre
            rise_ref[4 + c, x, 0:16, :] = z_shift(moved, True) - moved
        f_ref[8, x, 0:16, :] = gamma
        rise_ref[8, x, 0:16, :] = gammas[2][0] - gamma
        return carry

    lax.fori_loop(0, 17, plane, 0)
    row = iota((24, 128), 0)

    def x_up(value):
        return pltpu.roll(value, 23, 0)

    def x_down(value):
        return jnp.where(row == 0, value[18:19], pltpu.roll(value, 1, 0))

    keep = jnp.where(row == 16, x_in, 1.0) * y_in
    gamma = col_ref[3, 0]
    gamma_low = jnp.concatenate([gp_ref[:, 23, :], jnp.zeros((5, 128), f32)], axis=0)
    gammas = [
        (x_up(gamma), x_down(gamma)),
        (col_ref[3, 1], gamma_low),
        (z_shift(gamma, True), z_shift(gamma, False)),
    ]
    velocity = [col_ref[d, 0] for d in range(3)]
    for c in range(4):
        centre = yhi_ref[0, c]
        low = jnp.concatenate([mp_ref[c, :, 23, :], jnp.zeros((5, 128), f32)], axis=0)
        means = [
            (x_up(centre), x_down(centre)),
            (yhi_ref[1, c], low),
            (z_shift(centre, True), z_shift(centre, False)),
        ]
        sides = [(m[0], g[0], m[1], g[1]) for m, g in zip(means, gammas)]
        moved = flux(centre, gamma, sides, velocity) * keep
        f_ref[c, :, 16, :] = centre[0:17]
        f_ref[4 + c, :, 16, :] = moved[0:17]
        rise_ref[c, :, 16, :] = (means[2][0] - centre)[0:17]
        rise_ref[4 + c, :, 16, :] = (z_shift(moved, True) - moved)[0:17]
    f_ref[8, :, 16, :] = gamma[0:17]
    rise_ref[8, :, 16, :] = (gammas[2][0] - gamma)[0:17]


def outer_part(bound_ref, f_ref, inner_ref, xs_ref, out_ref, tab_ref, lhs_ref, new_ref):
    for x in range(17):
        for c in range(5):
            tab_ref[96 * x + 16 * c : 96 * x + 16 * c + 16, :] = f_ref[4 + c, x, 0:16, :]
        tab_ref[96 * x + 80 : 96 * x + 96, :] = jnp.concatenate(
            [f_ref[c, x, 16:17, :] for c in range(9)] + [jnp.zeros((7, 128), f32)], axis=0
        )
    tab_ref[96 * 17 :, :] = jnp.zeros((96 * (span - 1), 128), f32)
    widen(tab_ref, lhs_ref)
    new_ref[...] = jnp.zeros_like(new_ref)

    def finish(i, row, sums):
        def inner(c):
            return jnp.concatenate([inner_ref[c, pl.ds(2 * i + e, 1), :] for e in (0, 1)], axis=1)

        rim = sums[5]
        rate = mix_coeff * (total_y(sums[4]) + rim[8:9])
        for c in range(4):
            phi = row(c)
            mean = inner(c) + rim[c : c + 1]
            moved = total_y(sums[c]) + rim[4 + c : 5 + c]
            keep_row(new_ref, c, i, phi + moved - rate * (phi - mean))

    blend_tiles(lhs_ref, 96, 5, xs_ref, bound_ref, tiles_held, finish)
    half = xs_ref.shape[1]
    for r in range(2):
        both = jnp.concatenate([new_ref[2 * r], new_ref[2 * r + 1]], axis=0)
        out_ref[:, r, :] = both.T


def fields_body(
    last_ref, bound_ref, wide_ref, mean_ref, lo_ref, hi_ref, ylo_ref, yhi_ref, inner_ref, xs_ref,
    both_ref, out_ref,
    f_ref, rise_ref, brick_ref, col_ref, tall_ref, mp_ref, gp_ref, tab_ref, lhs_ref, new_ref, sems,
):
    brick_part(wide_ref, brick_ref, col_ref, tall_ref)
    transport_part(
        last_ref, mean_ref, lo_ref, hi_ref, ylo_ref, yhi_ref, brick_ref, col_ref, f_ref, rise_ref, mp_ref, gp_ref
    )
    first = pltpu.make_async_copy(f_ref, both_ref.at[0], sems.at[0])
    second = pltpu.make_async_copy(rise_ref, both_ref.at[1], sems.at[1])
    first.start()
    second.start()
    outer_part(bound_ref, f_ref, inner_ref, xs_ref, out_ref, tab_ref, lhs_ref, new_ref)
    first.wait()
    second.wait()


def update_body(
    phi_ref, off_ref, count_ref, f_ref, f_next_ref, rise_ref, rise_next_ref, out_ref, coef_ref
):
    deep, wy = count_ref.shape[0], count_ref.shape[1]
    slots = phi_ref.shape[1]
    width = 4
    for x in range(deep):
        for ch in range(9):
            for sz, (ref, after) in enumerate(((f_ref, f_next_ref), (rise_ref, rise_next_ref))):
                high, k = (ref, x + 1) if x + 1 < deep else (after, 0)
                c00 = ref[ch, x, 0:wy, :]
                c01 = ref[ch, x, 1 : wy + 1, :]
                c10 = high[ch, k, 0:wy, :]
                c11 = high[ch, k, 1 : wy + 1, :]
                dx = c10 - c00
                coef_ref[ch, sz] = c00
                coef_ref[ch, 2 + sz] = c01 - c00
                coef_ref[ch, 4 + sz] = dx
                coef_ref[ch, 6 + sz] = (c11 - c01) - dx
        count = count_ref[x]

        def group(i, carry):
            at = [i * width + s for s in range(width)]
            a = [off_ref[0, s, x] for s in at]
            b = [off_ref[1, s, x] for s in at]
            d = [off_ref[2, s, x] for s in at]

            def blend(ch):
                k = [coef_ref[ch, n] for n in range(8)]
                return [
                    ((k[7] * d[n] + k[6]) * b[n] + (k[5] * d[n] + k[4])) * a[n]
                    + ((k[3] * d[n] + k[2]) * b[n] + (k[1] * d[n] + k[0]))
                    for n in range(width)
                ]

            rate = [mix_coeff * value for value in blend(8)]
            for c in range(4):
                mean = blend(c)
                moved = blend(4 + c)
                for n in range(width):
                    phi = phi_ref[c, at[n], x]
                    fresh = phi + moved[n] - rate[n] * (phi - mean[n])
                    out_ref[c, at[n], x] = jnp.where(count > at[n], fresh, 0.0)
            return carry

        lax.fori_loop(0, slots // width, group, 0)


def shifted(value, axis, by):
    count = lax.axis_size(axis)
    pairs = [(i, i + by) for i in range(count) if 0 <= i + by < count]
    return lax.ppermute(value, axis, pairs)


def exchange(value, axis):
    return lax.all_to_all(value, axis, split_axis=0, concat_axis=0, tiled=True)


def shards(phi, offset, count, velocity, diffusivity, m_phi, m_offset, m_dest, m_cell):
    slots, wx, wy, depth = phi.shape[1:]
    groups_x, groups_y = lax.axis_size("gx"), lax.axis_size("yz")
    bricks = groups_x * groups_y
    rows = m_phi.shape[1]
    cap = 4 * rows // bricks

    dest = m_dest.reshape(1, rows)
    cell = m_cell.reshape(1, rows)
    sent, rank = call(
        functools.partial(dispatch_body, bricks=bricks, cap=cap),
        [((bricks, 4, 128), f32), ((1, rows), jnp.int32)],
        [WHOLE] * 4,
        vmem=60,
        name="dispatch",
    )(dest, cell, m_phi, m_offset)
    arrived = exchange(sent, ("gx", "yz"))

    pencil, = call(
        pencil_x_body, [((groups_x, 24, 512), f32)], [WHOLE] * 2, vmem=8, name="pencil_x"
    )(jnp.transpose(velocity, (0, 2, 3, 1)), jnp.transpose(diffusivity, (1, 2, 0)))
    def blocks(first, deep):
        return pl.BlockSpec((first, slots, deep, wy, depth), lambda i: (0, 0, i, 0, 0))

    def cells(deep):
        return pl.BlockSpec((deep, wy, depth), lambda i: (i, 0, 0))

    local_sum = pl.pallas_call(
        local_body,
        out_shape=jax.ShapeDtypeStruct((4, wx, wy, depth), f32),
        grid=(wx // 8,),
        in_specs=[blocks(4, 8), cells(8)],
        out_specs=pl.BlockSpec((4, 8, wy, depth), lambda i: (0, i, 0, 0)),
        compiler_params=pltpu.CompilerParams(vmem_limit_bytes=40 * MB),
        cost_estimate=pl.CostEstimate(flops=4 * 10**6, bytes_accessed=9 * 10**6, transcendentals=0),
        name="local_sum",
    )(phi, count)

    arrived, local_sum, pencil = lax.optimization_barrier((arrived, local_sum, pencil))
    pencil = exchange(pencil, "gx")
    mean, xs, bound, ehi, elo, e15, e01 = call(
        scatter_body,
        [
            ((4, wx, wy, depth), f32),
            ((8, cap, 128), f32),
            ((3, 128), jnp.int32),
            ((4, 1, wy, depth), f32),
            ((4, 2, wy, depth), f32),
            ((4, wx, depth), f32),
            ((2, 4, wx, depth), f32),
        ],
        [WHOLE] * 3,
        [pltpu.VMEM((9 * 128, 256), f32)],
        vmem=16,
        cost=pl.CostEstimate(flops=4 * 10**9, bytes_accessed=2 * 10**6, transcendentals=0),
        name="scatter",
    )(arrived, local_sum, count)

    pencil, xs = lax.optimization_barrier((pencil, xs))
    lo = shifted(ehi, "gx", 1)
    hi = shifted(elo, "gx", -1)
    wide, = call(
        pencil_y_body, [((groups_y, 16, 1280), f32)], [WHOLE], vmem=8, name="pencil_y"
    )(pencil)
    e15, _ = lax.optimization_barrier((e15, wide))
    up, down = call(
        edge_body,
        [((4, 24, depth), f32), ((2, 4, 24, depth), f32)],
        [WHOLE] * 4,
        vmem=4,
        name="edge",
    )(lo, hi, e15, e01)
    ylo = shifted(up, "yz", 1)
    yhi = shifted(down, "yz", -1)
    wide = exchange(wide, "yz")
    inner, = call(
        blend_inner_body,
        [((4, cap, 128), f32)],
        [SCALARS] + [WHOLE] * 3,
        [pltpu.VMEM((1536, 128), f32), pltpu.VMEM((1536, 384), bf16)],
        vmem=16,
        cost=pl.CostEstimate(flops=8 * 10**9, bytes_accessed=3 * 10**6, transcendentals=0),
        name="blend_inner",
    )(bound, mean, hi, xs)
    wide, inner = lax.optimization_barrier((wide, inner))
    last = jnp.stack(
        [
            (lax.axis_index("gx") == groups_x - 1).astype(jnp.int32),
            (lax.axis_index("yz") == groups_y - 1).astype(jnp.int32),
        ]
    )
    both, moved_new = pl.pallas_call(
        fields_body,
        out_shape=(
            jax.ShapeDtypeStruct((8, 9, 17, 24, depth), f32),
            jax.ShapeDtypeStruct((bricks, 2, 128), f32),
        ),
        in_specs=[SCALARS] * 2 + [WHOLE] * 8,
        out_specs=(pl.BlockSpec(memory_space=pl.ANY), WHOLE),
        scratch_shapes=[
            pltpu.VMEM((9, 17, 24, depth), f32),
            pltpu.VMEM((9, 17, 24, depth), f32),
            pltpu.VMEM((4, 19, wy, depth), f32),
            pltpu.VMEM((4, 3, 24, depth), f32),
            pltpu.VMEM((4 * 16 * 24, 128), f32),
            pltpu.VMEM((4, 19, 32, 128), f32),
            pltpu.VMEM((19, 32, 128), f32),
            pltpu.VMEM((2304, 128), f32),
            pltpu.VMEM((2304, 384), bf16),
            pltpu.VMEM((4, cap, 128), f32),
            pltpu.SemaphoreType.DMA((2,)),
        ],
        compiler_params=pltpu.CompilerParams(vmem_limit_bytes=48 * MB),
        name="fields",
    )(last, bound, wide, mean, lo, hi, ylo, yhi, inner, xs)
    back = exchange(moved_new, ("gx", "yz"))

    def planes(entry):
        return (
            pl.BlockSpec((None, 9, 2, 24, depth), lambda i: (entry, 0, i, 0, 0)),
            pl.BlockSpec((None, 9, 1, 24, depth), lambda i: (entry, 0, 2 * i + 2, 0, 0)),
        )

    particle_new = pl.pallas_call(
        update_body,
        out_shape=jax.ShapeDtypeStruct(phi.shape, f32),
        grid=(wx // 2,),
        in_specs=[blocks(4, 2), blocks(3, 2), cells(2), *planes(0), *planes(1)],
        out_specs=blocks(4, 2),
        scratch_shapes=[pltpu.VMEM((9, 8, wy, depth), f32)],
        compiler_params=pltpu.CompilerParams(vmem_limit_bytes=60 * MB),
        cost_estimate=pl.CostEstimate(flops=8 * 10**7, bytes_accessed=25 * 10**6, transcendentals=0),
        name="update",
    )(phi, offset, count, both, both, both, both)

    migrant_new, = call(
        functools.partial(collect_body, bricks=bricks, cap=cap),
        [((4, rows), f32)],
        [WHOLE] * 3,
        vmem=12,
        name="collect",
    )(dest, rank, back)
    return particle_new, migrant_new


def solution(mesh):
    placed = (
        P(None, None, "gx", "yz", None),
        P(None, None, "gx", "yz", None),
        P("gx", "yz", None),
        P(None, None, "gx", "yz"),
        P(None, "gx", "yz"),
        P(None, ("gx", "yz")),
        P(None, ("gx", "yz")),
        P(("gx", "yz"), None),
        P(("gx", "yz")),
    )
    return jax.shard_map(
        shards,
        mesh=mesh,
        in_specs=placed,
        out_specs=(P(None, None, "gx", "yz", None), P(None, ("gx", "yz"))),
        check_vma=False,
    )
```

```python
import functools

import jax
import jax.numpy as jnp
from jax import lax
from jax.experimental import pallas as pl
from jax.experimental.pallas import tpu as pltpu
from jax.sharding import PartitionSpec as P

time_step = 0.08
mix_coeff = 0.5
span = 8
further = 4
tiles_held = 16
f32 = jnp.float32
bf16 = jnp.bfloat16
MB = 2**20
WHOLE = pl.BlockSpec(memory_space=pltpu.VMEM)
SCALARS = pl.BlockSpec(memory_space=pltpu.SMEM)


def iota(shape, dim):
    return lax.broadcasted_iota(jnp.int32, shape, dim)


def split(value):
    top = value.astype(bf16).astype(f32)
    return top, value - top


def dot_nt(left, right):
    return lax.dot_general(left, right, (((1,), (1,)), ((), ())), preferred_element_type=f32)


def dot_nn(left, right):
    return lax.dot_general(left, right, (((1,), (0,)), ((), ())), preferred_element_type=f32)


def places(number, width):
    return iota((number, width), 0).astype(f32).astype(bf16)


def tall(row, number):
    part = jnp.broadcast_to(row, (16, row.shape[1])).astype(bf16)
    return jnp.concatenate([part] * (number // 16), axis=0)


def marked(spots, row):
    one, none = jnp.ones((), bf16), jnp.zeros((), bf16)
    return jnp.where(spots == tall(row, spots.shape[0]), one, none)


def call(body, outs, specs, scratch=(), vmem=48, cost=None, name=None):
    return pl.pallas_call(
        body,
        out_shape=tuple(jax.ShapeDtypeStruct(s, d) for s, d in outs),
        in_specs=list(specs),
        out_specs=tuple(WHOLE for _ in outs),
        scratch_shapes=list(scratch),
        compiler_params=pltpu.CompilerParams(vmem_limit_bytes=vmem * MB),
        cost_estimate=cost,
        name=name,
    )


def dispatch_body(dest_ref, cell_ref, phi_ref, off_ref, out_ref, rank_ref, *, bricks, cap):
    rows = dest_ref.shape[1]
    hot = jnp.where(iota((bricks, rows), 0) == dest_ref[...], 1.0, 0.0).astype(bf16)
    lines = 16
    line = cell_ref[...] >> 11
    on_line = jnp.where(iota((lines, rows), 0) == line, 1.0, 0.0)
    lined = on_line.astype(bf16)
    bucket = (dest_ref[...] * lines + line).astype(f32)
    bucket_down = jnp.broadcast_to(bucket, (8, rows)).T[:, 0:1]
    total = dot_nt(lined, hot)
    lasts = [None] * lines
    left = jnp.full((1, bricks), float(cap), f32)
    for k in range(lines - 1, -1, -1):
        left = left - total[k : k + 1]
        lasts[k] = left
    free = jnp.zeros((1, bricks), f32)
    starts = []
    for k in range(lines):
        free = jnp.maximum(free, float(k * cap // lines))
        starts.append(jnp.minimum(free, lasts[k]))
        free = free + total[k : k + 1]
    base = jnp.concatenate(starts, axis=0)
    step = 256
    earlier = iota((step, step), 0) < iota((step, step), 1)
    ranks = []
    for b in range(rows // step):
        cut = slice(b * step, (b + 1) * step)
        start = dot_nn(base.astype(bf16), hot[:, cut])
        start = jnp.sum(start * on_line[:, cut], axis=0, keepdims=True)
        same = (bucket_down[cut] == bucket[:, cut]) & earlier
        ranks.append(start + jnp.sum(jnp.where(same, 1.0, 0.0), axis=0, keepdims=True))
        base = base + dot_nt(lined[:, cut], hot[:, cut])
    rank = jnp.concatenate(ranks, axis=1).astype(jnp.int32)
    rank_ref[...] = rank
    here = iota((cap, rows), 0) == rank
    channels = [phi_ref[c : c + 1, :] for c in range(4)]
    channels += [off_ref[c : c + 1, :] for c in range(3)]
    channels.append((cell_ref[...] + 1).astype(f32))
    tops, rests = [], []
    for row in channels:
        top, rest = split(row)
        tops.append(jnp.where(here, top, 0.0).astype(bf16))
        rests.append(jnp.where(here, rest, 0.0).astype(bf16))
    sent = dot_nt(jnp.concatenate(tops, axis=0), hot) + dot_nt(
        jnp.concatenate(rests, axis=0), hot
    )
    sent = sent.T
    for r in range(4):
        out_ref[:, r, :] = sent[:, 128 * r : 128 * (r + 1)]


def collect_body(dest_ref, rank_ref, back_ref, out_ref, *, bricks, cap):
    rows = dest_ref.shape[1]
    hot = jnp.where(iota((bricks, rows), 0) == dest_ref[...], 1.0, 0.0).astype(bf16)
    table = jnp.concatenate([back_ref[:, 0, :], back_ref[:, 1, :]], axis=1).T
    top, rest = split(table)
    both = jnp.concatenate([top, rest], axis=1).astype(bf16)
    got = dot_nn(both, jnp.concatenate([hot, hot], axis=0))
    here = iota((cap, rows), 0) == rank_ref[...]
    for c in range(4):
        picked = jnp.where(here, got[c * cap : (c + 1) * cap], 0.0)
        out_ref[c : c + 1, :] = jnp.sum(picked, axis=0, keepdims=True)


def local_body(phi_ref, count_ref, out_ref):
    for x in range(count_ref.shape[0]):
        count = count_ref[x]
        for c in range(4):
            total = None
            for s in range(phi_ref.shape[1]):
                value = jnp.where(count > s, phi_ref[c, s, x], 0.0)
                total = value if total is None else total + value
            out_ref[c, x] = total


def scatter_body(
    arr_ref, local_ref, count_ref, mean_ref, xs_ref, bound_ref, ehi_ref, elo_ref, e15_ref, e01_ref, acc_ref
):
    half = xs_ref.shape[1]
    for r in range(4):
        turned = arr_ref[:, r, :].T
        xs_ref[2 * r] = turned[0:half]
        xs_ref[2 * r + 1] = turned[half : 2 * half]
    code = arr_ref[:, 3, :].astype(jnp.int32) - 1
    line = code >> 11
    bound_ref[0:1, :] = jnp.min(jnp.where(code >= 0, line, 16), axis=0, keepdims=True)
    most = jnp.max(jnp.where(code >= 0, line, -1), axis=0, keepdims=True)
    bound_ref[1:2, :] = most
    place = iota((1, 128), 1) - half
    in_use = jnp.where((place >= 0) & (most >= 0), place + 1, 0)
    used = jnp.max(in_use, axis=1, keepdims=True)
    used = (used + 2 * tiles_held - 1) // (2 * tiles_held)
    bound_ref[2:3, :] = jnp.broadcast_to(used, (1, 128))
    acc_ref[...] = jnp.zeros_like(acc_ref)
    spots = places(256, 128)

    def step(i, carry):
        at = pl.multiple_of(i * 32, 32)
        cell = xs_ref[7, pl.ds(at, 32), :].astype(jnp.int32) - 1
        plane = (cell >> 7).astype(f32)
        depth = (cell & 127).astype(f32)
        parts = [split(xs_ref[c, pl.ds(at, 32), :]) for c in range(4)]
        lefts, rights = [], []
        for u in range(32):
            rights.append(marked(spots, plane[u : u + 1]))
            at_z = marked(spots[0:128], depth[u : u + 1])
            pieces = [at_z]
            for top, rest in parts:
                pieces.append(at_z * tall(top[u : u + 1], 128))
                pieces.append(at_z * tall(rest[u : u + 1], 128))
            lefts.append(jnp.concatenate(pieces, axis=0))
        acc_ref[...] += dot_nt(
            jnp.concatenate(lefts, axis=1), jnp.concatenate(rights, axis=1)
        )
        return carry

    lax.fori_loop(0, half // 32, step, 0)
    wx, wy = count_ref.shape[0], count_ref.shape[1]
    number = acc_ref[0:128, :].T.reshape(wx, wy, 128)
    share = 1.0 / (count_ref[...].astype(f32) + number)
    for c in range(4):
        at = 128 + 256 * c
        moved = (acc_ref[at : at + 128, :] + acc_ref[at + 128 : at + 256, :]).T
        mean = (local_ref[c] + moved.reshape(wx, wy, 128)) * share
        mean_ref[c] = mean
        ehi_ref[c] = mean[wx - 1 : wx]
        elo_ref[c] = mean[0:2]
        e15_ref[c] = mean[:, wy - 1, :]
        e01_ref[0, c] = mean[:, 0, :]
        e01_ref[1, c] = mean[:, 1, :]


def edge_body(lo_ref, hi_ref, e15_ref, e01_ref, up_ref, down_ref):
    wy = lo_ref.shape[2]
    for ref, source, y in (
        (up_ref, lambda c: e15_ref[c], wy - 1),
        (down_ref.at[0], lambda c: e01_ref[0, c], 0),
        (down_ref.at[1], lambda c: e01_ref[1, c], 1),
    ):
        for c in range(4):
            ref[c, 0:16, :] = source(c)
            ref[c, 16:24, :] = jnp.concatenate(
                [
                    hi_ref[c, 0, y : y + 1, :],
                    hi_ref[c, 1, y : y + 1, :],
                    lo_ref[c, 0, y : y + 1, :],
                    jnp.zeros((5, 128), f32),
                ],
                axis=0,
            )


def pencil_x_body(vel_ref, gam_ref, out_ref):
    groups = out_ref.shape[0]
    pieces = [vel_ref[c].reshape(128, vel_ref.shape[3]).T for c in range(3)]
    pieces.append(gam_ref[...].reshape(128, gam_ref.shape[2]).T)
    rows = jnp.concatenate(pieces, axis=1)
    row = iota((8, 512), 0)
    zero = jnp.zeros((8, 512), f32)
    for p in range(groups):
        out_ref[p, 0:16, :] = rows[16 * p : 16 * p + 16]
        above = rows[16 * p + 16 : 16 * p + 24] if p < groups - 1 else zero
        below = pltpu.roll(rows[16 * p - 8 : 16 * p], 3, 0) if p > 0 else zero
        out_ref[p, 16:24, :] = jnp.where(
            row < 2, above, jnp.where(row == 2, below, 0.0)
        )


def pencil_y_body(in_ref, out_ref):
    groups = out_ref.shape[0]
    lane = iota((24, 128), 1)
    line = lane[0:16]
    zero = jnp.zeros((24, 128), f32)
    for q in range(groups):
        out_ref[q, :, 0:512] = in_ref[2 * q, 0:16, :]
        out_ref[q, :, 512:1024] = in_ref[2 * q + 1, 0:16, :]
        pieces = []
        for c in range(4):
            lanes = slice(128 * c, 128 * c + 128)
            above = in_ref[2 * q + 2, :, lanes] if q < groups - 1 else zero
            below = zero
            if c == 3 and q > 0:
                below = pltpu.roll(in_ref[2 * q - 1, :, lanes], 48, 1)
            pieces.append(jnp.where(lane < 32, above, jnp.where(lane < 48, below, 0.0)))
        first, second, third, fourth = pieces
        second = pltpu.roll(second, 16, 1)
        third = pltpu.roll(third, 32, 1)
        speeds = jnp.where(lane < 16, first, jnp.where(lane < 32, second, third))
        rows = [
            in_ref[2 * q + h, 16:17, 128 * c : 128 * c + 128] for c in range(3) for h in (0, 1)
        ]
        rows += [
            in_ref[2 * q + h, 16 + e : 17 + e, 384:512] for e in range(3) for h in (0, 1)
        ]
        rows.append(speeds[16:17])
        rows.append(fourth[16:19])
        out_ref[q, :, 1024:1152] = jnp.concatenate(rows, axis=0)
        out_ref[q, :, 1152:1280] = jnp.where(
            line < 48, speeds[0:16], pltpu.roll(fourth[0:16], 48, 1)
        )


def turned_lanes(group, lane):
    for bit in (4, 2, 1):
        shift = 16 * bit
        high = (lane // shift) % 2 == 1
        fresh = list(group)
        for j in range(8):
            if j & bit:
                continue
            first, second = group[j], group[j | bit]
            if bit == 4:
                moved = pltpu.roll(jnp.where(high, first, second), shift, 1)
                fresh[j] = jnp.where(high, moved, first)
                fresh[j | bit] = jnp.where(high, second, moved)
            else:
                fresh[j] = jnp.where(high, pltpu.roll(second, shift, 1), first)
                fresh[j | bit] = jnp.where(high, second, pltpu.roll(first, 128 - shift, 1))
        group = fresh
    return group


def brick_part(in_ref, brick_ref, col_ref, tall_ref):
    lane = iota((8, 128), 1)
    col_ref[...] = jnp.zeros_like(col_ref)
    for tile in range(10):
        for xt in range(2):
            group = turned_lanes(
                [in_ref[j, 8 * xt : 8 * xt + 8, 128 * tile : 128 * tile + 128] for j in range(8)],
                lane,
            )
            for g in range(8):
                if tile < 8:
                    at = (16 * (tile % 4) + 8 * (tile // 4) + g) * 24 + 8 * xt
                    tall_ref[at : at + 8, :] = group[g]
                elif tile == 9:
                    if g < 6:
                        c, y = (g, 0) if g < 3 else (3, g - 3)
                        col_ref[c, y, 8 * xt : 8 * xt + 8, :] = group[g]
                else:
                    for k in range(8):
                        n = 8 * xt + k
                        if n < 12:
                            c, e = (n // 2, 0) if n < 6 else (3, (n - 6) // 2)
                            at = (16 * c + 8 * (n % 2) + g) * 24 + 16 + e
                            tall_ref[at : at + 1, :] = group[g][k : k + 1]
                        elif n == 12 and g < 3:
                            col_ref[g, 0, 16:17, :] = group[g][k : k + 1]
                        elif n > 12 and g < 3:
                            col_ref[3, g, n + 3 : n + 4, :] = group[g][k : k + 1]
    for c in range(4):
        for x in range(19 if c == 3 else 17):
            for yt in (0, 8):
                brick_ref[c, x, yt : yt + 8, :] = tall_ref[
                    pl.ds((c * 16 + yt) * 24 + x, 8, stride=24), :
                ]


def z_shift(value, up):
    lane = iota(value.shape, value.ndim - 1)
    if up:
        return jnp.where(lane == 127, 0.0, pltpu.roll(value, 127, value.ndim - 1))
    return jnp.where(lane == 0, 0.0, pltpu.roll(value, 1, value.ndim - 1))


def flux(centre, gamma, sides, velocity):
    total = None
    drift = None
    for (up, gamma_up, down, gamma_down), speed in zip(sides, velocity):
        term = (gamma + gamma_up) * (up - centre) + (gamma + gamma_down) * (down - centre)
        total = term if total is None else total + term
        move = speed * (up - down)
        drift = move if drift is None else drift + move
    return (0.5 * time_step) * (total - drift)


def slot_terms(xs_ref, at):
    def row(c):
        return jnp.concatenate([xs_ref[c, pl.ds(at + e, 1), :] for e in (0, 1)], axis=1)

    cell = row(7).astype(jnp.int32) - 1
    filled = cell >= 0
    depth = cell & 127
    x = jnp.where(filled, cell >> 11, -2)
    y = (cell >> 7) & 15
    return row, x, y, depth


def hat(number, at, frac):
    spot = iota((number, at.shape[1]), 0)
    return jnp.where(spot == at, 1.0 - frac, 0.0) + jnp.where(spot == at + 1, frac, 0.0)


def depth_weights(spots, depth, frac):
    at = depth.astype(f32)
    here = spots == tall(at, 128)
    above = spots == tall(at + 1.0, 128)
    none = jnp.zeros((), bf16)
    parts = []
    for low, high in zip(split(1.0 - frac), split(frac)):
        parts.append(
            jnp.where(here, tall(low, 128), jnp.where(above, tall(high, 128), none))
        )
    return jnp.concatenate([parts[0], parts[0], parts[1]], axis=0)


def widen(tab_ref, lhs_ref):
    top, rest = split(tab_ref[...])
    top = top.astype(bf16)
    lhs_ref[:, 0:128] = top
    lhs_ref[:, 128:256] = rest.astype(bf16)
    lhs_ref[:, 256:384] = top


def total_y(value):
    return jnp.sum(value, axis=0, keepdims=True)


def tile_terms(spots, xs_ref, bound_ref, i):
    row, x, y, depth = slot_terms(xs_ref, 2 * i)
    half = xs_ref.shape[1]
    low = jnp.minimum(bound_ref[0, half + 2 * i], bound_ref[0, half + 2 * i + 1])
    high = jnp.maximum(bound_ref[1, half + 2 * i], bound_ref[1, half + 2 * i + 1])
    windows = (high + 1 - low - span + further) >> 2
    rows_z = depth_weights(spots, depth, row(6))
    wy = hat(24, y, row(5))
    return row, x, low, windows, rows_z, wy


def window_sums(lhs_ref, planes, per, blocks, low, x, frac, rows_z, wy, sums):
    at = pl.multiple_of(low * per, 16)
    along = dot_nn(lhs_ref[pl.ds(at, planes * per), :], rows_z)
    wx = hat(8, x - low, frac)
    sums = list(sums)
    for k in range(planes):
        inside = wx[k : k + 1] * wy[0:16]
        for n in range(blocks):
            sums[n] = sums[n] + along[per * k + 16 * n : per * k + 16 * n + 16] * inside
        if len(sums) > blocks:
            rim = wx[k : k + 1] * wy[16:17]
            sums[blocks] = sums[blocks] + along[per * k + 16 * blocks : per * (k + 1)] * rim
    return tuple(sums)


def blend_tiles(lhs_ref, per, blocks, xs_ref, bound_ref, tiles, finish):
    spots = places(128, 256)
    zero = tuple(jnp.zeros((16, 256), f32) for _ in range(per // 16))

    def group(g, carry):
        held = []
        for e in range(tiles):
            i = g * tiles + e
            row, x, low, windows, rows_z, wy = tile_terms(spots, xs_ref, bound_ref, i)
            args = (x, row(4), rows_z, wy)
            sums = window_sums(lhs_ref, span, per, blocks, low, *args, zero)
            held.append((i, row, low + span, windows, args, sums))
        for i, row, start, windows, args, sums in held:

            def more(w, now):
                return window_sums(
                    lhs_ref, further, per, blocks, start + further * w, *args, now
                )

            finish(i, row, lax.fori_loop(0, windows, more, sums))
        return carry

    lax.fori_loop(0, bound_ref[2, 0], group, 0)


def keep_row(ref, c, i, value):
    for e in (0, 1):
        ref[c, pl.ds(2 * i + e, 1), :] = value[:, 128 * e : 128 * e + 128]


def blend_inner_body(bound_ref, mean_ref, hi_ref, xs_ref, out_ref, tab_ref, lhs_ref):
    for c in range(4):
        for x in range(16):
            tab_ref[64 * x + 16 * c : 64 * x + 16 * c + 16, :] = mean_ref[c, x]
        tab_ref[1024 + 16 * c : 1040 + 16 * c, :] = hi_ref[c, 0]
    tab_ref[1088:, :] = jnp.zeros((64 * (span - 1), 128), f32)
    widen(tab_ref, lhs_ref)
    out_ref[...] = jnp.zeros_like(out_ref)

    def finish(i, row, sums):
        for c in range(4):
            keep_row(out_ref, c, i, total_y(sums[c]))

    blend_tiles(lhs_ref, 64, 4, xs_ref, bound_ref, tiles_held, finish)


def transport_part(
    last_ref, mean_ref, lo_ref, hi_ref, ylo_ref, yhi_ref, brick_ref, col_ref, f_ref, rise_ref, mp_ref, gp_ref
):
    x_in = jnp.where(last_ref[0] == 1, 0.0, 1.0).astype(f32)
    y_in = jnp.where(last_ref[1] == 1, 0.0, 1.0).astype(f32)
    for c in range(4):
        mp_ref[c, 0:16, 8:24, :] = mean_ref[c]
        mp_ref[c, 16:18, 8:24, :] = hi_ref[c]
        mp_ref[c, 18, 8:24, :] = lo_ref[c, 0]
        mp_ref[c, :, 7, :] = ylo_ref[c, 0:19, :]
        mp_ref[c, :, 24, :] = yhi_ref[0, c, 0:19, :]
    gp_ref[:, 8:24, :] = brick_ref[3]
    gp_ref[:, 7, :] = col_ref[3, 2, 0:19, :]
    gp_ref[:, 24, :] = col_ref[3, 0, 0:19, :]

    def plane(x, carry):
        below = jnp.where(x == 0, 18, x - 1)
        keep = jnp.where(x == 16, x_in, 1.0)
        gamma = gp_ref[x, 8:24, :]
        gammas = [
            (gp_ref[x + 1, 8:24, :], gp_ref[below, 8:24, :]),
            (gp_ref[x, 9:25, :], gp_ref[x, 7:23, :]),
            (z_shift(gamma, True), z_shift(gamma, False)),
        ]
        velocity = [brick_ref[d, x] for d in range(3)]
        for c in range(4):
            centre = mp_ref[c, x, 8:24, :]
            means = [
                (mp_ref[c, x + 1, 8:24, :], mp_ref[c, below, 8:24, :]),
                (mp_ref[c, x, 9:25, :], mp_ref[c, x, 7:23, :]),
                (z_shift(centre, True), z_shift(centre, False)),
            ]
            sides = [(m[0], g[0], m[1], g[1]) for m, g in zip(means, gammas)]
            moved = flux(centre, gamma, sides, velocity) * keep
            f_ref[c, x, 0:16, :] = centre
            f_ref[4 + c, x, 0:16, :] = moved
            rise_ref[c, x, 0:16, :] = means[2][0] - centre
            rise_ref[4 + c, x, 0:16, :] = z_shift(moved, True) - moved
        f_ref[8, x, 0:16, :] = gamma
        rise_ref[8, x, 0:16, :] = gammas[2][0] - gamma
        return carry

    lax.fori_loop(0, 17, plane, 0)
    row = iota((24, 128), 0)

    def x_up(value):
        return pltpu.roll(value, 23, 0)

    def x_down(value):
        return jnp.where(row == 0, value[18:19], pltpu.roll(value, 1, 0))

    keep = jnp.where(row == 16, x_in, 1.0) * y_in
    gamma = col_ref[3, 0]
    gamma_low = jnp.concatenate([gp_ref[:, 23, :], jnp.zeros((5, 128), f32)], axis=0)
    gammas = [
        (x_up(gamma), x_down(gamma)),
        (col_ref[3, 1], gamma_low),
        (z_shift(gamma, True), z_shift(gamma, False)),
    ]
    velocity = [col_ref[d, 0] for d in range(3)]
    for c in range(4):
        centre = yhi_ref[0, c]
        low = jnp.concatenate([mp_ref[c, :, 23, :], jnp.zeros((5, 128), f32)], axis=0)
        means = [
            (x_up(centre), x_down(centre)),
            (yhi_ref[1, c], low),
            (z_shift(centre, True), z_shift(centre, False)),
        ]
        sides = [(m[0], g[0], m[1], g[1]) for m, g in zip(means, gammas)]
        moved = flux(centre, gamma, sides, velocity) * keep
        f_ref[c, :, 16, :] = centre[0:17]
        f_ref[4 + c, :, 16, :] = moved[0:17]
        rise_ref[c, :, 16, :] = (means[2][0] - centre)[0:17]
        rise_ref[4 + c, :, 16, :] = (z_shift(moved, True) - moved)[0:17]
    f_ref[8, :, 16, :] = gamma[0:17]
    rise_ref[8, :, 16, :] = (gammas[2][0] - gamma)[0:17]


def outer_part(bound_ref, f_ref, inner_ref, xs_ref, out_ref, tab_ref, lhs_ref, new_ref):
    for x in range(17):
        for c in range(5):
            tab_ref[96 * x + 16 * c : 96 * x + 16 * c + 16, :] = f_ref[4 + c, x, 0:16, :]
        tab_ref[96 * x + 80 : 96 * x + 96, :] = jnp.concatenate(
            [f_ref[c, x, 16:17, :] for c in range(9)] + [jnp.zeros((7, 128), f32)], axis=0
        )
    tab_ref[96 * 17 :, :] = jnp.zeros((96 * (span - 1), 128), f32)
    widen(tab_ref, lhs_ref)
    new_ref[...] = jnp.zeros_like(new_ref)

    def finish(i, row, sums):
        def inner(c):
            return jnp.concatenate([inner_ref[c, pl.ds(2 * i + e, 1), :] for e in (0, 1)], axis=1)

        rim = sums[5]
        rate = mix_coeff * (total_y(sums[4]) + rim[8:9])
        for c in range(4):
            phi = row(c)
            mean = inner(c) + rim[c : c + 1]
            moved = total_y(sums[c]) + rim[4 + c : 5 + c]
            keep_row(new_ref, c, i, phi + moved - rate * (phi - mean))

    blend_tiles(lhs_ref, 96, 5, xs_ref, bound_ref, tiles_held, finish)
    half = xs_ref.shape[1]
    for r in range(2):
        both = jnp.concatenate([new_ref[2 * r], new_ref[2 * r + 1]], axis=0)
        out_ref[:, r, :] = both.T


def fields_body(
    last_ref, bound_ref, wide_ref, mean_ref, lo_ref, hi_ref, ylo_ref, yhi_ref, inner_ref, xs_ref,
    both_ref, out_ref,
    f_ref, rise_ref, brick_ref, col_ref, tall_ref, mp_ref, gp_ref, tab_ref, lhs_ref, new_ref, sems,
):
    brick_part(wide_ref, brick_ref, col_ref, tall_ref)
    transport_part(
        last_ref, mean_ref, lo_ref, hi_ref, ylo_ref, yhi_ref, brick_ref, col_ref, f_ref, rise_ref, mp_ref, gp_ref
    )
    first = pltpu.make_async_copy(f_ref, both_ref.at[0], sems.at[0])
    second = pltpu.make_async_copy(rise_ref, both_ref.at[1], sems.at[1])
    first.start()
    second.start()
    outer_part(bound_ref, f_ref, inner_ref, xs_ref, out_ref, tab_ref, lhs_ref, new_ref)
    first.wait()
    second.wait()


def update_body(
    phi_ref, off_ref, count_ref, f_ref, f_next_ref, rise_ref, rise_next_ref, out_ref, coef_ref
):
    deep, wy = count_ref.shape[0], count_ref.shape[1]
    slots = phi_ref.shape[1]
    width = 4
    for x in range(deep):
        for ch in range(9):
            for sz, (ref, after) in enumerate(((f_ref, f_next_ref), (rise_ref, rise_next_ref))):
                high, k = (ref, x + 1) if x + 1 < deep else (after, 0)
                c00 = ref[ch, x, 0:wy, :]
                c01 = ref[ch, x, 1 : wy + 1, :]
                c10 = high[ch, k, 0:wy, :]
                c11 = high[ch, k, 1 : wy + 1, :]
                dx = c10 - c00
                coef_ref[ch, sz] = c00
                coef_ref[ch, 2 + sz] = c01 - c00
                coef_ref[ch, 4 + sz] = dx
                coef_ref[ch, 6 + sz] = (c11 - c01) - dx
        count = count_ref[x]

        def group(i, carry):
            at = [i * width + s for s in range(width)]
            a = [off_ref[0, s, x] for s in at]
            b = [off_ref[1, s, x] for s in at]
            d = [off_ref[2, s, x] for s in at]

            def blend(ch):
                k = [coef_ref[ch, n] for n in range(8)]
                return [
                    ((k[7] * d[n] + k[6]) * b[n] + (k[5] * d[n] + k[4])) * a[n]
                    + ((k[3] * d[n] + k[2]) * b[n] + (k[1] * d[n] + k[0]))
                    for n in range(width)
                ]

            rate = [mix_coeff * value for value in blend(8)]
            for c in range(4):
                mean = blend(c)
                moved = blend(4 + c)
                for n in range(width):
                    phi = phi_ref[c, at[n], x]
                    fresh = phi + moved[n] - rate[n] * (phi - mean[n])
                    out_ref[c, at[n], x] = jnp.where(count > at[n], fresh, 0.0)
            return carry

        lax.fori_loop(0, slots // width, group, 0)


def shifted(value, axis, by):
    count = lax.axis_size(axis)
    pairs = [(i, i + by) for i in range(count) if 0 <= i + by < count]
    return lax.ppermute(value, axis, pairs)


def exchange(value, axis):
    return lax.all_to_all(value, axis, split_axis=0, concat_axis=0, tiled=True)


def shards(phi, offset, count, velocity, diffusivity, m_phi, m_offset, m_dest, m_cell):
    slots, wx, wy, depth = phi.shape[1:]
    groups_x, groups_y = lax.axis_size("gx"), lax.axis_size("yz")
    bricks = groups_x * groups_y
    rows = m_phi.shape[1]
    cap = 4 * rows // bricks

    dest = m_dest.reshape(1, rows)
    cell = m_cell.reshape(1, rows)
    sent, rank = call(
        functools.partial(dispatch_body, bricks=bricks, cap=cap),
        [((bricks, 4, 128), f32), ((1, rows), jnp.int32)],
        [WHOLE] * 4,
        vmem=60,
        name="dispatch",
    )(dest, cell, m_phi, m_offset)
    arrived = exchange(sent, ("gx", "yz"))

    pencil, = call(
        pencil_x_body, [((groups_x, 24, 512), f32)], [WHOLE] * 2, vmem=8, name="pencil_x"
    )(jnp.transpose(velocity, (0, 2, 3, 1)), jnp.transpose(diffusivity, (1, 2, 0)))
    def blocks(first, deep):
        return pl.BlockSpec((first, slots, deep, wy, depth), lambda i: (0, 0, i, 0, 0))

    def cells(deep):
        return pl.BlockSpec((deep, wy, depth), lambda i: (i, 0, 0))

    local_sum = pl.pallas_call(
        local_body,
        out_shape=jax.ShapeDtypeStruct((4, wx, wy, depth), f32),
        grid=(wx // 8,),
        in_specs=[blocks(4, 8), cells(8)],
        out_specs=pl.BlockSpec((4, 8, wy, depth), lambda i: (0, i, 0, 0)),
        compiler_params=pltpu.CompilerParams(vmem_limit_bytes=40 * MB),
        cost_estimate=pl.CostEstimate(flops=4 * 10**6, bytes_accessed=9 * 10**6, transcendentals=0),
        name="local_sum",
    )(phi, count)

    arrived, local_sum, pencil = lax.optimization_barrier((arrived, local_sum, pencil))
    pencil = exchange(pencil, "gx")
    mean, xs, bound, ehi, elo, e15, e01 = call(
        scatter_body,
        [
            ((4, wx, wy, depth), f32),
            ((8, cap, 128), f32),
            ((3, 128), jnp.int32),
            ((4, 1, wy, depth), f32),
            ((4, 2, wy, depth), f32),
            ((4, wx, depth), f32),
            ((2, 4, wx, depth), f32),
        ],
        [WHOLE] * 3,
        [pltpu.VMEM((9 * 128, 256), f32)],
        vmem=16,
        cost=pl.CostEstimate(flops=4 * 10**9, bytes_accessed=2 * 10**6, transcendentals=0),
        name="scatter",
    )(arrived, local_sum, count)

    pencil, xs = lax.optimization_barrier((pencil, xs))
    lo = shifted(ehi, "gx", 1)
    hi = shifted(elo, "gx", -1)
    wide, = call(
        pencil_y_body, [((groups_y, 16, 1280), f32)], [WHOLE], vmem=8, name="pencil_y"
    )(pencil)
    e15, _ = lax.optimization_barrier((e15, wide))
    up, down = call(
        edge_body,
        [((4, 24, depth), f32), ((2, 4, 24, depth), f32)],
        [WHOLE] * 4,
        vmem=4,
        name="edge",
    )(lo, hi, e15, e01)
    ylo = shifted(up, "yz", 1)
    yhi = shifted(down, "yz", -1)
    wide = exchange(wide, "yz")
    inner, = call(
        blend_inner_body,
        [((4, cap, 128), f32)],
        [SCALARS] + [WHOLE] * 3,
        [pltpu.VMEM((1536, 128), f32), pltpu.VMEM((1536, 384), bf16)],
        vmem=16,
        cost=pl.CostEstimate(flops=8 * 10**9, bytes_accessed=3 * 10**6, transcendentals=0),
        name="blend_inner",
    )(bound, mean, hi, xs)
    wide, inner = lax.optimization_barrier((wide, inner))
    last = jnp.stack(
        [
            (lax.axis_index("gx") == groups_x - 1).astype(jnp.int32),
            (lax.axis_index("yz") == groups_y - 1).astype(jnp.int32),
        ]
    )
    both, moved_new = pl.pallas_call(
        fields_body,
        out_shape=(
            jax.ShapeDtypeStruct((8, 9, 17, 24, depth), f32),
            jax.ShapeDtypeStruct((bricks, 2, 128), f32),
        ),
        in_specs=[SCALARS] * 2 + [WHOLE] * 8,
        out_specs=(pl.BlockSpec(memory_space=pl.ANY), WHOLE),
        scratch_shapes=[
            pltpu.VMEM((9, 17, 24, depth), f32),
            pltpu.VMEM((9, 17, 24, depth), f32),
            pltpu.VMEM((4, 19, wy, depth), f32),
            pltpu.VMEM((4, 3, 24, depth), f32),
            pltpu.VMEM((4 * 16 * 24, 128), f32),
            pltpu.VMEM((4, 19, 32, 128), f32),
            pltpu.VMEM((19, 32, 128), f32),
            pltpu.VMEM((2304, 128), f32),
            pltpu.VMEM((2304, 384), bf16),
            pltpu.VMEM((4, cap, 128), f32),
            pltpu.SemaphoreType.DMA((2,)),
        ],
        compiler_params=pltpu.CompilerParams(vmem_limit_bytes=48 * MB),
        name="fields",
    )(last, bound, wide, mean, lo, hi, ylo, yhi, inner, xs)
    back = exchange(moved_new, ("gx", "yz"))

    def planes(entry):
        return (
            pl.BlockSpec((None, 9, 2, 24, depth), lambda i: (entry, 0, i, 0, 0)),
            pl.BlockSpec((None, 9, 1, 24, depth), lambda i: (entry, 0, 2 * i + 2, 0, 0)),
        )

    particle_new = pl.pallas_call(
        update_body,
        out_shape=jax.ShapeDtypeStruct(phi.shape, f32),
        grid=(wx // 2,),
        in_specs=[blocks(4, 2), blocks(3, 2), cells(2), *planes(0), *planes(1)],
        out_specs=blocks(4, 2),
        scratch_shapes=[pltpu.VMEM((9, 8, wy, depth), f32)],
        compiler_params=pltpu.CompilerParams(vmem_limit_bytes=60 * MB),
        cost_estimate=pl.CostEstimate(flops=8 * 10**7, bytes_accessed=25 * 10**6, transcendentals=0),
        name="update",
    )(phi, offset, count, both, both, both, both)

    migrant_new, = call(
        functools.partial(collect_body, bricks=bricks, cap=cap),
        [((4, rows), f32)],
        [WHOLE] * 3,
        vmem=12,
        name="collect",
    )(dest, rank, back)
    return particle_new, migrant_new


def solution(mesh):
    placed = (
        P(None, None, "gx", "yz", None),
        P(None, None, "gx", "yz", None),
        P("gx", "yz", None),
        P(None, None, "gx", "yz"),
        P(None, "gx", "yz"),
        P(None, ("gx", "yz")),
        P(None, ("gx", "yz")),
        P(("gx", "yz"), None),
        P(("gx", "yz")),
    )
    return jax.shard_map(
        shards,
        mesh=mesh,
        in_specs=placed,
        out_specs=(P(None, None, "gx", "yz", None), P(None, ("gx", "yz"))),
        check_vma=False,
    )
```

```python
import functools

import jax
import jax.numpy as jnp
from jax import lax
from jax.experimental import pallas as pl
from jax.experimental.pallas import tpu as pltpu
from jax.sharding import PartitionSpec as P

time_step = 0.08
mix_coeff = 0.5
span = 8
further = 4
tiles_held = 16
f32 = jnp.float32
bf16 = jnp.bfloat16
MB = 2**20
WHOLE = pl.BlockSpec(memory_space=pltpu.VMEM)
SCALARS = pl.BlockSpec(memory_space=pltpu.SMEM)


def iota(shape, dim):
    return lax.broadcasted_iota(jnp.int32, shape, dim)


def split(value):
    top = value.astype(bf16).astype(f32)
    return top, value - top


def dot_nt(left, right):
    return lax.dot_general(left, right, (((1,), (1,)), ((), ())), preferred_element_type=f32)


def dot_nn(left, right):
    return lax.dot_general(left, right, (((1,), (0,)), ((), ())), preferred_element_type=f32)


def places(number, width):
    return iota((number, width), 0).astype(f32).astype(bf16)


def tall(row, number):
    part = jnp.broadcast_to(row, (16, row.shape[1])).astype(bf16)
    return jnp.concatenate([part] * (number // 16), axis=0)


def marked(spots, row):
    one, none = jnp.ones((), bf16), jnp.zeros((), bf16)
    return jnp.where(spots == tall(row, spots.shape[0]), one, none)


def call(body, outs, specs, scratch=(), vmem=48, cost=None, name=None):
    return pl.pallas_call(
        body,
        out_shape=tuple(jax.ShapeDtypeStruct(s, d) for s, d in outs),
        in_specs=list(specs),
        out_specs=tuple(WHOLE for _ in outs),
        scratch_shapes=list(scratch),
        compiler_params=pltpu.CompilerParams(vmem_limit_bytes=vmem * MB),
        cost_estimate=cost,
        name=name,
    )


def dispatch_body(dest_ref, cell_ref, phi_ref, off_ref, out_ref, rank_ref, *, bricks, cap):
    rows = dest_ref.shape[1]
    hot = jnp.where(iota((bricks, rows), 0) == dest_ref[...], 1.0, 0.0).astype(bf16)
    lines = 16
    line = cell_ref[...] >> 11
    on_line = jnp.where(iota((lines, rows), 0) == line, 1.0, 0.0)
    lined = on_line.astype(bf16)
    bucket = (dest_ref[...] * lines + line).astype(f32)
    bucket_down = jnp.broadcast_to(bucket, (8, rows)).T[:, 0:1]
    total = dot_nt(lined, hot)
    lasts = [None] * lines
    left = jnp.full((1, bricks), float(cap), f32)
    for k in range(lines - 1, -1, -1):
        left = left - total[k : k + 1]
        lasts[k] = left
    free = jnp.zeros((1, bricks), f32)
    starts = []
    for k in range(lines):
        free = jnp.maximum(free, float(k * cap // lines))
        starts.append(jnp.minimum(free, lasts[k]))
        free = free + total[k : k + 1]
    base = jnp.concatenate(starts, axis=0)
    step = 256
    earlier = iota((step, step), 0) < iota((step, step), 1)
    ranks = []
    for b in range(rows // step):
        cut = slice(b * step, (b + 1) * step)
        start = dot_nn(base.astype(bf16), hot[:, cut])
        start = jnp.sum(start * on_line[:, cut], axis=0, keepdims=True)
        same = (bucket_down[cut] == bucket[:, cut]) & earlier
        ranks.append(start + jnp.sum(jnp.where(same, 1.0, 0.0), axis=0, keepdims=True))
        base = base + dot_nt(lined[:, cut], hot[:, cut])
    rank = jnp.concatenate(ranks, axis=1).astype(jnp.int32)
    rank_ref[...] = rank
    here = iota((cap, rows), 0) == rank
    channels = [phi_ref[c : c + 1, :] for c in range(4)]
    channels += [off_ref[c : c + 1, :] for c in range(3)]
    channels.append((cell_ref[...] + 1).astype(f32))
    tops, rests = [], []
    for row in channels:
        top, rest = split(row)
        tops.append(jnp.where(here, top, 0.0).astype(bf16))
        rests.append(jnp.where(here, rest, 0.0).astype(bf16))
    sent = dot_nt(jnp.concatenate(tops, axis=0), hot) + dot_nt(
        jnp.concatenate(rests, axis=0), hot
    )
    sent = sent.T
    for r in range(4):
        out_ref[:, r, :] = sent[:, 128 * r : 128 * (r + 1)]


def collect_body(dest_ref, rank_ref, back_ref, out_ref, *, bricks, cap):
    rows = dest_ref.shape[1]
    hot = jnp.where(iota((bricks, rows), 0) == dest_ref[...], 1.0, 0.0).astype(bf16)
    table = jnp.concatenate([back_ref[:, 0, :], back_ref[:, 1, :]], axis=1).T
    top, rest = split(table)
    both = jnp.concatenate([top, rest], axis=1).astype(bf16)
    got = dot_nn(both, jnp.concatenate([hot, hot], axis=0))
    here = iota((cap, rows), 0) == rank_ref[...]
    for c in range(4):
        picked = jnp.where(here, got[c * cap : (c + 1) * cap], 0.0)
        out_ref[c : c + 1, :] = jnp.sum(picked, axis=0, keepdims=True)


def local_body(phi_ref, count_ref, out_ref):
    for x in range(count_ref.shape[0]):
        count = count_ref[x]
        for c in range(4):
            total = None
            for s in range(phi_ref.shape[1]):
                value = jnp.where(count > s, phi_ref[c, s, x], 0.0)
                total = value if total is None else total + value
            out_ref[c, x] = total


def scatter_body(
    arr_ref, local_ref, count_ref, mean_ref, xs_ref, bound_ref, ehi_ref, elo_ref, e15_ref, e01_ref, acc_ref
):
    half = xs_ref.shape[1]
    for r in range(4):
        turned = arr_ref[:, r, :].T
        xs_ref[2 * r] = turned[0:half]
        xs_ref[2 * r + 1] = turned[half : 2 * half]
    code = arr_ref[:, 3, :].astype(jnp.int32) - 1
    line = code >> 11
    bound_ref[0:1, :] = jnp.min(jnp.where(code >= 0, line, 16), axis=0, keepdims=True)
    most = jnp.max(jnp.where(code >= 0, line, -1), axis=0, keepdims=True)
    bound_ref[1:2, :] = most
    place = iota((1, 128), 1) - half
    in_use = jnp.where((place >= 0) & (most >= 0), place + 1, 0)
    used = jnp.max(in_use, axis=1, keepdims=True)
    used = (used + 2 * tiles_held - 1) // (2 * tiles_held)
    bound_ref[2:3, :] = jnp.broadcast_to(used, (1, 128))
    acc_ref[...] = jnp.zeros_like(acc_ref)
    spots = places(256, 128)

    def step(i, carry):
        at = pl.multiple_of(i * 32, 32)
        cell = xs_ref[7, pl.ds(at, 32), :].astype(jnp.int32) - 1
        plane = (cell >> 7).astype(f32)
        depth = (cell & 127).astype(f32)
        parts = [split(xs_ref[c, pl.ds(at, 32), :]) for c in range(4)]
        lefts, rights = [], []
        for u in range(32):
            rights.append(marked(spots, plane[u : u + 1]))
            at_z = marked(spots[0:128], depth[u : u + 1])
            pieces = [at_z]
            for top, rest in parts:
                pieces.append(at_z * tall(top[u : u + 1], 128))
                pieces.append(at_z * tall(rest[u : u + 1], 128))
            lefts.append(jnp.concatenate(pieces, axis=0))
        acc_ref[...] += dot_nt(
            jnp.concatenate(lefts, axis=1), jnp.concatenate(rights, axis=1)
        )
        return carry

    lax.fori_loop(0, half // 32, step, 0)
    wx, wy = count_ref.shape[0], count_ref.shape[1]
    number = acc_ref[0:128, :].T.reshape(wx, wy, 128)
    share = 1.0 / (count_ref[...].astype(f32) + number)
    for c in range(4):
        at = 128 + 256 * c
        moved = (acc_ref[at : at + 128, :] + acc_ref[at + 128 : at + 256, :]).T
        mean = (local_ref[c] + moved.reshape(wx, wy, 128)) * share
        mean_ref[c] = mean
        ehi_ref[c] = mean[wx - 1 : wx]
        elo_ref[c] = mean[0:2]
        e15_ref[c] = mean[:, wy - 1, :]
        e01_ref[0, c] = mean[:, 0, :]
        e01_ref[1, c] = mean[:, 1, :]


def edge_body(lo_ref, hi_ref, e15_ref, e01_ref, up_ref, down_ref):
    wy = lo_ref.shape[2]
    for ref, source, y in (
        (up_ref, lambda c: e15_ref[c], wy - 1),
        (down_ref.at[0], lambda c: e01_ref[0, c], 0),
        (down_ref.at[1], lambda c: e01_ref[1, c], 1),
    ):
        for c in range(4):
            ref[c, 0:16, :] = source(c)
            ref[c, 16:24, :] = jnp.concatenate(
                [
                    hi_ref[c, 0, y : y + 1, :],
                    hi_ref[c, 1, y : y + 1, :],
                    lo_ref[c, 0, y : y + 1, :],
                    jnp.zeros((5, 128), f32),
                ],
                axis=0,
            )


def pencil_x_body(vel_ref, gam_ref, out_ref):
    groups = out_ref.shape[0]
    pieces = [vel_ref[c].reshape(128, vel_ref.shape[3]).T for c in range(3)]
    pieces.append(gam_ref[...].reshape(128, gam_ref.shape[2]).T)
    rows = jnp.concatenate(pieces, axis=1)
    row = iota((8, 512), 0)
    zero = jnp.zeros((8, 512), f32)
    for p in range(groups):
        out_ref[p, 0:16, :] = rows[16 * p : 16 * p + 16]
        above = rows[16 * p + 16 : 16 * p + 24] if p < groups - 1 else zero
        below = pltpu.roll(rows[16 * p - 8 : 16 * p], 3, 0) if p > 0 else zero
        out_ref[p, 16:24, :] = jnp.where(
            row < 2, above, jnp.where(row == 2, below, 0.0)
        )


def pencil_y_body(in_ref, out_ref):
    groups = out_ref.shape[0]
    lane = iota((24, 128), 1)
    line = lane[0:16]
    zero = jnp.zeros((24, 128), f32)
    for q in range(groups):
        out_ref[q, :, 0:512] = in_ref[2 * q, 0:16, :]
        out_ref[q, :, 512:1024] = in_ref[2 * q + 1, 0:16, :]
        pieces = []
        for c in range(4):
            lanes = slice(128 * c, 128 * c + 128)
            above = in_ref[2 * q + 2, :, lanes] if q < groups - 1 else zero
            below = zero
            if c == 3 and q > 0:
                below = pltpu.roll(in_ref[2 * q - 1, :, lanes], 48, 1)
            pieces.append(jnp.where(lane < 32, above, jnp.where(lane < 48, below, 0.0)))
        first, second, third, fourth = pieces
        second = pltpu.roll(second, 16, 1)
        third = pltpu.roll(third, 32, 1)
        speeds = jnp.where(lane < 16, first, jnp.where(lane < 32, second, third))
        rows = [
            in_ref[2 * q + h, 16:17, 128 * c : 128 * c + 128] for c in range(3) for h in (0, 1)
        ]
        rows += [
            in_ref[2 * q + h, 16 + e : 17 + e, 384:512] for e in range(3) for h in (0, 1)
        ]
        rows.append(speeds[16:17])
        rows.append(fourth[16:19])
        out_ref[q, :, 1024:1152] = jnp.concatenate(rows, axis=0)
        out_ref[q, :, 1152:1280] = jnp.where(
            line < 48, speeds[0:16], pltpu.roll(fourth[0:16], 48, 1)
        )


def turned_lanes(group, lane):
    for bit in (4, 2, 1):
        shift = 16 * bit
        high = (lane // shift) % 2 == 1
        fresh = list(group)
        for j in range(8):
            if j & bit:
                continue
            first, second = group[j], group[j | bit]
            if bit == 4:
                moved = pltpu.roll(jnp.where(high, first, second), shift, 1)
                fresh[j] = jnp.where(high, moved, first)
                fresh[j | bit] = jnp.where(high, second, moved)
            else:
                fresh[j] = jnp.where(high, pltpu.roll(second, shift, 1), first)
                fresh[j | bit] = jnp.where(high, second, pltpu.roll(first, 128 - shift, 1))
        group = fresh
    return group


def brick_part(in_ref, brick_ref, col_ref, tall_ref):
    lane = iota((8, 128), 1)
    col_ref[...] = jnp.zeros_like(col_ref)
    for tile in range(10):
        for xt in range(2):
            group = turned_lanes(
                [in_ref[j, 8 * xt : 8 * xt + 8, 128 * tile : 128 * tile + 128] for j in range(8)],
                lane,
            )
            for g in range(8):
                if tile < 8:
                    at = (16 * (tile % 4) + 8 * (tile // 4) + g) * 24 + 8 * xt
                    tall_ref[at : at + 8, :] = group[g]
                elif tile == 9:
                    if g < 6:
                        c, y = (g, 0) if g < 3 else (3, g - 3)
                        col_ref[c, y, 8 * xt : 8 * xt + 8, :] = group[g]
                else:
                    for k in range(8):
                        n = 8 * xt + k
                        if n < 12:
                            c, e = (n // 2, 0) if n < 6 else (3, (n - 6) // 2)
                            at = (16 * c + 8 * (n % 2) + g) * 24 + 16 + e
                            tall_ref[at : at + 1, :] = group[g][k : k + 1]
                        elif n == 12 and g < 3:
                            col_ref[g, 0, 16:17, :] = group[g][k : k + 1]
                        elif n > 12 and g < 3:
                            col_ref[3, g, n + 3 : n + 4, :] = group[g][k : k + 1]
    for c in range(4):
        for x in range(19 if c == 3 else 17):
            for yt in (0, 8):
                brick_ref[c, x, yt : yt + 8, :] = tall_ref[
                    pl.ds((c * 16 + yt) * 24 + x, 8, stride=24), :
                ]


def z_shift(value, up):
    lane = iota(value.shape, value.ndim - 1)
    if up:
        return jnp.where(lane == 127, 0.0, pltpu.roll(value, 127, value.ndim - 1))
    return jnp.where(lane == 0, 0.0, pltpu.roll(value, 1, value.ndim - 1))


def flux(centre, gamma, sides, velocity):
    total = None
    drift = None
    for (up, gamma_up, down, gamma_down), speed in zip(sides, velocity):
        term = (gamma + gamma_up) * (up - centre) + (gamma + gamma_down) * (down - centre)
        total = term if total is None else total + term
        move = speed * (up - down)
        drift = move if drift is None else drift + move
    return (0.5 * time_step) * (total - drift)


def slot_terms(xs_ref, at):
    def row(c):
        return jnp.concatenate([xs_ref[c, pl.ds(at + e, 1), :] for e in (0, 1)], axis=1)

    cell = row(7).astype(jnp.int32) - 1
    filled = cell >= 0
    depth = cell & 127
    x = jnp.where(filled, cell >> 11, -2)
    y = (cell >> 7) & 15
    return row, x, y, depth


def hat(number, at, frac):
    spot = iota((number, at.shape[1]), 0)
    return jnp.where(spot == at, 1.0 - frac, 0.0) + jnp.where(spot == at + 1, frac, 0.0)


def depth_weights(spots, depth, frac):
    at = depth.astype(f32)
    here = spots == tall(at, 128)
    above = spots == tall(at + 1.0, 128)
    none = jnp.zeros((), bf16)
    parts = []
    for low, high in zip(split(1.0 - frac), split(frac)):
        parts.append(
            jnp.where(here, tall(low, 128), jnp.where(above, tall(high, 128), none))
        )
    return jnp.concatenate([parts[0], parts[0], parts[1]], axis=0)


def widen(tab_ref, lhs_ref):
    top, rest = split(tab_ref[...])
    top = top.astype(bf16)
    lhs_ref[:, 0:128] = top
    lhs_ref[:, 128:256] = rest.astype(bf16)
    lhs_ref[:, 256:384] = top


def total_y(value):
    return jnp.sum(value, axis=0, keepdims=True)


def tile_terms(spots, xs_ref, bound_ref, i):
    row, x, y, depth = slot_terms(xs_ref, 2 * i)
    half = xs_ref.shape[1]
    low = jnp.minimum(bound_ref[0, half + 2 * i], bound_ref[0, half + 2 * i + 1])
    high = jnp.maximum(bound_ref[1, half + 2 * i], bound_ref[1, half + 2 * i + 1])
    windows = (high + 1 - low - span + further) >> 2
    rows_z = depth_weights(spots, depth, row(6))
    wy = hat(24, y, row(5))
    return row, x, low, windows, rows_z, wy


def window_sums(lhs_ref, planes, per, blocks, low, x, frac, rows_z, wy, sums):
    at = pl.multiple_of(low * per, 16)
    along = dot_nn(lhs_ref[pl.ds(at, planes * per), :], rows_z)
    wx = hat(8, x - low, frac)
    sums = list(sums)
    for k in range(planes):
        inside = wx[k : k + 1] * wy[0:16]
        for n in range(blocks):
            sums[n] = sums[n] + along[per * k + 16 * n : per * k + 16 * n + 16] * inside
        if len(sums) > blocks:
            rim = wx[k : k + 1] * wy[16:17]
            sums[blocks] = sums[blocks] + along[per * k + 16 * blocks : per * (k + 1)] * rim
    return tuple(sums)


def blend_tiles(lhs_ref, per, blocks, xs_ref, bound_ref, tiles, finish):
    spots = places(128, 256)
    zero = tuple(jnp.zeros((16, 256), f32) for _ in range(per // 16))

    def group(g, carry):
        held = []
        for e in range(tiles):
            i = g * tiles + e
            row, x, low, windows, rows_z, wy = tile_terms(spots, xs_ref, bound_ref, i)
            args = (x, row(4), rows_z, wy)
            sums = window_sums(lhs_ref, span, per, blocks, low, *args, zero)
            held.append((i, row, low + span, windows, args, sums))
        for i, row, start, windows, args, sums in held:

            def more(w, now):
                return window_sums(
                    lhs_ref, further, per, blocks, start + further * w, *args, now
                )

            finish(i, row, lax.fori_loop(0, windows, more, sums))
        return carry

    lax.fori_loop(0, bound_ref[2, 0], group, 0)


def keep_row(ref, c, i, value):
    for e in (0, 1):
        ref[c, pl.ds(2 * i + e, 1), :] = value[:, 128 * e : 128 * e + 128]


def blend_inner_body(bound_ref, mean_ref, hi_ref, xs_ref, out_ref, tab_ref, lhs_ref):
    for c in range(4):
        for x in range(16):
            tab_ref[64 * x + 16 * c : 64 * x + 16 * c + 16, :] = mean_ref[c, x]
        tab_ref[1024 + 16 * c : 1040 + 16 * c, :] = hi_ref[c, 0]
    tab_ref[1088:, :] = jnp.zeros((64 * (span - 1), 128), f32)
    widen(tab_ref, lhs_ref)
    out_ref[...] = jnp.zeros_like(out_ref)

    def finish(i, row, sums):
        for c in range(4):
            keep_row(out_ref, c, i, total_y(sums[c]))

    blend_tiles(lhs_ref, 64, 4, xs_ref, bound_ref, tiles_held, finish)


def transport_part(
    last_ref, mean_ref, lo_ref, hi_ref, ylo_ref, yhi_ref, brick_ref, col_ref, f_ref, rise_ref, mp_ref, gp_ref
):
    x_in = jnp.where(last_ref[0] == 1, 0.0, 1.0).astype(f32)
    y_in = jnp.where(last_ref[1] == 1, 0.0, 1.0).astype(f32)
    for c in range(4):
        mp_ref[c, 0:16, 8:24, :] = mean_ref[c]
        mp_ref[c, 16:18, 8:24, :] = hi_ref[c]
        mp_ref[c, 18, 8:24, :] = lo_ref[c, 0]
        mp_ref[c, :, 7, :] = ylo_ref[c, 0:19, :]
        mp_ref[c, :, 24, :] = yhi_ref[0, c, 0:19, :]
    gp_ref[:, 8:24, :] = brick_ref[3]
    gp_ref[:, 7, :] = col_ref[3, 2, 0:19, :]
    gp_ref[:, 24, :] = col_ref[3, 0, 0:19, :]

    def plane(x, carry):
        below = jnp.where(x == 0, 18, x - 1)
        keep = jnp.where(x == 16, x_in, 1.0)
        gamma = gp_ref[x, 8:24, :]
        gammas = [
            (gp_ref[x + 1, 8:24, :], gp_ref[below, 8:24, :]),
            (gp_ref[x, 9:25, :], gp_ref[x, 7:23, :]),
            (z_shift(gamma, True), z_shift(gamma, False)),
        ]
        velocity = [brick_ref[d, x] for d in range(3)]
        for c in range(4):
            centre = mp_ref[c, x, 8:24, :]
            means = [
                (mp_ref[c, x + 1, 8:24, :], mp_ref[c, below, 8:24, :]),
                (mp_ref[c, x, 9:25, :], mp_ref[c, x, 7:23, :]),
                (z_shift(centre, True), z_shift(centre, False)),
            ]
            sides = [(m[0], g[0], m[1], g[1]) for m, g in zip(means, gammas)]
            moved = flux(centre, gamma, sides, velocity) * keep
            f_ref[c, x, 0:16, :] = centre
            f_ref[4 + c, x, 0:16, :] = moved
            rise_ref[c, x, 0:16, :] = means[2][0] - centre
            rise_ref[4 + c, x, 0:16, :] = z_shift(moved, True) - moved
        f_ref[8, x, 0:16, :] = gamma
        rise_ref[8, x, 0:16, :] = gammas[2][0] - gamma
        return carry

    def several(i, carry):
        for k in range(4):
            plane(4 * i + k, carry)
        return carry

    lax.fori_loop(0, 4, several, 0)
    plane(16, 0)
    row = iota((24, 128), 0)

    def x_up(value):
        return pltpu.roll(value, 23, 0)

    def x_down(value):
        return jnp.where(row == 0, value[18:19], pltpu.roll(value, 1, 0))

    keep = jnp.where(row == 16, x_in, 1.0) * y_in
    gamma = col_ref[3, 0]
    gamma_low = jnp.concatenate([gp_ref[:, 23, :], jnp.zeros((5, 128), f32)], axis=0)
    gammas = [
        (x_up(gamma), x_down(gamma)),
        (col_ref[3, 1], gamma_low),
        (z_shift(gamma, True), z_shift(gamma, False)),
    ]
    velocity = [col_ref[d, 0] for d in range(3)]
    for c in range(4):
        centre = yhi_ref[0, c]
        low = jnp.concatenate([mp_ref[c, :, 23, :], jnp.zeros((5, 128), f32)], axis=0)
        means = [
            (x_up(centre), x_down(centre)),
            (yhi_ref[1, c], low),
            (z_shift(centre, True), z_shift(centre, False)),
        ]
        sides = [(m[0], g[0], m[1], g[1]) for m, g in zip(means, gammas)]
        moved = flux(centre, gamma, sides, velocity) * keep
        f_ref[c, :, 16, :] = centre[0:17]
        f_ref[4 + c, :, 16, :] = moved[0:17]
        rise_ref[c, :, 16, :] = (means[2][0] - centre)[0:17]
        rise_ref[4 + c, :, 16, :] = (z_shift(moved, True) - moved)[0:17]
    f_ref[8, :, 16, :] = gamma[0:17]
    rise_ref[8, :, 16, :] = (gammas[2][0] - gamma)[0:17]


def outer_part(bound_ref, f_ref, inner_ref, xs_ref, out_ref, tab_ref, lhs_ref, new_ref):
    for x in range(17):
        for c in range(5):
            tab_ref[96 * x + 16 * c : 96 * x + 16 * c + 16, :] = f_ref[4 + c, x, 0:16, :]
        tab_ref[96 * x + 80 : 96 * x + 96, :] = jnp.concatenate(
            [f_ref[c, x, 16:17, :] for c in range(9)] + [jnp.zeros((7, 128), f32)], axis=0
        )
    tab_ref[96 * 17 :, :] = jnp.zeros((96 * (span - 1), 128), f32)
    widen(tab_ref, lhs_ref)
    new_ref[...] = jnp.zeros_like(new_ref)

    def finish(i, row, sums):
        def inner(c):
            return jnp.concatenate([inner_ref[c, pl.ds(2 * i + e, 1), :] for e in (0, 1)], axis=1)

        rim = sums[5]
        rate = mix_coeff * (total_y(sums[4]) + rim[8:9])
        for c in range(4):
            phi = row(c)
            mean = inner(c) + rim[c : c + 1]
            moved = total_y(sums[c]) + rim[4 + c : 5 + c]
            keep_row(new_ref, c, i, phi + moved - rate * (phi - mean))

    blend_tiles(lhs_ref, 96, 5, xs_ref, bound_ref, tiles_held, finish)
    half = xs_ref.shape[1]
    for r in range(2):
        both = jnp.concatenate([new_ref[2 * r], new_ref[2 * r + 1]], axis=0)
        out_ref[:, r, :] = both.T


def fields_body(
    last_ref, bound_ref, wide_ref, mean_ref, lo_ref, hi_ref, ylo_ref, yhi_ref, inner_ref, xs_ref,
    both_ref, out_ref,
    f_ref, rise_ref, brick_ref, col_ref, tall_ref, mp_ref, gp_ref, tab_ref, lhs_ref, new_ref, sems,
):
    brick_part(wide_ref, brick_ref, col_ref, tall_ref)
    transport_part(
        last_ref, mean_ref, lo_ref, hi_ref, ylo_ref, yhi_ref, brick_ref, col_ref, f_ref, rise_ref, mp_ref, gp_ref
    )
    first = pltpu.make_async_copy(f_ref, both_ref.at[0], sems.at[0])
    second = pltpu.make_async_copy(rise_ref, both_ref.at[1], sems.at[1])
    first.start()
    second.start()
    outer_part(bound_ref, f_ref, inner_ref, xs_ref, out_ref, tab_ref, lhs_ref, new_ref)
    first.wait()
    second.wait()


def update_body(
    phi_ref, off_ref, count_ref, f_ref, f_next_ref, rise_ref, rise_next_ref, out_ref, coef_ref
):
    deep, wy = count_ref.shape[0], count_ref.shape[1]
    slots = phi_ref.shape[1]
    width = 4
    for x in range(deep):
        for ch in range(9):
            for sz, (ref, after) in enumerate(((f_ref, f_next_ref), (rise_ref, rise_next_ref))):
                high, k = (ref, x + 1) if x + 1 < deep else (after, 0)
                c00 = ref[ch, x, 0:wy, :]
                c01 = ref[ch, x, 1 : wy + 1, :]
                c10 = high[ch, k, 0:wy, :]
                c11 = high[ch, k, 1 : wy + 1, :]
                dx = c10 - c00
                coef_ref[ch, sz] = c00
                coef_ref[ch, 2 + sz] = c01 - c00
                coef_ref[ch, 4 + sz] = dx
                coef_ref[ch, 6 + sz] = (c11 - c01) - dx
        count = count_ref[x]

        def group(i, carry):
            at = [i * width + s for s in range(width)]
            a = [off_ref[0, s, x] for s in at]
            b = [off_ref[1, s, x] for s in at]
            d = [off_ref[2, s, x] for s in at]

            def blend(ch):
                k = [coef_ref[ch, n] for n in range(8)]
                return [
                    ((k[7] * d[n] + k[6]) * b[n] + (k[5] * d[n] + k[4])) * a[n]
                    + ((k[3] * d[n] + k[2]) * b[n] + (k[1] * d[n] + k[0]))
                    for n in range(width)
                ]

            rate = [mix_coeff * value for value in blend(8)]
            for c in range(4):
                mean = blend(c)
                moved = blend(4 + c)
                for n in range(width):
                    phi = phi_ref[c, at[n], x]
                    fresh = phi + moved[n] - rate[n] * (phi - mean[n])
                    out_ref[c, at[n], x] = jnp.where(count > at[n], fresh, 0.0)
            return carry

        lax.fori_loop(0, slots // width, group, 0)


def shifted(value, axis, by):
    count = lax.axis_size(axis)
    pairs = [(i, i + by) for i in range(count) if 0 <= i + by < count]
    return lax.ppermute(value, axis, pairs)


def exchange(value, axis):
    return lax.all_to_all(value, axis, split_axis=0, concat_axis=0, tiled=True)


def shards(phi, offset, count, velocity, diffusivity, m_phi, m_offset, m_dest, m_cell):
    slots, wx, wy, depth = phi.shape[1:]
    groups_x, groups_y = lax.axis_size("gx"), lax.axis_size("yz")
    bricks = groups_x * groups_y
    rows = m_phi.shape[1]
    cap = 4 * rows // bricks

    dest = m_dest.reshape(1, rows)
    cell = m_cell.reshape(1, rows)
    sent, rank = call(
        functools.partial(dispatch_body, bricks=bricks, cap=cap),
        [((bricks, 4, 128), f32), ((1, rows), jnp.int32)],
        [WHOLE] * 4,
        vmem=60,
        name="dispatch",
    )(dest, cell, m_phi, m_offset)
    arrived = exchange(sent, ("gx", "yz"))

    pencil, = call(
        pencil_x_body, [((groups_x, 24, 512), f32)], [WHOLE] * 2, vmem=8, name="pencil_x"
    )(jnp.transpose(velocity, (0, 2, 3, 1)), jnp.transpose(diffusivity, (1, 2, 0)))
    def blocks(first, deep):
        return pl.BlockSpec((first, slots, deep, wy, depth), lambda i: (0, 0, i, 0, 0))

    def cells(deep):
        return pl.BlockSpec((deep, wy, depth), lambda i: (i, 0, 0))

    local_sum = pl.pallas_call(
        local_body,
        out_shape=jax.ShapeDtypeStruct((4, wx, wy, depth), f32),
        grid=(wx // 8,),
        in_specs=[blocks(4, 8), cells(8)],
        out_specs=pl.BlockSpec((4, 8, wy, depth), lambda i: (0, i, 0, 0)),
        compiler_params=pltpu.CompilerParams(vmem_limit_bytes=40 * MB),
        cost_estimate=pl.CostEstimate(flops=4 * 10**6, bytes_accessed=9 * 10**6, transcendentals=0),
        name="local_sum",
    )(phi, count)

    arrived, local_sum, pencil = lax.optimization_barrier((arrived, local_sum, pencil))
    pencil = exchange(pencil, "gx")
    mean, xs, bound, ehi, elo, e15, e01 = call(
        scatter_body,
        [
            ((4, wx, wy, depth), f32),
            ((8, cap, 128), f32),
            ((3, 128), jnp.int32),
            ((4, 1, wy, depth), f32),
            ((4, 2, wy, depth), f32),
            ((4, wx, depth), f32),
            ((2, 4, wx, depth), f32),
        ],
        [WHOLE] * 3,
        [pltpu.VMEM((9 * 128, 256), f32)],
        vmem=16,
        cost=pl.CostEstimate(flops=4 * 10**9, bytes_accessed=2 * 10**6, transcendentals=0),
        name="scatter",
    )(arrived, local_sum, count)

    pencil, xs = lax.optimization_barrier((pencil, xs))
    lo = shifted(ehi, "gx", 1)
    hi = shifted(elo, "gx", -1)
    wide, = call(
        pencil_y_body, [((groups_y, 16, 1280), f32)], [WHOLE], vmem=8, name="pencil_y"
    )(pencil)
    e15, _ = lax.optimization_barrier((e15, wide))
    up, down = call(
        edge_body,
        [((4, 24, depth), f32), ((2, 4, 24, depth), f32)],
        [WHOLE] * 4,
        vmem=4,
        name="edge",
    )(lo, hi, e15, e01)
    ylo = shifted(up, "yz", 1)
    yhi = shifted(down, "yz", -1)
    wide = exchange(wide, "yz")
    inner, = call(
        blend_inner_body,
        [((4, cap, 128), f32)],
        [SCALARS] + [WHOLE] * 3,
        [pltpu.VMEM((1536, 128), f32), pltpu.VMEM((1536, 384), bf16)],
        vmem=16,
        cost=pl.CostEstimate(flops=8 * 10**9, bytes_accessed=3 * 10**6, transcendentals=0),
        name="blend_inner",
    )(bound, mean, hi, xs)
    wide, inner = lax.optimization_barrier((wide, inner))
    last = jnp.stack(
        [
            (lax.axis_index("gx") == groups_x - 1).astype(jnp.int32),
            (lax.axis_index("yz") == groups_y - 1).astype(jnp.int32),
        ]
    )
    both, moved_new = pl.pallas_call(
        fields_body,
        out_shape=(
            jax.ShapeDtypeStruct((8, 9, 17, 24, depth), f32),
            jax.ShapeDtypeStruct((bricks, 2, 128), f32),
        ),
        in_specs=[SCALARS] * 2 + [WHOLE] * 8,
        out_specs=(pl.BlockSpec(memory_space=pl.ANY), WHOLE),
        scratch_shapes=[
            pltpu.VMEM((9, 17, 24, depth), f32),
            pltpu.VMEM((9, 17, 24, depth), f32),
            pltpu.VMEM((4, 19, wy, depth), f32),
            pltpu.VMEM((4, 3, 24, depth), f32),
            pltpu.VMEM((4 * 16 * 24, 128), f32),
            pltpu.VMEM((4, 19, 32, 128), f32),
            pltpu.VMEM((19, 32, 128), f32),
            pltpu.VMEM((2304, 128), f32),
            pltpu.VMEM((2304, 384), bf16),
            pltpu.VMEM((4, cap, 128), f32),
            pltpu.SemaphoreType.DMA((2,)),
        ],
        compiler_params=pltpu.CompilerParams(vmem_limit_bytes=48 * MB),
        name="fields",
    )(last, bound, wide, mean, lo, hi, ylo, yhi, inner, xs)
    back = exchange(moved_new, ("gx", "yz"))

    def planes(entry):
        return (
            pl.BlockSpec((None, 9, 2, 24, depth), lambda i: (entry, 0, i, 0, 0)),
            pl.BlockSpec((None, 9, 1, 24, depth), lambda i: (entry, 0, 2 * i + 2, 0, 0)),
        )

    particle_new = pl.pallas_call(
        update_body,
        out_shape=jax.ShapeDtypeStruct(phi.shape, f32),
        grid=(wx // 2,),
        in_specs=[blocks(4, 2), blocks(3, 2), cells(2), *planes(0), *planes(1)],
        out_specs=blocks(4, 2),
        scratch_shapes=[pltpu.VMEM((9, 8, wy, depth), f32)],
        compiler_params=pltpu.CompilerParams(vmem_limit_bytes=60 * MB),
        cost_estimate=pl.CostEstimate(flops=8 * 10**7, bytes_accessed=25 * 10**6, transcendentals=0),
        name="update",
    )(phi, offset, count, both, both, both, both)

    migrant_new, = call(
        functools.partial(collect_body, bricks=bricks, cap=cap),
        [((4, rows), f32)],
        [WHOLE] * 3,
        vmem=12,
        name="collect",
    )(dest, rank, back)
    return particle_new, migrant_new


def solution(mesh):
    placed = (
        P(None, None, "gx", "yz", None),
        P(None, None, "gx", "yz", None),
        P("gx", "yz", None),
        P(None, None, "gx", "yz"),
        P(None, "gx", "yz"),
        P(None, ("gx", "yz")),
        P(None, ("gx", "yz")),
        P(("gx", "yz"), None),
        P(("gx", "yz")),
    )
    return jax.shard_map(
        shards,
        mesh=mesh,
        in_specs=placed,
        out_specs=(P(None, None, "gx", "yz", None), P(None, ("gx", "yz"))),
        check_vma=False,
    )
```
